32 devices in a mesh: gx: 16 (over z, y, x), gy: 2 (over core).
Axes of the slice: x: 2, y: 2, z: 4, core: 2. Of those that a mesh axis runs over, the one named last changes fastest.
Arguments:
- velocity: float32 [3, 128, 96, 256], P(None, 'gx', 'gy'), may hold values from -6 to 6
- pressure: float32 [128, 96, 256], P('gx', 'gy'), may hold values from -6 to 6
- viscosity: float32 [128, 96, 256], P('gx', 'gy'), may hold values from 0.12 to 0.6
- wind_profile: float32 [256], replicated, may hold values from 0.5 to 1.5
- panel_area: float32 [4096], P('gy'), may hold values from 0.5 to 2
- slot_cell: int32 [2, 4096], P('gy', 'gx'), may hold values from 0 to 98303
- slot_panel: int32 [2, 4096], P('gy'), may hold values from -1 to 2047, as said below
- panel_shapes: bfloat16 [4096, 2048], P('gy', 'gx'), may hold values from -0.09375 to 0.09375
- node_shapes: bfloat16 [1024, 2048], P(None, 'gx'), may hold values from -0.125 to 0.125
- damper_node: int32 [128], P('gy'), may hold values from 0 to 1022
- damper_viscous: float32 [128], P('gy'), may hold values from 0.2 to 2
- damper_hysteretic: float32 [128], P('gy'), may hold values from 0.2 to 2
- frequency: float32 [2048], P('gx'), may hold values from 0.2 to 1.8
- damping_ratio: float32 [2048], P('gx'), may hold values from 0.05 to 0.5
- modal_state: float32 [2, 2048], P(None, 'gx'), may hold values from -6 to 6
- damper_state: float32 [128], P('gy'), may hold values from -1 to 1
Outputs:
- velocity_next: float32 [3, 128, 96, 256], P(None, 'gx', 'gy')
- pressure_next: float32 [128, 96, 256], P('gx', 'gy')
- modal_next: float32 [2, 2048], P(None, 'gx')
- damper_next: float32 [128], P('gy')
The draws below stay inside these ranges and needn't reach their ends.
Inputs may be any that keep to these rules, and one draw needn't show every extreme that they name: `slot_panel`: in every row each panel number 0 to 2047 stands in exactly one slot; every other slot holds -1.
All inputs are finite; a program needn't handle non-finite values.
Results may differ from the reference program's by a relative error of at most 0.0013.
Values may be sent and summed in bfloat16 or wider, within the bound.
No kernel may reach another device: no remote copies, remote signals or barrier semaphores. Data moves between devices by JAX's collectives and lax.ppermute only.
A program may use at most 64 MiB of HBM per device.

```python
import math
import jax
import jax.numpy as jnp
from jax import lax

CX = 8
CY = 48
NZ = 256
MODES = 2048
PAN_COL = 2048
NODES = 1024
SLOTS = 256
NX = 128
NY = 96
PANELS = 4096
DAMPERS = 128
N_GX = 16
N_GY = 2


def draw_slot_panel(key, part):
    piece_total = NY // CY
    slot_total = NX // CX * SLOTS
    piece_keys = jax.random.split(key, piece_total)
    orders = jax.vmap(lambda single: jax.random.permutation(single, slot_total))(piece_keys).astype(jnp.int32)
    return jnp.where(orders < PAN_COL, orders, -1).astype(jnp.int32)


def set_ends(values, key, smallest, largest):
    longest = values.shape.index(max(values.shape))
    spots = []
    for shift in (0, 1):
        where = [jax.random.randint(jax.random.fold_in(key, axis), (), 0, length) for axis, length in enumerate(values.shape)]
        where[longest] = (where[longest] + shift) % values.shape[longest]
        spots.append(tuple(where))
    return values.at[spots[0]].set(smallest).at[spots[1]].set(largest)


def block_scale(rng, shape, shards, smallest, largest):
    factor_of = 1.0
    for position, parts in shards:
        steps = jax.random.uniform(jax.random.fold_in(jax.random.fold_in(rng, 6), position), (parts,), jnp.float32, smallest / len(shards), largest / len(shards))
        factor_of = factor_of * jnp.repeat(jnp.exp(steps), shape[position] // parts).reshape((-1,) + (1,) * (len(shape) - 1 - position))
    return factor_of


def noise(own_key, dims, deviation, most, cuts=(), kind=jnp.bfloat16):
    loudness = block_scale(own_key, dims, cuts, -0.22, 0.18) if cuts else 1.0
    drawn = jax.random.normal(own_key, dims, jnp.float32) * deviation * loudness
    return jnp.minimum(jnp.maximum(drawn, -most), most).astype(kind)


def setup_inputs(seed: int = 0) -> dict:
    key_list = jax.random.split(jax.random.key(seed), 17)
    velocity = noise(key_list[0], (3, NX, NY, NZ), 1.0, 6.0, ((1, 16), (2, 2)), jnp.float32)
    pressure = noise(key_list[1], (NX, NY, NZ), 1.0, 6.0, ((0, 16), (1, 2)), jnp.float32)
    viscosity = jnp.clip(jnp.exp(math.log(0.6) - 1.609438 * jax.random.uniform(key_list[2], (NX, NY, NZ), jnp.float32) ** block_scale(key_list[2], (NX, NY, NZ), ((0, 16), (1, 2)), -0.2, 0.2)), 0.12, 0.6)
    wind_profile = jnp.clip(jax.random.uniform(key_list[3], (NZ,), jnp.float32, 0.5, 1.5), 0.5, 1.5)
    panel_area = jnp.clip(jnp.exp(math.log(2.0) - 1.3862944 * jax.random.uniform(key_list[4], (PANELS,), jnp.float32) ** block_scale(key_list[4], (PANELS,), ((0, 2),), -0.2, 0.2)), 0.5, 2.0)
    slot_cell = set_ends(jax.random.randint(key_list[5], (N_GY, N_GX * SLOTS), 0, CX * CY * NZ), jax.random.fold_in(key_list[5], 1), 0, (CX * CY * NZ) - 1).astype(jnp.int32)
    slot_panel = draw_slot_panel(jax.random.fold_in(key_list[16], 71), 0)
    panel_shapes = noise(key_list[7], (PANELS, MODES), PANELS ** -0.5, 0.09375, ((0, 2), (1, 16)))
    node_shapes = noise(key_list[8], (NODES, MODES), MODES ** -0.5, 0.125, ((1, 16),))
    damper_node = set_ends(jax.random.randint(key_list[9], (DAMPERS,), 0, NODES - 1), jax.random.fold_in(key_list[9], 1), 0, (NODES - 1) - 1).astype(jnp.int32)
    damper_viscous = jnp.clip(jnp.exp(math.log(2.0) - 2.3025851 * jax.random.uniform(key_list[10], (DAMPERS,), jnp.float32) ** block_scale(key_list[10], (DAMPERS,), ((0, 2),), -0.2, 0.2)), 0.2, 2.0)
    damper_hysteretic = jnp.clip(jnp.exp(math.log(2.0) - 2.3025851 * jax.random.uniform(key_list[11], (DAMPERS,), jnp.float32) ** block_scale(key_list[11], (DAMPERS,), ((0, 2),), -0.2, 0.2)), 0.2, 2.0)
    frequency = jnp.clip(jnp.exp(math.log(1.8) - 2.1972245 * jax.random.uniform(key_list[12], (MODES,), jnp.float32) ** block_scale(key_list[12], (MODES,), ((0, 16),), -0.2, 0.2)), 0.2, 1.8)
    damping_ratio = jnp.clip(jnp.exp(math.log(0.5) - 2.3025851 * jax.random.uniform(key_list[13], (MODES,), jnp.float32) ** block_scale(key_list[13], (MODES,), ((0, 16),), -0.2, 0.2)), 0.05, 0.5)
    modal_state = noise(key_list[14], (2, MODES), 1.0, 6.0, ((1, 16),), jnp.float32)
    damper_state = jnp.clip(jax.random.uniform(key_list[15], (DAMPERS,), jnp.float32, -1.0, 1.0) * block_scale(key_list[15], (DAMPERS,), ((0, 2),), -0.4, 0.0), -1.0, 1.0)
    return {"velocity": velocity, "pressure": pressure, "viscosity": viscosity, "wind_profile": wind_profile, "panel_area": panel_area, "slot_cell": slot_cell, "slot_panel": slot_panel, "panel_shapes": panel_shapes, "node_shapes": node_shapes, "damper_node": damper_node, "damper_viscous": damper_viscous, "damper_hysteretic": damper_hysteretic, "frequency": frequency, "damping_ratio": damping_ratio, "modal_state": modal_state, "damper_state": damper_state}


time_step = 0.1
sound_squared = 1.0
modal_step = 0.5
hysteresis_gain = 1.0
shape_beta = 0.5
shape_gamma = 0.5
spring_rate = 0.5


def advance(padded, local_viscosity, wind_profile):
    centre_cells = padded[:, 1:-1, 1:-1, 1:-1]
    ahead_cells = padded[:, 2:, 1:-1, 1:-1]
    behind_cells = padded[:, :-2, 1:-1, 1:-1]
    right_cells = padded[:, 1:-1, 2:, 1:-1]
    left_cells = padded[:, 1:-1, :-2, 1:-1]
    above_cells = padded[:, 1:-1, 1:-1, 2:]
    below_cells = padded[:, 1:-1, 1:-1, :-2]
    slope_stream = 0.5 * (ahead_cells - behind_cells)
    slope_span = 0.5 * (right_cells - left_cells)
    slope_vertical = 0.5 * (above_cells - below_cells)
    laplacian = ahead_cells + behind_cells + right_cells + left_cells + above_cells + below_cells - 6.0 * centre_cells
    pressure_slope = jnp.stack([slope_stream[3], slope_span[3], slope_vertical[3]])
    velocity_new = centre_cells[:3] + time_step * (-wind_profile * slope_stream[:3] + local_viscosity * laplacian[:3] - pressure_slope)
    pressure_new = centre_cells[3] - time_step * sound_squared * (slope_stream[0] + slope_span[1] + slope_vertical[2])
    return jnp.concatenate([velocity_new, pressure_new[None]], axis=0)


def reference(velocity, pressure, viscosity, wind_profile, panel_area, slot_cell, slot_panel, panel_shapes, node_shapes, damper_node, damper_viscous, damper_hysteretic, frequency, damping_ratio, modal_state, damper_state):
    fields = jnp.concatenate([velocity, pressure[None]], axis=0)
    for substep in range(2):
        padded = jnp.pad(fields, ((0, 0), (1, 1), (1, 1), (1, 1)))

        def slab_update(slab_number, padded=padded):
            start = slab_number * CX
            piece = lax.dynamic_slice_in_dim(padded, start, CX + 2, 1)
            local_viscosity = lax.dynamic_slice_in_dim(viscosity, start, CX, 0)
            return advance(piece, local_viscosity, wind_profile)

        updated = lax.map(slab_update, jnp.arange(N_GX, dtype=jnp.int32))
        fields = jnp.moveaxis(updated, 0, 1).reshape(4, NX, NY, NZ)
    velocity_next = fields[:3]
    pressure_next = fields[3]

    pressure_blocks = pressure_next.reshape(N_GX, CX, N_GY, CY, NZ).transpose(2, 0, 1, 3, 4).reshape(N_GY, N_GX, CX * CY * NZ)
    cell_table = slot_cell.reshape(N_GY, N_GX, SLOTS)
    sampled = jnp.take_along_axis(pressure_blocks, cell_table, axis=2).reshape(N_GY, N_GX * SLOTS)
    area_table = panel_area.reshape(N_GY, PAN_COL)
    safe_ids = jnp.where(slot_panel < 0, 0, slot_panel).astype(jnp.int32)
    slot_load = (jnp.take_along_axis(area_table, safe_ids, axis=1) * sampled).astype(jnp.bfloat16)
    target = jnp.where(slot_panel < 0, PAN_COL, slot_panel).astype(jnp.int32)

    def place(row_target, row_loads):
        return jnp.zeros((PAN_COL + 1,), jnp.bfloat16).at[row_target].set(row_loads)[:PAN_COL]

    panel_load = jax.vmap(place)(target, slot_load).reshape(PANELS)
    panel_modal = jnp.dot(panel_load, panel_shapes, preferred_element_type=jnp.float32)

    drift = node_shapes[damper_node + 1].astype(jnp.float32) - node_shapes[damper_node].astype(jnp.float32)
    displacement = modal_state[0]
    modal_velocity = modal_state[1]
    hysteresis = damper_state
    for modal_turn in range(2):
        stretch = jnp.dot(drift, displacement, precision=lax.Precision.HIGHEST)
        stretch_rate = jnp.dot(drift, modal_velocity, precision=lax.Precision.HIGHEST)
        hysteresis = hysteresis + modal_step * (hysteresis_gain * stretch_rate - shape_beta * jnp.abs(stretch_rate) * hysteresis - shape_gamma * stretch_rate * jnp.abs(hysteresis))
        damper_force = -(damper_viscous * stretch_rate + spring_rate * stretch + damper_hysteretic * hysteresis)
        modal_load = panel_modal + jnp.dot(damper_force, drift, precision=lax.Precision.HIGHEST)
        acceleration = modal_load - 2.0 * damping_ratio * frequency * modal_velocity - frequency * frequency * displacement
        modal_velocity = modal_velocity + modal_step * acceleration
        displacement = displacement + modal_step * modal_velocity
    return velocity_next, pressure_next, jnp.stack([displacement, modal_velocity]), hysteresis
```

```python
import functools

import jax
import jax.numpy as jnp
from jax import lax
from jax.experimental import pallas as pl
from jax.experimental.pallas import tpu as pltpu
from jax.sharding import PartitionSpec as P

f32 = jnp.float32
bf16 = jnp.bfloat16
time_step = 0.1
modal_step = 0.5
shape_beta = 0.5
shape_gamma = 0.5
spring_rate = 0.5
LANES = 128
PAD = 8
VMEM_BYTES = 40 * 1024 * 1024


def shifts(size, step, cyclic):
    if cyclic:
        return [((i + step) % size, i) for i in range(size)]
    return [(i, i + step) for i in range(size) if 0 <= i + step < size]


def parts_of(row):
    high = row.astype(bf16).astype(f32)
    rest = row - high
    middle = rest.astype(bf16).astype(f32)
    return [high, middle, rest - middle]


def stacked(rows):
    filler = jnp.zeros((16 - len(rows), rows[0].shape[1]), f32)
    return jnp.concatenate(rows + [filler], axis=0).astype(bf16)


def flow_kernel(
    count_x,
    count_y,
    vel,
    pre,
    vis,
    wind,
    before,
    after,
    left,
    right,
    cell,
    area,
    partial,
    vel_out,
    pre_out,
    payload,
    old,
    mid,
    visc,
    sem,
):
    layers, rows, height = pre.shape
    last = PAD + rows
    ix = lax.axis_index("gx")
    iy = lax.axis_index("gy")
    inner = pl.ds(2, layers)
    own = [
        pltpu.make_async_copy(vel.at[i], old.at[i, inner, pl.ds(PAD, rows)], sem.at[i])
        for i in range(3)
    ]
    own.append(pltpu.make_async_copy(pre, old.at[3, inner, pl.ds(PAD, rows)], sem.at[3]))
    own.append(pltpu.make_async_copy(vis, visc.at[inner, pl.ds(PAD, rows)], sem.at[4]))
    side_left = pltpu.make_async_copy(
        left.at[pl.ds(0, 4)], old.at[:, inner, pl.ds(0, PAD)], sem.at[5]
    )
    side_left_visc = pltpu.make_async_copy(left.at[4], visc.at[inner, pl.ds(0, PAD)], sem.at[6])
    side_right = pltpu.make_async_copy(
        right.at[pl.ds(0, 4)], old.at[:, inner, pl.ds(last, PAD)], sem.at[7]
    )
    side_right_visc = pltpu.make_async_copy(
        right.at[4], visc.at[inner, pl.ds(last, PAD)], sem.at[8]
    )
    for copy in own:
        copy.start()
    has_left = iy > 0
    has_right = iy < count_y - 1
    has_before = ix > 0
    has_after = ix < count_x - 1

    @pl.when(has_left)
    def _():
        side_left.start()
        side_left_visc.start()

    @pl.when(has_right)
    def _():
        side_right.start()
        side_right_visc.start()

    blank = jnp.zeros((4, layers, PAD, height), f32)

    @pl.when(jnp.logical_not(has_left))
    def _():
        old[:, 2 : 2 + layers, 0:PAD, :] = blank
        mid[:, 2 : 2 + layers, 0:PAD, :] = blank

    @pl.when(jnp.logical_not(has_right))
    def _():
        old[:, 2 : 2 + layers, last : last + PAD, :] = blank
        mid[:, 2 : 2 + layers, last : last + PAD, :] = blank

    for message, first, near in ((before, 0, 1), (after, layers + 2, layers + 2)):
        for field in range(4):
            for depth in range(2):
                start = (field * 2 + depth) * rows
                old[field, first + depth, PAD:last, :] = message[start : start + rows, :].astype(f32)
        start = 8 * rows
        visc[near, PAD:last, :] = message[start : start + rows, :].astype(f32)
        corner = message[9 * rows : 9 * rows + 16, :].astype(f32)
        for field in range(4):
            old[field, near, PAD - 1 : PAD, :] = corner[field : field + 1]
            old[field, near, last : last + 1, :] = corner[4 + field : 5 + field]

    for copy in own:
        copy.wait()

    @pl.when(has_left)
    def _():
        side_left.wait()
        side_left_visc.wait()

    @pl.when(has_right)
    def _():
        side_right.wait()
        side_right_visc.wait()

    lane = lax.broadcasted_iota(jnp.int32, (8, height), 1)
    top = lane == height - 1
    bottom = lane == 0
    wind_part = jnp.broadcast_to(wind[...] * (0.5 * time_step), (8, height))
    half = 0.5 * time_step

    def step(source, layer, row, edge):
        here = pl.ds(row, 8)
        centre = [source[f, layer, here, :] for f in range(4)]
        ahead = [source[f, layer + 1, here, :] for f in range(4)]
        behind = [source[f, layer - 1, here, :] for f in range(4)]
        if edge < 0:
            lower = [pltpu.roll(c, 1, 0) for c in centre]
        else:
            lower = [source[f, layer, pl.ds(row - 1, 8), :] for f in range(4)]
        if edge > 0:
            upper = [pltpu.roll(c, 7, 0) for c in centre]
        else:
            upper = [source[f, layer, pl.ds(row + 1, 8), :] for f in range(4)]
        above = [jnp.where(top, 0.0, pltpu.roll(c, height - 1, 1)) for c in centre]
        below = [jnp.where(bottom, 0.0, pltpu.roll(c, 1, 1)) for c in centre]
        factor = visc[layer, here, :] * time_step
        slopes = (ahead[3] - behind[3], upper[3] - lower[3], above[3] - below[3])
        result = []
        for i in range(3):
            around = (ahead[i] + behind[i]) + (upper[i] + lower[i]) + (above[i] + below[i])
            result.append(
                centre[i]
                + factor * (around - 6.0 * centre[i])
                - wind_part * (ahead[i] - behind[i])
                - half * slopes[i]
            )
        result.append(
            centre[3]
            - half * ((ahead[0] - behind[0]) + (upper[1] - lower[1]) + (above[2] - below[2]))
        )
        return result

    def first_step(layer, row, edge=0):
        result = step(old, layer, row, edge)
        for f in range(4):
            mid[f, layer, pl.ds(row, 8), :] = result[f]

    @pl.loop(2, 2 + layers)
    def _(layer):
        for row in range(PAD, last, 8):
            first_step(layer, row)

    @pl.when(has_left)
    def _():
        @pl.loop(2, 2 + layers)
        def _(layer):
            first_step(layer, 0, -1)

    @pl.when(has_right)
    def _():
        @pl.loop(2, 2 + layers)
        def _(layer):
            first_step(layer, last, 1)

    for there, layer in ((has_before, 1), (has_after, layers + 2)):

        @pl.when(there)
        def _(layer=layer):
            for row in range(PAD, last, 8):
                first_step(layer, row)

        @pl.when(jnp.logical_not(there))
        def _(layer=layer):
            mid[:, layer, PAD:last, :] = jnp.zeros((4, rows, height), f32)

    @pl.loop(2, 2 + layers)
    def _(layer):
        for row in range(PAD, last, 8):
            result = step(mid, layer, row, 0)
            for i in range(3):
                vel_out[i, layer - 2, row - PAD : row - PAD + 8, :] = result[i]
            pre_out[layer - 2, row - PAD : row - PAD + 8, :] = result[3]

    slots = cell.shape[0]
    cells = layers * rows
    flat = pre_out[...].reshape(cells, height)
    place = cell[...]
    column = place // height
    level = place - column * height
    pick = (lax.broadcasted_iota(jnp.int32, (slots, cells), 1) == column).astype(f32).astype(bf16)
    found = jnp.zeros((slots, height), f32)
    for part in parts_of(flat):
        found = found + jnp.dot(pick, part.astype(bf16), preferred_element_type=f32)
    at_level = lax.broadcasted_iota(jnp.int32, (slots, height), 1) == level
    sampled = jnp.sum(jnp.where(at_level, found, 0.0), axis=1, keepdims=True)
    loads = (area[...] * sampled).astype(bf16).astype(f32)
    same = lax.broadcasted_iota(jnp.int32, (LANES, LANES), 0) == lax.broadcasted_iota(
        jnp.int32, (LANES, LANES), 1
    )
    lines = []
    for start in range(0, slots, LANES):
        chosen = jnp.where(same, loads[start : start + LANES], 0.0)
        lines.append(jnp.sum(chosen, axis=0, keepdims=True))
    message = jnp.concatenate(lines + [partial[...]], axis=0)
    payload[...] = jnp.broadcast_to(message[None], payload.shape)


def respond(stretch, rate, hysteresis, coefficients):
    hysteresis = hysteresis + modal_step * (
        rate
        - shape_beta * jnp.abs(rate) * hysteresis
        - shape_gamma * rate * jnp.abs(hysteresis)
    )
    force = -(
        coefficients[0:1] * rate + spring_rate * stretch + coefficients[1:2] * hysteresis
    )
    return hysteresis, force


def pulled(forces, shapes):
    sides = []
    for force in forces:
        three = jnp.concatenate(parts_of(force) + [jnp.zeros((13, force.shape[1]), f32)], axis=0)
        sides += [three, -three]
    left = jnp.concatenate(sides, axis=1).astype(bf16)
    right = shapes[...].reshape(-1, shapes.shape[-1])
    return jnp.sum(jnp.dot(left, right, preferred_element_type=f32), axis=0, keepdims=True)


def advance_modes(load, modes, displacement, velocity):
    frequency = modes[2:3]
    acceleration = (
        load
        - 2.0 * modes[3:4] * frequency * velocity
        - frequency * frequency * displacement
    )
    velocity = velocity + modal_step * acceleration
    return displacement + modal_step * velocity, velocity


def first_kernel(count_x, count_y, load_rows, *refs):
    received, panels, dampers, shapes, modes = refs[:5]
    tables = refs[5 : 5 + count_y]
    payload, state, hysteresis_out, held, sem = refs[5 + count_y :]
    iy = lax.axis_index("gy")
    copies = [
        pltpu.make_async_copy(tables[q], held.at[q], sem.at[q]) for q in range(count_y)
    ]
    for copy in copies:
        copy.start()
    panel_count = tables[0].shape[0]
    high_count = panel_count // LANES
    slot_count = panels.shape[-1]
    rank = lax.broadcasted_iota(jnp.int32, (high_count, LANES), 0)
    low_rank = lax.broadcasted_iota(jnp.int32, (LANES, slot_count), 0)
    sides = []
    forces = []
    for q in range(count_y):
        piece = lax.rem(iy + q, count_y)
        ids = panels[q]
        high = ids // LANES
        high = jnp.where(ids < 0, -1, high)
        low = ids - high * LANES
        chunks = []
        for i in range(count_x):
            for r in range(load_rows):
                start = (i * load_rows + r) * LANES
                line = received[i, piece, r : r + 1, :]
                chunks.append(
                    jnp.where(rank == high[:, start : start + LANES], line, 0.0).astype(bf16)
                )
        spread = (low_rank == low).astype(f32).astype(bf16)
        sorted_loads = lax.dot_general(
            jnp.concatenate(chunks, axis=1),
            spread,
            (((1,), (1,)), ((), ())),
            preferred_element_type=f32,
        )
        sides.append(
            jnp.concatenate(
                [jnp.where(rank == c, sorted_loads, 0.0).astype(bf16) for c in range(high_count)],
                axis=1,
            )
        )
        stretch = received[0, piece, load_rows : load_rows + 1, :]
        rate = received[0, piece, load_rows + 1 : load_rows + 2, :]
        for i in range(1, count_x):
            stretch = stretch + received[i, piece, load_rows : load_rows + 1, :]
            rate = rate + received[i, piece, load_rows + 1 : load_rows + 2, :]
        coefficients = dampers[q]
        hysteresis, force = respond(stretch, rate, coefficients[2:3], coefficients)
        hysteresis_out[q] = hysteresis
        forces.append(force)
    for copy in copies:
        copy.wait()
    rows = jnp.zeros((high_count, modes.shape[1]), f32)
    for q in range(count_y):
        rows = rows + jnp.dot(sides[q], held[q], preferred_element_type=f32)
    panel_modal = jnp.sum(rows, axis=0, keepdims=True)
    table = modes[...]
    load = panel_modal + pulled(forces, shapes)
    displacement, velocity = advance_modes(load, table, table[0:1], table[1:2])
    state[0:1, :] = displacement
    state[1:2, :] = velocity
    state[2:3, :] = panel_modal
    state[3:4, :] = panel_modal
    pair = lax.dot_general(
        stacked(parts_of(displacement) + parts_of(velocity)),
        shapes[0].reshape(-1, shapes.shape[-1]),
        (((1,), (1,)), ((), ())),
        preferred_element_type=f32,
    )
    width = pair.shape[1] // 2
    drift = pair[:, :width] - pair[:, width:]
    message = jnp.concatenate(
        [
            jnp.sum(drift[0:3], axis=0, keepdims=True),
            jnp.sum(drift[3:6], axis=0, keepdims=True),
        ],
        axis=0,
    )
    payload[...] = jnp.broadcast_to(message[None], payload.shape)


def second_kernel(count_x, count_y, received, dampers, shapes, modes, state, held, modal, damper):
    iy = lax.axis_index("gy")
    forces = []
    for q in range(count_y):
        piece = lax.rem(iy + q, count_y)
        stretch = received[0, piece, 0:1, :]
        rate = received[0, piece, 1:2, :]
        for i in range(1, count_x):
            stretch = stretch + received[i, piece, 0:1, :]
            rate = rate + received[i, piece, 1:2, :]
        hysteresis, force = respond(stretch, rate, held[q], dampers[q])
        if q == 0:
            damper[...] = hysteresis
        forces.append(force)
    load = state[2:3, :] + pulled(forces, shapes)
    displacement, velocity = advance_modes(load, modes[...], state[0:1, :], state[1:2, :])
    modal[0:1, :] = displacement
    modal[1:2, :] = velocity


def whole(space=pltpu.VMEM):
    return pl.BlockSpec(memory_space=space)


def body(
    velocity,
    pressure,
    viscosity,
    wind_profile,
    panel_area,
    slot_cell,
    slot_panel,
    panel_shapes,
    node_shapes,
    damper_node,
    damper_viscous,
    damper_hysteretic,
    frequency,
    damping_ratio,
    modal_state,
    damper_state,
):
    count_x = lax.axis_size("gx")
    count_y = lax.axis_size("gy")
    total = count_x * count_y
    both = ("gx", "gy")
    ix = lax.axis_index("gx")
    iy = lax.axis_index("gy")
    layers, rows, height = pressure.shape
    slots = slot_cell.shape[1]
    slots_padded = -(-slots // LANES) * LANES
    load_rows = slots_padded // LANES
    damper_count = damper_node.shape[0]
    damper_padded = -(-damper_count // LANES) * LANES
    mode_count = frequency.shape[0]

    def side(start):
        parts = [velocity, pressure[None], viscosity[None]]
        cut = [lax.dynamic_slice_in_dim(part, start, PAD, axis=2) for part in parts]
        return jnp.concatenate(cut, axis=0)

    if count_y == 2:
        facing = side(jnp.where(iy == 0, rows - PAD, 0))
        left = right = lax.ppermute(facing, "gy", [(0, 1), (1, 0)])
    else:
        left = lax.ppermute(side(rows - PAD), "gy", shifts(count_y, 1, False))
        right = lax.ppermute(side(0), "gy", shifts(count_y, -1, False))

    def message(first, near):
        fields = jnp.concatenate(
            [velocity[:, first : first + 2], pressure[None, first : first + 2]], axis=0
        )
        corner_left = jnp.where(iy > 0, left[:4, near, PAD - 1], 0.0)
        corner_right = jnp.where(iy < count_y - 1, right[:4, near, 0], 0.0)
        return jnp.concatenate(
            [
                fields.reshape(8 * rows, height).astype(bf16),
                viscosity[near].astype(bf16),
                corner_left.astype(bf16),
                corner_right.astype(bf16),
                jnp.zeros((8, height), bf16),
            ],
            axis=0,
        )

    before = lax.ppermute(message(layers - 2, layers - 1), "gx", shifts(count_x, 1, False))
    after = lax.ppermute(message(0, 0), "gx", shifts(count_x, -1, False))

    def around(value):
        return [value] + [
            lax.ppermute(value, "gy", shifts(count_y, q, True)) for q in range(1, count_y)
        ]

    tables = around(panel_shapes)
    small = jnp.concatenate(
        [
            damper_viscous,
            damper_hysteretic,
            damper_state,
            damper_node.astype(f32),
            slot_panel[0].astype(f32),
        ]
    )
    smalls = jnp.stack(around(small))
    cut = 4 * damper_count
    dampers = smalls[:, :cut].reshape(count_y, 4, damper_count)
    dampers = jnp.pad(dampers, ((0, 0), (0, 0), (0, damper_padded - damper_count)))
    nodes = smalls[:, cut - damper_count : cut].astype(jnp.int32)
    nodes = jnp.pad(
        nodes, ((0, 0), (0, damper_padded - damper_count)), constant_values=-2
    )
    panels = smalls[:, cut:].astype(jnp.int32).reshape(count_y, count_x, slots)
    panels = jnp.pad(panels, ((0, 0), (0, 0), (0, slots_padded - slots)), constant_values=-1)
    panels = panels.reshape(count_y, 1, count_x * slots_padded)

    node_numbers = jnp.arange(node_shapes.shape[0], dtype=jnp.int32)
    ends = jnp.stack([nodes + 1, nodes], axis=1)
    ends = jnp.where(ends < 0, -1, ends).reshape(-1, 1)
    chosen = (ends == node_numbers[None, :]).astype(bf16)
    shapes = jnp.dot(chosen, node_shapes, preferred_element_type=f32).astype(bf16)
    shapes = shapes.reshape(count_y, 2, damper_padded, mode_count)
    drift = shapes[0, 0].astype(f32) - shapes[0, 1].astype(f32)
    partial = lax.dot_general(
        modal_state, drift, (((1,), (1,)), ((), ())), precision=lax.Precision.HIGHEST
    )

    own_ids = lax.dynamic_slice_in_dim(slot_panel[0], ix * slots, slots)
    area = jnp.where(own_ids < 0, 0.0, panel_area[jnp.maximum(own_ids, 0)])
    area = jnp.pad(area, (0, slots_padded - slots))[:, None]
    cell = jnp.pad(slot_cell[0], (0, slots_padded - slots))[:, None]

    padded = (4, layers + 4, rows + 2 * PAD, height)
    message_rows = load_rows + 2
    velocity_next, pressure_next, payload = pl.pallas_call(
        functools.partial(flow_kernel, count_x, count_y),
        out_shape=(
            jax.ShapeDtypeStruct(velocity.shape, f32),
            jax.ShapeDtypeStruct(pressure.shape, f32),
            jax.ShapeDtypeStruct((total, message_rows, LANES), f32),
        ),
        in_specs=[whole(pl.ANY)] * 3
        + [whole()] * 3
        + [whole(pl.ANY)] * 2
        + [whole()] * 3,
        out_specs=(whole(), whole(), whole()),
        scratch_shapes=[
            pltpu.VMEM(padded, f32),
            pltpu.VMEM(padded, f32),
            pltpu.VMEM(padded[1:], f32),
            pltpu.SemaphoreType.DMA((9,)),
        ],
        compiler_params=pltpu.CompilerParams(vmem_limit_bytes=VMEM_BYTES),
        name="flow",
    )(
        velocity,
        pressure,
        viscosity,
        wind_profile[None, :],
        before,
        after,
        left,
        right,
        cell,
        area,
        partial,
    )
    received = lax.all_to_all(payload, both, 0, 0, tiled=True)
    received = received.reshape(count_x, count_y, message_rows, LANES)

    modes = jnp.concatenate([modal_state, frequency[None], damping_ratio[None]], axis=0)
    payload, state, hysteresis = pl.pallas_call(
        functools.partial(first_kernel, count_x, count_y, load_rows),
        out_shape=(
            jax.ShapeDtypeStruct((total, 2, damper_padded), f32),
            jax.ShapeDtypeStruct((4, mode_count), f32),
            jax.ShapeDtypeStruct((count_y, 1, damper_padded), f32),
        ),
        in_specs=[whole()] * 5 + [whole(pl.ANY)] * count_y,
        out_specs=(whole(), whole(), whole()),
        scratch_shapes=[
            pltpu.VMEM((count_y,) + panel_shapes.shape, bf16),
            pltpu.SemaphoreType.DMA((count_y,)),
        ],
        compiler_params=pltpu.CompilerParams(vmem_limit_bytes=VMEM_BYTES),
        name="first",
    )(received, panels, dampers, shapes, modes, *tables)
    received = lax.all_to_all(payload, both, 0, 0, tiled=True)
    received = received.reshape(count_x, count_y, 2, damper_padded)

    modal_next, damper_next = pl.pallas_call(
        functools.partial(second_kernel, count_x, count_y),
        out_shape=(
            jax.ShapeDtypeStruct((2, mode_count), f32),
            jax.ShapeDtypeStruct((1, damper_padded), f32),
        ),
        in_specs=[whole()] * 6,
        out_specs=(whole(), whole()),
        compiler_params=pltpu.CompilerParams(vmem_limit_bytes=VMEM_BYTES),
        name="second",
    )(received, dampers, shapes, modes, state, hysteresis)
    return (velocity_next, pressure_next, modal_next, damper_next[0, :damper_count])


def solution(mesh):
    placed = (
        P(None, "gx", "gy", None),
        P("gx", "gy", None),
        P("gx", "gy", None),
        P(),
        P("gy"),
        P("gy", "gx"),
        P("gy", None),
        P("gy", "gx"),
        P(None, "gx"),
        P("gy"),
        P("gy"),
        P("gy"),
        P("gx"),
        P("gx"),
        P(None, "gx"),
        P("gy"),
    )
    return jax.shard_map(
        body,
        mesh=mesh,
        in_specs=placed,
        out_specs=(P(None, "gx", "gy", None), P("gx", "gy", None), P(None, "gx"), P("gy")),
        check_vma=False,
    )
```

```python
import functools

import jax
import jax.numpy as jnp
from jax import lax
from jax.experimental import pallas as pl
from jax.experimental.pallas import tpu as pltpu
from jax.sharding import PartitionSpec as P

f32 = jnp.float32
bf16 = jnp.bfloat16
time_step = 0.1
modal_step = 0.5
shape_beta = 0.5
shape_gamma = 0.5
spring_rate = 0.5
LANES = 128
PAD = 8
VMEM_BYTES = 40 * 1024 * 1024


def shifts(size, step, cyclic):
    if cyclic:
        return [((i + step) % size, i) for i in range(size)]
    return [(i, i + step) for i in range(size) if 0 <= i + step < size]


def parts_of(row):
    high = row.astype(bf16).astype(f32)
    rest = row - high
    middle = rest.astype(bf16).astype(f32)
    return [high, middle, rest - middle]


def stacked(rows):
    filler = jnp.zeros((16 - len(rows), rows[0].shape[1]), f32)
    return jnp.concatenate(rows + [filler], axis=0).astype(bf16)


def side_kernel(starts, vel, pre, vis, *refs):
    outs, sem = refs[:-1], refs[-1]
    copies = []
    for place, (start, out) in enumerate(zip(starts, outs)):
        if start is None:
            start = jnp.where(lax.axis_index("gy") == 0, pre.shape[1] - PAD, 0)
        here = pl.ds(pl.multiple_of(start, PAD), PAD)
        copies += [
            pltpu.make_async_copy(vel.at[:, :, here], out.at[pl.ds(0, 3)], sem.at[place, 0]),
            pltpu.make_async_copy(pre.at[:, here], out.at[3], sem.at[place, 1]),
            pltpu.make_async_copy(vis.at[:, here], out.at[4], sem.at[place, 2]),
        ]
    for copy in copies:
        copy.start()
    for copy in copies:
        copy.wait()


def pack_kernel(count_y, vel, pre, vis, left, right, up, down, stage, corner, sem):
    layers, rows, height = pre.shape
    iy = lax.axis_index("gy")
    has = (iy > 0, iy < count_y - 1)
    messages = ((up, layers - 2, layers - 1), (down, 0, 0))
    copies = []
    for side, (out, first, near) in enumerate(messages):
        copies += [
            pltpu.make_async_copy(
                vel.at[:, pl.ds(first, 2)], stage.at[side, pl.ds(0, 3)], sem.at[side, 0]
            ),
            pltpu.make_async_copy(pre.at[pl.ds(first, 2)], stage.at[side, 3], sem.at[side, 1]),
            pltpu.make_async_copy(vis.at[near], stage.at[side, 4, 0], sem.at[side, 2]),
            pltpu.make_async_copy(
                left.at[pl.ds(0, 4), near], corner.at[side, 0], sem.at[side, 3]
            ),
            pltpu.make_async_copy(
                right.at[pl.ds(0, 4), near], corner.at[side, 1], sem.at[side, 4]
            ),
        ]
    for copy in copies:
        copy.start()
    for copy in copies:
        copy.wait()
    for side, (out, first, near) in enumerate(messages):
        for field in range(4):
            for depth in range(2):
                start = (field * 2 + depth) * rows
                out[start : start + rows, :] = stage[side, field, depth].astype(bf16)
        out[8 * rows : 9 * rows, :] = stage[side, 4, 0].astype(bf16)
        lines = [corner[side, 0, f, PAD - 1 : PAD, :] for f in range(4)]
        lines = [jnp.where(has[0], line, 0.0) for line in lines]
        others = [corner[side, 1, f, 0:1, :] for f in range(4)]
        lines += [jnp.where(has[1], line, 0.0) for line in others]
        lines.append(jnp.zeros((8, height), f32))
        out[9 * rows : 9 * rows + 16, :] = jnp.concatenate(lines, axis=0).astype(bf16)


def stepper(wind, height):
    lane = lax.broadcasted_iota(jnp.int32, (8, height), 1)
    top = lane == height - 1
    bottom = lane == 0
    half = 0.5 * time_step
    wind_part = jnp.broadcast_to(wind[...] * half, (8, height))

    def step(get, factor, row, edge):
        def at(offset, low):
            return [get(f, offset, low) for f in range(4)]

        centre, ahead, behind = at(0, row), at(1, row), at(-1, row)
        lower = [pltpu.roll(c, 1, 0) for c in centre] if edge < 0 else at(0, row - 1)
        upper = [pltpu.roll(c, 7, 0) for c in centre] if edge > 0 else at(0, row + 1)
        above = [jnp.where(top, 0.0, pltpu.roll(c, height - 1, 1)) for c in centre]
        below = [jnp.where(bottom, 0.0, pltpu.roll(c, 1, 1)) for c in centre]
        factor = factor * time_step
        slopes = (ahead[3] - behind[3], upper[3] - lower[3], above[3] - below[3])
        result = []
        for i in range(3):
            around = (ahead[i] + behind[i]) + (upper[i] + lower[i]) + (above[i] + below[i])
            result.append(
                centre[i]
                + factor * (around - 6.0 * centre[i])
                - wind_part * (ahead[i] - behind[i])
                - half * slopes[i]
            )
        result.append(
            centre[3]
            - half * ((ahead[0] - behind[0]) + (upper[1] - lower[1]) + (above[2] - below[2]))
        )
        return result

    return step


def inner_kernel(
    count_y, vel, pre, vis, wind, left, right,
    vel_out, old_edge, mid_edge, visc_edge, pre_core,
    old, mid, visc, vel_core, sem, out_sem,
):
    layers, rows, height = pre.shape
    last = PAD + rows
    iy = lax.axis_index("gy")
    has_left = iy > 0
    has_right = iy < count_y - 1
    core = pl.ds(PAD, rows)
    copies = [
        pltpu.make_async_copy(vel.at[i], old.at[i, :, core], sem.at[i]) for i in range(3)
    ]
    copies.append(pltpu.make_async_copy(pre, old.at[3, :, core], sem.at[3]))
    copies.append(pltpu.make_async_copy(vis, visc.at[:, core], sem.at[4]))
    for place, (source, row) in enumerate(((left, 0), (right, last))):
        copies.append(
            pltpu.make_async_copy(
                source.at[pl.ds(0, 4)], old.at[:, :, pl.ds(row, PAD)], sem.at[5 + 2 * place]
            )
        )
        copies.append(
            pltpu.make_async_copy(
                source.at[4], visc.at[:, pl.ds(row, PAD)], sem.at[6 + 2 * place]
            )
        )
    for copy in copies:
        copy.start()
    for copy in copies:
        copy.wait()
    blank = jnp.zeros((4, layers, PAD, height), f32)

    @pl.when(jnp.logical_not(has_left))
    def _():
        old[:, :, 0:PAD, :] = blank
        mid[:, :, 0:PAD, :] = blank

    @pl.when(jnp.logical_not(has_right))
    def _():
        old[:, :, last : last + PAD, :] = blank
        mid[:, :, last : last + PAD, :] = blank

    step = stepper(wind, height)

    def advance(source, layer, row, edge=0):
        def get(f, offset, low):
            return source[f, layer + offset, pl.ds(low, 8), :]

        return step(get, visc[layer, pl.ds(row, 8), :], row, edge)

    def first(layer, row, edge=0):
        result = advance(old, layer, row, edge)
        for f in range(4):
            mid[f, layer, pl.ds(row, 8), :] = result[f]

    @pl.loop(1, layers - 1)
    def _(layer):
        for row in range(PAD, last, 8):
            first(layer, row)

    @pl.when(has_left)
    def _():
        @pl.loop(1, layers - 1)
        def _(layer):
            first(layer, 0, -1)

    @pl.when(has_right)
    def _():
        @pl.loop(1, layers - 1)
        def _(layer):
            first(layer, last, 1)

    @pl.loop(2, layers - 2)
    def _(layer):
        for row in range(PAD, last, 8):
            result = advance(mid, layer, row)
            for i in range(3):
                vel_core[i, layer - 2, row - PAD : row - PAD + 8, :] = result[i]
            pre_core[layer - 2, row - PAD : row - PAD + 8, :] = result[3]

    result = pltpu.make_async_copy(
        vel_core, vel_out.at[:, pl.ds(2, layers - 4)], out_sem
    )
    result.start()
    for side, first_old, place_old, first_mid, place_mid in (
        (0, 0, 2, 1, 3),
        (1, layers - 2, 1, layers - 3, 0),
    ):
        for depth in range(2):
            visc_edge[side, place_old + depth] = visc[first_old + depth]
            for f in range(4):
                old_edge[side, f, place_old + depth] = old[f, first_old + depth]
                mid_edge[side, f, place_mid + depth] = mid[f, first_mid + depth]
    result.wait()


def edge_kernel(
    count_x, count_y, before, after, wind, cell, area, partial, pre_core,
    vel_in, old_in, mid_in, visc_in,
    vel_out, pre_out, payload, old, mid, visc,
    stage, pre_full, vel_edge, sem, out_sem,
):
    layers, rows, height = pre_full.shape
    last = PAD + rows
    ix = lax.axis_index("gx")
    iy = lax.axis_index("gy")
    has_left = iy > 0
    has_right = iy < count_y - 1
    has_before = ix > 0
    has_after = ix < count_x - 1
    copies = [
        pltpu.make_async_copy(message, stage.at[side], sem.at[side])
        for side, message in enumerate((before, after))
    ]
    for copy in copies:
        copy.start()
    pre_full[2 : layers - 2] = pre_core[...]
    slots = cell.shape[1]
    cells = layers * rows
    same = lax.broadcasted_iota(jnp.int32, (LANES, LANES), 0) == lax.broadcasted_iota(
        jnp.int32, (LANES, LANES), 1
    )
    place = cell[...]
    line = place // height
    level = place - line * height

    def stand(row):
        lines = [
            jnp.sum(jnp.where(same, row[:, k : k + LANES], 0.0), axis=1, keepdims=True)
            for k in range(0, slots, LANES)
        ]
        return jnp.concatenate(lines, axis=0)

    line, level = stand(line.astype(f32)), stand(level.astype(f32))
    own_area = stand(area[...])
    pick = lax.broadcasted_iota(jnp.int32, (slots, cells), 1).astype(f32) == line
    pick = pick.astype(f32).astype(bf16)
    at_level = lax.broadcasted_iota(jnp.int32, (slots, height), 1).astype(f32) == level
    for copy in copies:
        copy.wait()
    for side in range(2):
        near = 1 + 2 * side
        for field in range(4):
            for depth in range(2):
                start = (field * 2 + depth) * rows
                old[side, field, 3 * side + depth, PAD:last, :] = stage[
                    side, start : start + rows, :
                ].astype(f32)
        visc[side, near, PAD:last, :] = stage[side, 8 * rows : 9 * rows, :].astype(f32)
        corner = stage[side, 9 * rows : 9 * rows + 16, :].astype(f32)
        for field in range(4):
            old[side, field, near, PAD - 1 : PAD, :] = corner[field : field + 1]
            old[side, field, near, last : last + 1, :] = corner[4 + field : 5 + field]

    step = stepper(wind, height)

    def advance(source, side, layer, row, edge=0):
        def get(f, offset, low):
            return source[side, f, layer + offset, pl.ds(low, 8), :]

        return step(get, visc[side, layer, pl.ds(row, 8), :], row, edge)

    def first(side, layer, row, edge=0):
        result = advance(old, side, layer, row, edge)
        for f in range(4):
            mid[side, f, layer, pl.ds(row, 8), :] = result[f]

    blank = jnp.zeros((4, PAD, height), f32)

    @pl.loop(0, 2)
    def _(side):
        there = jnp.where(side == 0, has_before, has_after)
        outside = 1 + 2 * side
        for row in range(PAD, last, 8):
            first(side, 2, row)

        @pl.when(has_left)
        def _():
            first(side, 2, 0, -1)

        @pl.when(jnp.logical_not(has_left))
        def _():
            mid[side, :, 2, 0:PAD, :] = blank

        @pl.when(has_right)
        def _():
            first(side, 2, last, 1)

        @pl.when(jnp.logical_not(has_right))
        def _():
            mid[side, :, 2, last : last + PAD, :] = blank

        @pl.when(there)
        def _():
            for row in range(PAD, last, 8):
                first(side, outside, row)

        @pl.when(jnp.logical_not(there))
        def _():
            mid[side, :, outside, PAD:last, :] = jnp.zeros((4, rows, height), f32)

        for row in range(PAD, last, 8):
            for layer, place in ((2, side), (3 - 2 * side, 1 - side)):
                result = advance(mid, side, layer, row)
                here = pl.ds(row - PAD, 8)
                for i in range(3):
                    vel_edge[side, i, place, here, :] = result[i]
                pre_full[side * (layers - 2) + place, here, :] = result[3]

    results = [
        pltpu.make_async_copy(
            vel_edge.at[side], vel_out.at[:, pl.ds(side * (layers - 2), 2)], out_sem.at[side]
        )
        for side in range(2)
    ]
    results.append(pltpu.make_async_copy(pre_full, pre_out, out_sem.at[2]))
    for result in results:
        result.start()
    flat = pre_full[...].reshape(cells, height)
    found = jnp.zeros((slots, height), f32)
    for part in parts_of(flat):
        found = found + jnp.dot(pick, part.astype(bf16), preferred_element_type=f32)
    sampled = jnp.sum(jnp.where(at_level, found, 0.0), axis=1, keepdims=True)
    loads = (own_area * sampled).astype(bf16).astype(f32)
    lines = []
    for start in range(0, slots, LANES):
        chosen = jnp.where(same, loads[start : start + LANES], 0.0)
        lines.append(jnp.sum(chosen, axis=0, keepdims=True))
    message = jnp.concatenate(lines + [partial[...]], axis=0)
    payload[...] = jnp.broadcast_to(message[None], payload.shape)
    for result in results:
        result.wait()


def prepare_kernel(slot_count, damper_width, own_ids, areas, nodes, modal, *refs):
    smalls = refs[:-3]
    shapes, partial, area = refs[-3:]
    high_count = areas.shape[0]
    slots = own_ids.shape[1]
    ids = own_ids[...]
    high = jnp.where(ids < 0, -1, ids // LANES)
    low = ids - high * LANES
    high_pick = lax.broadcasted_iota(jnp.int32, (high_count, slots), 0) == high
    low_pick = lax.broadcasted_iota(jnp.int32, (LANES, slots), 0) == low
    high_pick = high_pick.astype(f32).astype(bf16)
    spread = jnp.zeros((LANES, slots), f32)
    for part in parts_of(areas[...]):
        spread = spread + lax.dot_general(
            part.astype(bf16),
            high_pick,
            (((0,), (0,)), ((), ())),
            preferred_element_type=f32,
        )
    area[...] = jnp.sum(jnp.where(low_pick, spread, 0.0), axis=0, keepdims=True)
    node_rank = lax.broadcasted_iota(jnp.int32, (nodes.shape[0], damper_width), 0).astype(f32)
    table = nodes[...]
    for q, small in enumerate(smalls):
        lower = small[:, slot_count + 3 * damper_width : slot_count + 4 * damper_width]
        for end in range(2):
            pick = (node_rank == lower + (1.0 - end)).astype(f32).astype(bf16)
            rows = lax.dot_general(
                pick, table, (((0,), (0,)), ((), ())), preferred_element_type=f32
            )
            shapes[q, end] = rows.astype(bf16)
    state = modal[...]
    partial[...] = drift_times(state[0:1], state[1:2], shapes)


def respond(stretch, rate, hysteresis, viscous, hysteretic):
    hysteresis = hysteresis + modal_step * (
        rate
        - shape_beta * jnp.abs(rate) * hysteresis
        - shape_gamma * rate * jnp.abs(hysteresis)
    )
    force = -(viscous * rate + spring_rate * stretch + hysteretic * hysteresis)
    return hysteresis, force


def pulled(forces, shapes):
    sides = []
    for force in forces:
        three = jnp.concatenate(parts_of(force) + [jnp.zeros((13, force.shape[1]), f32)], axis=0)
        sides += [three, -three]
    left = jnp.concatenate(sides, axis=1).astype(bf16)
    right = shapes[...].reshape(-1, shapes.shape[-1])
    return jnp.sum(jnp.dot(left, right, preferred_element_type=f32), axis=0, keepdims=True)


def drift_times(displacement, velocity, shapes):
    pair = lax.dot_general(
        stacked(parts_of(displacement) + parts_of(velocity)),
        shapes[0].reshape(-1, shapes.shape[-1]),
        (((1,), (1,)), ((), ())),
        preferred_element_type=f32,
    )
    width = pair.shape[1] // 2
    drift = pair[:, :width] - pair[:, width:]
    return jnp.concatenate(
        [
            jnp.sum(drift[0:3], axis=0, keepdims=True),
            jnp.sum(drift[3:6], axis=0, keepdims=True),
        ],
        axis=0,
    )


def advance_modes(load, frequency, ratio, displacement, velocity):
    acceleration = (
        load
        - 2.0 * ratio * frequency * velocity
        - frequency * frequency * displacement
    )
    velocity = velocity + modal_step * acceleration
    return displacement + modal_step * velocity, velocity


def damper_rows(small, slot_count, width):
    return [small[:, slot_count + k * width : slot_count + (k + 1) * width] for k in range(3)]


def first_kernel(count_x, count_y, load_rows, *refs):
    received, shapes, modal, frequency, ratio = refs[:5]
    smalls = refs[5 : 5 + count_y]
    tables = refs[5 + count_y : 5 + 2 * count_y]
    payload, state, hysteresis_out, held, sem = refs[5 + 2 * count_y :]
    iy = lax.axis_index("gy")
    copies = [
        pltpu.make_async_copy(tables[q], held.at[q], sem.at[q]) for q in range(count_y)
    ]
    for copy in copies:
        copy.start()
    panel_count = tables[0].shape[0]
    high_count = panel_count // LANES
    slot_count = count_x * load_rows * LANES
    width = payload.shape[-1]
    rank = lax.broadcasted_iota(jnp.int32, (high_count, LANES), 0).astype(f32)
    low_rank = lax.broadcasted_iota(jnp.int32, (LANES, slot_count), 0).astype(f32)
    sides = []
    forces = []
    for q in range(count_y):
        piece = lax.rem(iy + q, count_y)
        ids = smalls[q][:, :slot_count]
        high = jnp.floor(ids * (1.0 / LANES))
        low = ids - high * LANES
        chunks = []
        for i in range(count_x):
            for r in range(load_rows):
                start = (i * load_rows + r) * LANES
                line = received[i, piece, r : r + 1, :]
                chunks.append(
                    jnp.where(rank == high[:, start : start + LANES], line, 0.0).astype(bf16)
                )
        spread = (low_rank == low).astype(f32).astype(bf16)
        sorted_loads = lax.dot_general(
            jnp.concatenate(chunks, axis=1),
            spread,
            (((1,), (1,)), ((), ())),
            preferred_element_type=f32,
        )
        sides.append(
            jnp.concatenate(
                [jnp.where(rank == c, sorted_loads, 0.0).astype(bf16) for c in range(high_count)],
                axis=1,
            )
        )
        stretch = received[0, piece, load_rows : load_rows + 1, :]
        rate = received[0, piece, load_rows + 1 : load_rows + 2, :]
        for i in range(1, count_x):
            stretch = stretch + received[i, piece, load_rows : load_rows + 1, :]
            rate = rate + received[i, piece, load_rows + 1 : load_rows + 2, :]
        viscous, hysteretic, held_state = damper_rows(smalls[q], slot_count, width)
        hysteresis, force = respond(stretch, rate, held_state, viscous, hysteretic)
        hysteresis_out[q] = hysteresis
        forces.append(force)
    load = pulled(forces, shapes)
    for copy in copies:
        copy.wait()
    rows = jnp.zeros((high_count, modal.shape[1]), f32)
    for q in range(count_y):
        rows = rows + jnp.dot(sides[q], held[q], preferred_element_type=f32)
    panel_modal = jnp.sum(rows, axis=0, keepdims=True)
    displacement, velocity = advance_modes(
        panel_modal + load, frequency[...], ratio[...], modal[0:1, :], modal[1:2, :]
    )
    state[0:1, :] = displacement
    state[1:2, :] = velocity
    state[2:3, :] = panel_modal
    state[3:4, :] = panel_modal
    message = drift_times(displacement, velocity, shapes)
    payload[...] = jnp.broadcast_to(message[None], payload.shape)


def second_kernel(count_x, count_y, slot_count, *refs):
    received, shapes, frequency, ratio, state, held = refs[:6]
    smalls = refs[6 : 6 + count_y]
    modal, damper = refs[6 + count_y :]
    iy = lax.axis_index("gy")
    forces = []
    for q in range(count_y):
        piece = lax.rem(iy + q, count_y)
        stretch = received[0, piece, 0:1, :]
        rate = received[0, piece, 1:2, :]
        for i in range(1, count_x):
            stretch = stretch + received[i, piece, 0:1, :]
            rate = rate + received[i, piece, 1:2, :]
        viscous, hysteretic, _ = damper_rows(smalls[q], slot_count, stretch.shape[1])
        hysteresis, force = respond(stretch, rate, held[q], viscous, hysteretic)
        if q == 0:
            damper[...] = hysteresis[:, : damper.shape[1]]
        forces.append(force)
    load = state[2:3, :] + pulled(forces, shapes)
    displacement, velocity = advance_modes(
        load, frequency[...], ratio[...], state[0:1, :], state[1:2, :]
    )
    modal[0:1, :] = displacement
    modal[1:2, :] = velocity


def whole(space=pltpu.VMEM):
    return pl.BlockSpec(memory_space=space)


def body(
    velocity,
    pressure,
    viscosity,
    wind_profile,
    panel_area,
    slot_cell,
    slot_panel,
    panel_shapes,
    node_shapes,
    damper_node,
    damper_viscous,
    damper_hysteretic,
    frequency,
    damping_ratio,
    modal_state,
    damper_state,
):
    count_x = lax.axis_size("gx")
    count_y = lax.axis_size("gy")
    total = count_x * count_y
    both = ("gx", "gy")
    ix = lax.axis_index("gx")
    layers, rows, height = pressure.shape
    slots = slot_cell.shape[1]
    slots_padded = -(-slots // LANES) * LANES
    load_rows = slots_padded // LANES
    slot_count = count_x * slots_padded
    damper_count = damper_node.shape[0]
    damper_padded = -(-damper_count // LANES) * LANES
    mode_count = frequency.shape[0]
    params = pltpu.CompilerParams(vmem_limit_bytes=VMEM_BYTES)
    shape = jax.ShapeDtypeStruct

    starts = (None,) if count_y == 2 else (rows - PAD, 0)
    sides = pl.pallas_call(
        functools.partial(side_kernel, starts),
        out_shape=tuple(shape((5, layers, PAD, height), f32) for _ in starts),
        in_specs=[whole(pl.ANY)] * 3,
        out_specs=tuple(whole(pl.ANY) for _ in starts),
        scratch_shapes=[pltpu.SemaphoreType.DMA((len(starts), 3))],
        compiler_params=params,
        name="side",
    )(velocity, pressure, viscosity)
    if count_y == 2:
        left = right = lax.ppermute(sides[0], "gy", [(0, 1), (1, 0)])
    else:
        left = lax.ppermute(sides[0], "gy", shifts(count_y, 1, False))
        right = lax.ppermute(sides[1], "gy", shifts(count_y, -1, False))

    message_shape = (9 * rows + 16, height)
    up, down = pl.pallas_call(
        functools.partial(pack_kernel, count_y),
        out_shape=(shape(message_shape, bf16), shape(message_shape, bf16)),
        in_specs=[whole(pl.ANY)] * 5,
        out_specs=(whole(), whole()),
        scratch_shapes=[
            pltpu.VMEM((2, 5, 2, rows, height), f32),
            pltpu.VMEM((2, 2, 4, PAD, height), f32),
            pltpu.SemaphoreType.DMA((2, 5)),
        ],
        compiler_params=params,
        name="pack",
    )(velocity, pressure, viscosity, left, right)
    tied = lax.optimization_barrier(
        (
            up, down, left, right, panel_shapes, node_shapes, panel_area, slot_panel,
            damper_node, damper_viscous, damper_hysteretic, damper_state, modal_state,
        )
    )
    (
        up, down, left, right, panel_shapes, node_shapes, panel_area, slot_panel,
        damper_node, damper_viscous, damper_hysteretic, damper_state, modal_state,
    ) = tied
    before = lax.ppermute(up, "gx", shifts(count_x, 1, False))
    after = lax.ppermute(down, "gx", shifts(count_x, -1, False))

    def around(value):
        return [value] + [
            lax.ppermute(value, "gy", shifts(count_y, q, True)) for q in range(1, count_y)
        ]

    def damper_row(value, filler=0.0):
        extra = damper_padded - damper_count
        return jnp.pad(value, (0, extra), constant_values=filler)[None]

    tables = around(panel_shapes)
    ids = slot_panel
    if slots != slots_padded:
        ids = jnp.pad(
            ids.reshape(count_x, slots),
            ((0, 0), (0, slots_padded - slots)),
            constant_values=-1,
        ).reshape(1, slot_count)
    own_ids = lax.dynamic_slice_in_dim(ids, ix * slots_padded, slots_padded, axis=1)
    small = jnp.concatenate(
        [
            ids.astype(f32),
            damper_row(damper_viscous),
            damper_row(damper_hysteretic),
            damper_row(damper_state),
            damper_row(damper_node.astype(f32), -4.0),
        ],
        axis=1,
    )
    smalls = around(small)
    cell = jnp.pad(slot_cell, ((0, 0), (0, slots_padded - slots)))

    shapes, partial, area = pl.pallas_call(
        functools.partial(prepare_kernel, slot_count, damper_padded),
        out_shape=(
            shape((count_y, 2, damper_padded, mode_count), bf16),
            shape((2, damper_padded), f32),
            shape((1, slots_padded), f32),
        ),
        in_specs=[whole()] * (4 + count_y),
        out_specs=(whole(), whole(), whole()),
        compiler_params=params,
        name="prepare",
    )(own_ids, panel_area.reshape(-1, LANES), node_shapes, modal_state, *smalls)

    tall = rows + 2 * PAD
    wind = wind_profile[None, :]
    velocity_next, old, mid, visc, pre_core = pl.pallas_call(
        functools.partial(inner_kernel, count_y),
        out_shape=(
            shape(velocity.shape, f32),
            shape((2, 4, 5, tall, height), f32),
            shape((2, 4, 5, tall, height), f32),
            shape((2, 5, tall, height), f32),
            shape((layers - 4, rows, height), f32),
        ),
        in_specs=[whole(pl.ANY)] * 3 + [whole()] + [whole(pl.ANY)] * 2,
        out_specs=(whole(pl.ANY), whole(), whole(), whole(), whole()),
        scratch_shapes=[
            pltpu.VMEM((4, layers, tall, height), f32),
            pltpu.VMEM((4, layers, tall, height), f32),
            pltpu.VMEM((layers, tall, height), f32),
            pltpu.VMEM((3, layers - 4, rows, height), f32),
            pltpu.SemaphoreType.DMA((9,)),
            pltpu.SemaphoreType.DMA,
        ],
        compiler_params=params,
        name="inner",
    )(velocity, pressure, viscosity, wind, left, right)

    velocity_next, pressure_next, payload, *_ = pl.pallas_call(
        functools.partial(edge_kernel, count_x, count_y),
        out_shape=(
            shape(velocity.shape, f32),
            shape(pressure.shape, f32),
            shape((total, load_rows + 2, LANES), f32),
            shape(old.shape, f32),
            shape(mid.shape, f32),
            shape(visc.shape, f32),
        ),
        in_specs=[whole(pl.ANY)] * 2
        + [whole()] * 5
        + [whole(pl.ANY)]
        + [whole()] * 3,
        out_specs=(whole(pl.ANY), whole(pl.ANY), whole(), whole(), whole(), whole()),
        input_output_aliases={7: 0, 8: 3, 9: 4, 10: 5},
        scratch_shapes=[
            pltpu.VMEM((2,) + message_shape, bf16),
            pltpu.VMEM((layers, rows, height), f32),
            pltpu.VMEM((2, 3, 2, rows, height), f32),
            pltpu.SemaphoreType.DMA((2,)),
            pltpu.SemaphoreType.DMA((3,)),
        ],
        compiler_params=params,
        name="edge",
    )(before, after, wind, cell, area, partial, pre_core, velocity_next, old, mid, visc)
    received = lax.all_to_all(payload, both, 0, 0, tiled=True)
    received = received.reshape(count_x, count_y, load_rows + 2, LANES)

    frequency = frequency[None]
    damping_ratio = damping_ratio[None]
    payload, state, hysteresis = pl.pallas_call(
        functools.partial(first_kernel, count_x, count_y, load_rows),
        out_shape=(
            shape((total, 2, damper_padded), f32),
            shape((4, mode_count), f32),
            shape((count_y, 1, damper_padded), f32),
        ),
        in_specs=[whole()] * (5 + count_y) + [whole(pl.ANY)] * count_y,
        out_specs=(whole(), whole(), whole()),
        scratch_shapes=[
            pltpu.VMEM((count_y,) + panel_shapes.shape, bf16),
            pltpu.SemaphoreType.DMA((count_y,)),
        ],
        compiler_params=params,
        name="first",
    )(received, shapes, modal_state, frequency, damping_ratio, *smalls, *tables)
    received = lax.all_to_all(payload, both, 0, 0, tiled=True)
    received = received.reshape(count_x, count_y, 2, damper_padded)

    modal_next, damper_next = pl.pallas_call(
        functools.partial(second_kernel, count_x, count_y, slot_count),
        out_shape=(
            shape((2, mode_count), f32),
            shape((1, damper_count), f32),
        ),
        in_specs=[whole()] * (6 + count_y),
        out_specs=(whole(), whole()),
        compiler_params=params,
        name="second",
    )(received, shapes, frequency, damping_ratio, state, hysteresis, *smalls)
    return (velocity_next, pressure_next, modal_next, damper_next.reshape(damper_count))


def solution(mesh):
    placed = (
        P(None, "gx", "gy", None),
        P("gx", "gy", None),
        P("gx", "gy", None),
        P(),
        P("gy"),
        P("gy", "gx"),
        P("gy", None),
        P("gy", "gx"),
        P(None, "gx"),
        P("gy"),
        P("gy"),
        P("gy"),
        P("gx"),
        P("gx"),
        P(None, "gx"),
        P("gy"),
    )
    return jax.shard_map(
        body,
        mesh=mesh,
        in_specs=placed,
        out_specs=(P(None, "gx", "gy", None), P("gx", "gy", None), P(None, "gx"), P("gy")),
        check_vma=False,
    )
```

```python
import functools

import jax
import jax.numpy as jnp
from jax import lax
from jax.experimental import pallas as pl
from jax.experimental.pallas import tpu as pltpu
from jax.sharding import PartitionSpec as P

f32 = jnp.float32
bf16 = jnp.bfloat16
time_step = 0.1
modal_step = 0.5
shape_beta = 0.5
shape_gamma = 0.5
spring_rate = 0.5
LANES = 128
PAD = 8
VMEM_BYTES = 40 * 1024 * 1024


def shifts(size, step, cyclic):
    if cyclic:
        return [((i + step) % size, i) for i in range(size)]
    return [(i, i + step) for i in range(size) if 0 <= i + step < size]


def pairs(size, first):
    lower = range(first, size - 1, 2)
    return [(i, i + 1) for i in lower] + [(i + 1, i) for i in lower]


def parts_of(row):
    high = row.astype(bf16).astype(f32)
    rest = row - high
    middle = rest.astype(bf16).astype(f32)
    return [high, middle, rest - middle]


def stacked(rows):
    filler = jnp.zeros((16 - len(rows), rows[0].shape[1]), f32)
    return jnp.concatenate(rows + [filler], axis=0).astype(bf16)


def side_kernel(starts, vel, pre, vis, *refs):
    outs, sem = refs[:-1], refs[-1]
    copies = []
    for place, (start, out) in enumerate(zip(starts, outs)):
        if start is None:
            start = jnp.where(lax.axis_index("gy") == 0, pre.shape[1] - PAD, 0)
        here = pl.ds(pl.multiple_of(start, PAD), PAD)
        copies += [
            pltpu.make_async_copy(vel.at[:, :, here], out.at[pl.ds(0, 3)], sem.at[place, 0]),
            pltpu.make_async_copy(pre.at[:, here], out.at[3], sem.at[place, 1]),
            pltpu.make_async_copy(vis.at[:, here], out.at[4], sem.at[place, 2]),
        ]
    for copy in copies:
        copy.start()
    for copy in copies:
        copy.wait()


def pack_kernel(vel, pre, vis, near_out, far_out, stage, sem):
    layers, rows, height = pre.shape
    odd = lax.rem(lax.axis_index("gx"), 2)
    messages = ((near_out, 1 - odd), (far_out, odd))
    copies = []
    for place, (out, upward) in enumerate(messages):
        first = upward * (layers - 2)
        near = upward * (layers - 1)
        copies += [
            pltpu.make_async_copy(
                vel.at[:, pl.ds(first, 2)], stage.at[place, pl.ds(0, 3)], sem.at[place, 0]
            ),
            pltpu.make_async_copy(pre.at[pl.ds(first, 2)], stage.at[place, 3], sem.at[place, 1]),
            pltpu.make_async_copy(vis.at[near], stage.at[place, 4, 0], sem.at[place, 2]),
        ]
    for copy in copies:
        copy.start()
    for copy in copies:
        copy.wait()
    for place, (out, _) in enumerate(messages):
        for field in range(4):
            for depth in range(2):
                start = (field * 2 + depth) * rows
                out[start : start + rows, :] = stage[place, field, depth].astype(bf16)
        out[8 * rows : 9 * rows, :] = stage[place, 4, 0].astype(bf16)


def corner_kernel(count_y, left, right, near_in, far_in, near_out, far_out):
    layers, height = left.shape[1], left.shape[3]
    start = near_out.shape[0] - 16
    odd = lax.rem(lax.axis_index("gx"), 2)
    iy = lax.axis_index("gy")
    for out, upward in ((near_out, 1 - odd), (far_out, odd)):
        near = upward * (layers - 1)
        lines = [left[f, near, PAD - 1 : PAD, :] for f in range(4)]
        lines = [jnp.where(iy > 0, line, 0.0) for line in lines]
        others = [right[f, near, 0:1, :] for f in range(4)]
        lines += [jnp.where(iy < count_y - 1, line, 0.0) for line in others]
        lines.append(jnp.zeros((8, height), f32))
        out[start : start + 16, :] = jnp.concatenate(lines, axis=0).astype(bf16)


def stepper(wind, height):
    lane = lax.broadcasted_iota(jnp.int32, (8, height), 1)
    top = lane == height - 1
    bottom = lane == 0
    half = 0.5 * time_step
    wind_part = jnp.broadcast_to(wind[...] * half, (8, height))

    def step(get, factor, row, edge):
        def at(offset, low):
            return [get(f, offset, low) for f in range(4)]

        centre, ahead, behind = at(0, row), at(1, row), at(-1, row)
        lower = [pltpu.roll(c, 1, 0) for c in centre] if edge < 0 else at(0, row - 1)
        upper = [pltpu.roll(c, 7, 0) for c in centre] if edge > 0 else at(0, row + 1)
        above = [jnp.where(top, 0.0, pltpu.roll(c, height - 1, 1)) for c in centre]
        below = [jnp.where(bottom, 0.0, pltpu.roll(c, 1, 1)) for c in centre]
        factor = factor * time_step
        slopes = (ahead[3] - behind[3], upper[3] - lower[3], above[3] - below[3])
        result = []
        for i in range(3):
            around = (ahead[i] + behind[i]) + (upper[i] + lower[i]) + (above[i] + below[i])
            result.append(
                centre[i]
                + factor * (around - 6.0 * centre[i])
                - wind_part * (ahead[i] - behind[i])
                - half * slopes[i]
            )
        result.append(
            centre[3]
            - half * ((ahead[0] - behind[0]) + (upper[1] - lower[1]) + (above[2] - below[2]))
        )
        return result

    return step


def inner_kernel(
    count_y, vel, pre, vis, wind, left, right,
    vel_out, old_edge, mid_edge, visc_edge, pre_core,
    old, mid, visc, vel_core, sem, out_sem,
):
    layers, rows, height = pre.shape
    last = PAD + rows
    iy = lax.axis_index("gy")
    has_left = iy > 0
    has_right = iy < count_y - 1
    core = pl.ds(PAD, rows)
    copies = [
        pltpu.make_async_copy(vel.at[i], old.at[i, :, core], sem.at[i]) for i in range(3)
    ]
    copies.append(pltpu.make_async_copy(pre, old.at[3, :, core], sem.at[3]))
    copies.append(pltpu.make_async_copy(vis, visc.at[:, core], sem.at[4]))
    for place, (source, row) in enumerate(((left, 0), (right, last))):
        copies.append(
            pltpu.make_async_copy(
                source.at[pl.ds(0, 4)], old.at[:, :, pl.ds(row, PAD)], sem.at[5 + 2 * place]
            )
        )
        copies.append(
            pltpu.make_async_copy(
                source.at[4], visc.at[:, pl.ds(row, PAD)], sem.at[6 + 2 * place]
            )
        )
    for copy in copies:
        copy.start()
    for copy in copies:
        copy.wait()
    blank = jnp.zeros((4, layers, PAD, height), f32)

    @pl.when(jnp.logical_not(has_left))
    def _():
        old[:, :, 0:PAD, :] = blank
        mid[:, :, 0:PAD, :] = blank

    @pl.when(jnp.logical_not(has_right))
    def _():
        old[:, :, last : last + PAD, :] = blank
        mid[:, :, last : last + PAD, :] = blank

    step = stepper(wind, height)

    def advance(source, layer, row, edge=0):
        def get(f, offset, low):
            return source[f, layer + offset, pl.ds(low, 8), :]

        return step(get, visc[layer, pl.ds(row, 8), :], row, edge)

    def first(layer, row, edge=0):
        result = advance(old, layer, row, edge)
        for f in range(4):
            mid[f, layer, pl.ds(row, 8), :] = result[f]

    @pl.loop(1, layers - 1)
    def _(layer):
        for row in range(PAD, last, 8):
            first(layer, row)

    @pl.when(has_left)
    def _():
        @pl.loop(1, layers - 1)
        def _(layer):
            first(layer, 0, -1)

    @pl.when(has_right)
    def _():
        @pl.loop(1, layers - 1)
        def _(layer):
            first(layer, last, 1)

    @pl.loop(2, layers - 2)
    def _(layer):
        for row in range(PAD, last, 8):
            result = advance(mid, layer, row)
            for i in range(3):
                vel_core[i, layer - 2, row - PAD : row - PAD + 8, :] = result[i]
            pre_core[layer - 2, row - PAD : row - PAD + 8, :] = result[3]

    result = pltpu.make_async_copy(
        vel_core, vel_out.at[:, pl.ds(2, layers - 4)], out_sem
    )
    result.start()
    for side, first_old, place_old, first_mid, place_mid in (
        (0, 0, 2, 1, 3),
        (1, layers - 2, 1, layers - 3, 0),
    ):
        for depth in range(2):
            visc_edge[side, place_old + depth] = visc[first_old + depth]
            for f in range(4):
                old_edge[side, f, place_old + depth] = old[f, first_old + depth]
                mid_edge[side, f, place_mid + depth] = mid[f, first_mid + depth]
    result.wait()


def edge_kernel(
    count_x, count_y, near_message, far_message, wind, cell, area, partial, pre_core,
    vel_in, old_in, mid_in, visc_in,
    vel_out, pre_out, payload, old, mid, visc,
    stage, pre_full, vel_edge, sem, out_sem,
):
    layers, rows, height = pre_full.shape
    last = PAD + rows
    ix = lax.axis_index("gx")
    iy = lax.axis_index("gy")
    has_left = iy > 0
    has_right = iy < count_y - 1
    has_before = ix > 0
    has_after = ix < count_x - 1
    odd = lax.rem(ix, 2)
    copies = [
        pltpu.make_async_copy(near_message, stage.at[1 - odd], sem.at[0]),
        pltpu.make_async_copy(far_message, stage.at[odd], sem.at[1]),
    ]
    for copy in copies:
        copy.start()
    pre_full[2 : layers - 2] = pre_core[...]
    slots = cell.shape[1]
    cells = layers * rows
    same = lax.broadcasted_iota(jnp.int32, (LANES, LANES), 0) == lax.broadcasted_iota(
        jnp.int32, (LANES, LANES), 1
    )
    place = cell[...]
    line = place // height
    level = place - line * height

    def stand(row):
        lines = [
            jnp.sum(jnp.where(same, row[:, k : k + LANES], 0.0), axis=1, keepdims=True)
            for k in range(0, slots, LANES)
        ]
        return jnp.concatenate(lines, axis=0)

    line, level = stand(line.astype(f32)), stand(level.astype(f32))
    own_area = stand(area[...])
    pick = lax.broadcasted_iota(jnp.int32, (slots, cells), 1).astype(f32) == line
    pick = pick.astype(f32).astype(bf16)
    at_level = lax.broadcasted_iota(jnp.int32, (slots, height), 1).astype(f32) == level
    for copy in copies:
        copy.wait()
    for side in range(2):
        near = 1 + 2 * side
        for field in range(4):
            for depth in range(2):
                start = (field * 2 + depth) * rows
                old[side, field, 3 * side + depth, PAD:last, :] = stage[
                    side, start : start + rows, :
                ].astype(f32)
        visc[side, near, PAD:last, :] = stage[side, 8 * rows : 9 * rows, :].astype(f32)
        corner = stage[side, 9 * rows : 9 * rows + 16, :].astype(f32)
        for field in range(4):
            old[side, field, near, PAD - 1 : PAD, :] = corner[field : field + 1]
            old[side, field, near, last : last + 1, :] = corner[4 + field : 5 + field]

    step = stepper(wind, height)

    def advance(source, side, layer, row, edge=0):
        def get(f, offset, low):
            return source[side, f, layer + offset, pl.ds(low, 8), :]

        return step(get, visc[side, layer, pl.ds(row, 8), :], row, edge)

    def first(side, layer, row, edge=0):
        result = advance(old, side, layer, row, edge)
        for f in range(4):
            mid[side, f, layer, pl.ds(row, 8), :] = result[f]

    blank = jnp.zeros((4, PAD, height), f32)

    @pl.loop(0, 2)
    def _(side):
        there = jnp.where(side == 0, has_before, has_after)
        outside = 1 + 2 * side
        for row in range(PAD, last, 8):
            first(side, 2, row)

        @pl.when(has_left)
        def _():
            first(side, 2, 0, -1)

        @pl.when(jnp.logical_not(has_left))
        def _():
            mid[side, :, 2, 0:PAD, :] = blank

        @pl.when(has_right)
        def _():
            first(side, 2, last, 1)

        @pl.when(jnp.logical_not(has_right))
        def _():
            mid[side, :, 2, last : last + PAD, :] = blank

        @pl.when(there)
        def _():
            for row in range(PAD, last, 8):
                first(side, outside, row)

        @pl.when(jnp.logical_not(there))
        def _():
            mid[side, :, outside, PAD:last, :] = jnp.zeros((4, rows, height), f32)

        for row in range(PAD, last, 8):
            for layer, place in ((2, side), (3 - 2 * side, 1 - side)):
                result = advance(mid, side, layer, row)
                here = pl.ds(row - PAD, 8)
                for i in range(3):
                    vel_edge[side, i, place, here, :] = result[i]
                pre_full[side * (layers - 2) + place, here, :] = result[3]

    results = [
        pltpu.make_async_copy(
            vel_edge.at[side], vel_out.at[:, pl.ds(side * (layers - 2), 2)], out_sem.at[side]
        )
        for side in range(2)
    ]
    results.append(pltpu.make_async_copy(pre_full, pre_out, out_sem.at[2]))
    for result in results:
        result.start()
    flat = pre_full[...].reshape(cells, height)
    found = jnp.zeros((slots, height), f32)
    for part in parts_of(flat):
        found = found + jnp.dot(pick, part.astype(bf16), preferred_element_type=f32)
    sampled = jnp.sum(jnp.where(at_level, found, 0.0), axis=1, keepdims=True)
    loads = (own_area * sampled).astype(bf16).astype(f32)
    lines = []
    for start in range(0, slots, LANES):
        chosen = jnp.where(same, loads[start : start + LANES], 0.0)
        lines.append(jnp.sum(chosen, axis=0, keepdims=True))
    message = jnp.concatenate(lines + [partial[...]], axis=0)
    payload[...] = jnp.broadcast_to(message[None], payload.shape)
    for result in results:
        result.wait()


def prepare_kernel(slot_count, damper_width, own_ids, areas, nodes, modal, *refs):
    smalls = refs[:-3]
    shapes, partial, area = refs[-3:]
    high_count = areas.shape[0]
    slots = own_ids.shape[1]
    ids = own_ids[...]
    high = jnp.where(ids < 0, -1, ids // LANES)
    low = ids - high * LANES
    high_pick = lax.broadcasted_iota(jnp.int32, (high_count, slots), 0) == high
    low_pick = lax.broadcasted_iota(jnp.int32, (LANES, slots), 0) == low
    high_pick = high_pick.astype(f32).astype(bf16)
    spread = jnp.zeros((LANES, slots), f32)
    for part in parts_of(areas[...]):
        spread = spread + lax.dot_general(
            part.astype(bf16),
            high_pick,
            (((0,), (0,)), ((), ())),
            preferred_element_type=f32,
        )
    area[...] = jnp.sum(jnp.where(low_pick, spread, 0.0), axis=0, keepdims=True)
    node_rank = lax.broadcasted_iota(jnp.int32, (nodes.shape[0], damper_width), 0).astype(f32)
    table = nodes[...]
    for q, small in enumerate(smalls):
        lower = small[:, slot_count + 3 * damper_width : slot_count + 4 * damper_width]
        for end in range(2):
            pick = (node_rank == lower + (1.0 - end)).astype(f32).astype(bf16)
            rows = lax.dot_general(
                pick, table, (((0,), (0,)), ((), ())), preferred_element_type=f32
            )
            shapes[q, end] = rows.astype(bf16)
    state = modal[...]
    partial[...] = drift_times(state[0:1], state[1:2], shapes)


def respond(stretch, rate, hysteresis, viscous, hysteretic):
    hysteresis = hysteresis + modal_step * (
        rate
        - shape_beta * jnp.abs(rate) * hysteresis
        - shape_gamma * rate * jnp.abs(hysteresis)
    )
    force = -(viscous * rate + spring_rate * stretch + hysteretic * hysteresis)
    return hysteresis, force


def pulled(forces, shapes):
    sides = []
    for force in forces:
        three = jnp.concatenate(parts_of(force) + [jnp.zeros((13, force.shape[1]), f32)], axis=0)
        sides += [three, -three]
    left = jnp.concatenate(sides, axis=1).astype(bf16)
    right = shapes[...].reshape(-1, shapes.shape[-1])
    return jnp.sum(jnp.dot(left, right, preferred_element_type=f32), axis=0, keepdims=True)


def drift_times(displacement, velocity, shapes):
    pair = lax.dot_general(
        stacked(parts_of(displacement) + parts_of(velocity)),
        shapes[0].reshape(-1, shapes.shape[-1]),
        (((1,), (1,)), ((), ())),
        preferred_element_type=f32,
    )
    width = pair.shape[1] // 2
    drift = pair[:, :width] - pair[:, width:]
    return jnp.concatenate(
        [
            jnp.sum(drift[0:3], axis=0, keepdims=True),
            jnp.sum(drift[3:6], axis=0, keepdims=True),
        ],
        axis=0,
    )


def advance_modes(load, frequency, ratio, displacement, velocity):
    acceleration = (
        load
        - 2.0 * ratio * frequency * velocity
        - frequency * frequency * displacement
    )
    velocity = velocity + modal_step * acceleration
    return displacement + modal_step * velocity, velocity


def damper_rows(small, slot_count, width):
    return [small[:, slot_count + k * width : slot_count + (k + 1) * width] for k in range(3)]


def first_kernel(count_x, count_y, load_rows, *refs):
    received, shapes, modal, frequency, ratio = refs[:5]
    smalls = refs[5 : 5 + count_y]
    tables = refs[5 + count_y : 5 + 2 * count_y]
    payload, state, hysteresis_out, held, sem = refs[5 + 2 * count_y :]
    iy = lax.axis_index("gy")
    copies = [
        pltpu.make_async_copy(tables[q], held.at[q], sem.at[q]) for q in range(count_y)
    ]
    for copy in copies:
        copy.start()
    panel_count = tables[0].shape[0]
    high_count = panel_count // LANES
    slot_count = count_x * load_rows * LANES
    width = payload.shape[-1]
    rank = lax.broadcasted_iota(jnp.int32, (high_count, LANES), 0).astype(f32)
    low_rank = lax.broadcasted_iota(jnp.int32, (LANES, slot_count), 0).astype(f32)
    sides = []
    forces = []
    for q in range(count_y):
        piece = lax.rem(iy + q, count_y)
        ids = smalls[q][:, :slot_count]
        high = jnp.floor(ids * (1.0 / LANES))
        low = ids - high * LANES
        chunks = []
        for i in range(count_x):
            for r in range(load_rows):
                start = (i * load_rows + r) * LANES
                line = received[i, piece, r : r + 1, :]
                chunks.append(
                    jnp.where(rank == high[:, start : start + LANES], line, 0.0).astype(bf16)
                )
        spread = (low_rank == low).astype(f32).astype(bf16)
        sorted_loads = lax.dot_general(
            jnp.concatenate(chunks, axis=1),
            spread,
            (((1,), (1,)), ((), ())),
            preferred_element_type=f32,
        )
        sides.append(
            jnp.concatenate(
                [jnp.where(rank == c, sorted_loads, 0.0).astype(bf16) for c in range(high_count)],
                axis=1,
            )
        )
        stretch = received[0, piece, load_rows : load_rows + 1, :]
        rate = received[0, piece, load_rows + 1 : load_rows + 2, :]
        for i in range(1, count_x):
            stretch = stretch + received[i, piece, load_rows : load_rows + 1, :]
            rate = rate + received[i, piece, load_rows + 1 : load_rows + 2, :]
        viscous, hysteretic, held_state = damper_rows(smalls[q], slot_count, width)
        hysteresis, force = respond(stretch, rate, held_state, viscous, hysteretic)
        hysteresis_out[q] = hysteresis
        forces.append(force)
    load = pulled(forces, shapes)
    for copy in copies:
        copy.wait()
    rows = jnp.zeros((high_count, modal.shape[1]), f32)
    for q in range(count_y):
        rows = rows + jnp.dot(sides[q], held[q], preferred_element_type=f32)
    panel_modal = jnp.sum(rows, axis=0, keepdims=True)
    displacement, velocity = advance_modes(
        panel_modal + load, frequency[...], ratio[...], modal[0:1, :], modal[1:2, :]
    )
    state[0:1, :] = displacement
    state[1:2, :] = velocity
    state[2:3, :] = panel_modal
    state[3:4, :] = panel_modal
    message = drift_times(displacement, velocity, shapes)
    payload[...] = jnp.broadcast_to(message[None], payload.shape)


def second_kernel(count_x, count_y, slot_count, *refs):
    received, shapes, frequency, ratio, state, held = refs[:6]
    smalls = refs[6 : 6 + count_y]
    modal, damper = refs[6 + count_y :]
    iy = lax.axis_index("gy")
    forces = []
    for q in range(count_y):
        piece = lax.rem(iy + q, count_y)
        stretch = received[0, piece, 0:1, :]
        rate = received[0, piece, 1:2, :]
        for i in range(1, count_x):
            stretch = stretch + received[i, piece, 0:1, :]
            rate = rate + received[i, piece, 1:2, :]
        viscous, hysteretic, _ = damper_rows(smalls[q], slot_count, stretch.shape[1])
        hysteresis, force = respond(stretch, rate, held[q], viscous, hysteretic)
        if q == 0:
            damper[...] = hysteresis[:, : damper.shape[1]]
        forces.append(force)
    load = state[2:3, :] + pulled(forces, shapes)
    displacement, velocity = advance_modes(
        load, frequency[...], ratio[...], state[0:1, :], state[1:2, :]
    )
    modal[0:1, :] = displacement
    modal[1:2, :] = velocity


def whole(space=pltpu.VMEM):
    return pl.BlockSpec(memory_space=space)


def body(
    velocity,
    pressure,
    viscosity,
    wind_profile,
    panel_area,
    slot_cell,
    slot_panel,
    panel_shapes,
    node_shapes,
    damper_node,
    damper_viscous,
    damper_hysteretic,
    frequency,
    damping_ratio,
    modal_state,
    damper_state,
):
    count_x = lax.axis_size("gx")
    count_y = lax.axis_size("gy")
    total = count_x * count_y
    both = ("gx", "gy")
    ix = lax.axis_index("gx")
    layers, rows, height = pressure.shape
    slots = slot_cell.shape[1]
    slots_padded = -(-slots // LANES) * LANES
    load_rows = slots_padded // LANES
    slot_count = count_x * slots_padded
    damper_count = damper_node.shape[0]
    damper_padded = -(-damper_count // LANES) * LANES
    mode_count = frequency.shape[0]
    params = pltpu.CompilerParams(vmem_limit_bytes=VMEM_BYTES)
    shape = jax.ShapeDtypeStruct

    raw = [
        pltpu.with_memory_space_constraint(value, pltpu.HBM)
        for value in (velocity, pressure, viscosity)
    ]
    starts = (None,) if count_y == 2 else (rows - PAD, 0)
    sides = pl.pallas_call(
        functools.partial(side_kernel, starts),
        out_shape=tuple(shape((5, layers, PAD, height), f32) for _ in starts),
        in_specs=[whole(pl.ANY)] * 3,
        out_specs=tuple(whole(pl.ANY) for _ in starts),
        scratch_shapes=[pltpu.SemaphoreType.DMA((len(starts), 3))],
        compiler_params=params,
        name="side",
    )(*raw)
    if count_y == 2:
        left = right = lax.ppermute(sides[0], "gy", [(0, 1), (1, 0)])
    else:
        left = lax.ppermute(sides[0], "gy", shifts(count_y, 1, False))
        right = lax.ppermute(sides[1], "gy", shifts(count_y, -1, False))

    message_shape = (9 * rows + 16, height)
    near_message, far_message = pl.pallas_call(
        pack_kernel,
        out_shape=(shape(message_shape, bf16), shape(message_shape, bf16)),
        in_specs=[whole(pl.ANY)] * 3,
        out_specs=(whole(), whole()),
        scratch_shapes=[
            pltpu.VMEM((2, 5, 2, rows, height), f32),
            pltpu.SemaphoreType.DMA((2, 3)),
        ],
        compiler_params=params,
        name="pack",
    )(*raw)
    near_message, far_message = pl.pallas_call(
        functools.partial(corner_kernel, count_y),
        out_shape=(shape(message_shape, bf16), shape(message_shape, bf16)),
        in_specs=[whole()] * 4,
        out_specs=(whole(), whole()),
        input_output_aliases={2: 0, 3: 1},
        compiler_params=params,
        name="corner",
    )(left, right, near_message, far_message)
    tied = lax.optimization_barrier(
        (
            near_message, far_message, left, right, panel_shapes, node_shapes, panel_area, slot_panel,
            damper_node, damper_viscous, damper_hysteretic, damper_state, modal_state,
        )
    )
    (
        near_message, far_message, left, right, panel_shapes, node_shapes, panel_area, slot_panel,
        damper_node, damper_viscous, damper_hysteretic, damper_state, modal_state,
    ) = tied
    near_message = lax.ppermute(near_message, "gx", pairs(count_x, 0))
    far_message = lax.ppermute(far_message, "gx", pairs(count_x, 1))

    def around(value):
        return [value] + [
            lax.ppermute(value, "gy", shifts(count_y, q, True)) for q in range(1, count_y)
        ]

    def damper_row(value, filler=0.0):
        extra = damper_padded - damper_count
        return jnp.pad(value, (0, extra), constant_values=filler)[None]

    tables = around(panel_shapes)
    ids = slot_panel
    if slots != slots_padded:
        ids = jnp.pad(
            ids.reshape(count_x, slots),
            ((0, 0), (0, slots_padded - slots)),
            constant_values=-1,
        ).reshape(1, slot_count)
    own_ids = lax.dynamic_slice_in_dim(ids, ix * slots_padded, slots_padded, axis=1)
    small = jnp.concatenate(
        [
            ids.astype(f32),
            damper_row(damper_viscous),
            damper_row(damper_hysteretic),
            damper_row(damper_state),
            damper_row(damper_node.astype(f32), -4.0),
        ],
        axis=1,
    )
    smalls = around(small)
    cell = jnp.pad(slot_cell, ((0, 0), (0, slots_padded - slots)))

    shapes, partial, area = pl.pallas_call(
        functools.partial(prepare_kernel, slot_count, damper_padded),
        out_shape=(
            shape((count_y, 2, damper_padded, mode_count), bf16),
            shape((2, damper_padded), f32),
            shape((1, slots_padded), f32),
        ),
        in_specs=[whole()] * (4 + count_y),
        out_specs=(whole(), whole(), whole()),
        compiler_params=params,
        name="prepare",
    )(own_ids, panel_area.reshape(-1, LANES), node_shapes, modal_state, *smalls)

    tall = rows + 2 * PAD
    wind = wind_profile[None, :]
    velocity_next, old, mid, visc, pre_core = pl.pallas_call(
        functools.partial(inner_kernel, count_y),
        out_shape=(
            shape(velocity.shape, f32),
            shape((2, 4, 5, tall, height), f32),
            shape((2, 4, 5, tall, height), f32),
            shape((2, 5, tall, height), f32),
            shape((layers - 4, rows, height), f32),
        ),
        in_specs=[whole(pl.ANY)] * 3 + [whole()] + [whole(pl.ANY)] * 2,
        out_specs=(whole(pl.ANY), whole(), whole(), whole(), whole()),
        scratch_shapes=[
            pltpu.VMEM((4, layers, tall, height), f32),
            pltpu.VMEM((4, layers, tall, height), f32),
            pltpu.VMEM((layers, tall, height), f32),
            pltpu.VMEM((3, layers - 4, rows, height), f32),
            pltpu.SemaphoreType.DMA((9,)),
            pltpu.SemaphoreType.DMA,
        ],
        compiler_params=params,
        name="inner",
    )(*raw, wind, left, right)

    velocity_next, pressure_next, payload, *_ = pl.pallas_call(
        functools.partial(edge_kernel, count_x, count_y),
        out_shape=(
            shape(velocity.shape, f32),
            shape(pressure.shape, f32),
            shape((total, load_rows + 2, LANES), f32),
            shape(old.shape, f32),
            shape(mid.shape, f32),
            shape(visc.shape, f32),
        ),
        in_specs=[whole(pl.ANY)] * 2
        + [whole()] * 5
        + [whole(pl.ANY)]
        + [whole()] * 3,
        out_specs=(whole(pl.ANY), whole(pl.ANY), whole(), whole(), whole(), whole()),
        input_output_aliases={7: 0, 8: 3, 9: 4, 10: 5},
        scratch_shapes=[
            pltpu.VMEM((2,) + message_shape, bf16),
            pltpu.VMEM((layers, rows, height), f32),
            pltpu.VMEM((2, 3, 2, rows, height), f32),
            pltpu.SemaphoreType.DMA((2,)),
            pltpu.SemaphoreType.DMA((3,)),
        ],
        compiler_params=params,
        name="edge",
    )(near_message, far_message, wind, cell, area, partial, pre_core, velocity_next, old, mid, visc)
    received = lax.all_to_all(payload, both, 0, 0, tiled=True)
    received = received.reshape(count_x, count_y, load_rows + 2, LANES)

    frequency = frequency[None]
    damping_ratio = damping_ratio[None]
    payload, state, hysteresis = pl.pallas_call(
        functools.partial(first_kernel, count_x, count_y, load_rows),
        out_shape=(
            shape((total, 2, damper_padded), f32),
            shape((4, mode_count), f32),
            shape((count_y, 1, damper_padded), f32),
        ),
        in_specs=[whole()] * (5 + count_y) + [whole(pl.ANY)] * count_y,
        out_specs=(whole(), whole(), whole()),
        scratch_shapes=[
            pltpu.VMEM((count_y,) + panel_shapes.shape, bf16),
            pltpu.SemaphoreType.DMA((count_y,)),
        ],
        compiler_params=params,
        name="first",
    )(received, shapes, modal_state, frequency, damping_ratio, *smalls, *tables)
    received = lax.all_to_all(payload, both, 0, 0, tiled=True)
    received = received.reshape(count_x, count_y, 2, damper_padded)

    modal_next, damper_next = pl.pallas_call(
        functools.partial(second_kernel, count_x, count_y, slot_count),
        out_shape=(
            shape((2, mode_count), f32),
            shape((1, damper_count), f32),
        ),
        in_specs=[whole()] * (6 + count_y),
        out_specs=(whole(), whole()),
        compiler_params=params,
        name="second",
    )(received, shapes, frequency, damping_ratio, state, hysteresis, *smalls)
    return (velocity_next, pressure_next, modal_next, damper_next.reshape(damper_count))


def solution(mesh):
    placed = (
        P(None, "gx", "gy", None),
        P("gx", "gy", None),
        P("gx", "gy", None),
        P(),
        P("gy"),
        P("gy", "gx"),
        P("gy", None),
        P("gy", "gx"),
        P(None, "gx"),
        P("gy"),
        P("gy"),
        P("gy"),
        P("gx"),
        P("gx"),
        P(None, "gx"),
        P("gy"),
    )
    return jax.shard_map(
        body,
        mesh=mesh,
        in_specs=placed,
        out_specs=(P(None, "gx", "gy", None), P("gx", "gy", None), P(None, "gx"), P("gy")),
        check_vma=False,
    )
```

```python
import functools

import jax
import jax.numpy as jnp
from jax import lax
from jax.experimental import pallas as pl
from jax.experimental.pallas import tpu as pltpu
from jax.sharding import PartitionSpec as P

f32 = jnp.float32
bf16 = jnp.bfloat16
time_step = 0.1
modal_step = 0.5
shape_beta = 0.5
shape_gamma = 0.5
spring_rate = 0.5
LANES = 128
PAD = 8
VMEM_BYTES = 40 * 1024 * 1024


def shifts(size, step, cyclic):
    if cyclic:
        return [((i + step) % size, i) for i in range(size)]
    return [(i, i + step) for i in range(size) if 0 <= i + step < size]


def pairs(size, first):
    lower = range(first, size - 1, 2)
    return [(i, i + 1) for i in lower] + [(i + 1, i) for i in lower]


def parts_of(row):
    high = row.astype(bf16).astype(f32)
    rest = row - high
    middle = rest.astype(bf16).astype(f32)
    return [high, middle, rest - middle]


def stacked(rows):
    filler = jnp.zeros((16 - len(rows), rows[0].shape[1]), f32)
    return jnp.concatenate(rows + [filler], axis=0).astype(bf16)


def side_kernel(starts, vel, pre, vis, *refs):
    outs, sem = refs[:-1], refs[-1]
    copies = []
    for place, (start, out) in enumerate(zip(starts, outs)):
        if start is None:
            start = jnp.where(lax.axis_index("gy") == 0, pre.shape[1] - PAD, 0)
        here = pl.ds(pl.multiple_of(start, PAD), PAD)
        copies += [
            pltpu.make_async_copy(vel.at[:, :, here], out.at[pl.ds(0, 3)], sem.at[place, 0]),
            pltpu.make_async_copy(pre.at[:, here], out.at[3], sem.at[place, 1]),
            pltpu.make_async_copy(vis.at[:, here], out.at[4], sem.at[place, 2]),
        ]
    for copy in copies:
        copy.start()
    for copy in copies:
        copy.wait()


def pack_kernel(vel, pre, vis, near_out, far_out, stage, sem):
    layers, rows, height = pre.shape
    odd = lax.rem(lax.axis_index("gx"), 2)
    messages = ((near_out, 1 - odd), (far_out, odd))
    copies = []
    for place, (out, upward) in enumerate(messages):
        first = upward * (layers - 2)
        near = upward * (layers - 1)
        copies += [
            pltpu.make_async_copy(
                vel.at[:, pl.ds(first, 2)], stage.at[place, pl.ds(0, 3)], sem.at[place, 0]
            ),
            pltpu.make_async_copy(pre.at[pl.ds(first, 2)], stage.at[place, 3], sem.at[place, 1]),
            pltpu.make_async_copy(vis.at[near], stage.at[place, 4, 0], sem.at[place, 2]),
        ]
    for copy in copies:
        copy.start()
    for copy in copies:
        copy.wait()
    for place, (out, _) in enumerate(messages):
        for field in range(4):
            for depth in range(2):
                start = (field * 2 + depth) * rows
                out[start : start + rows, :] = stage[place, field, depth].astype(bf16)
        out[8 * rows : 9 * rows, :] = stage[place, 4, 0].astype(bf16)


def corner_kernel(count_y, left, right, near_in, far_in, near_out, far_out):
    layers, height = left.shape[1], left.shape[3]
    start = near_out.shape[0] - 16
    odd = lax.rem(lax.axis_index("gx"), 2)
    iy = lax.axis_index("gy")
    for out, upward in ((near_out, 1 - odd), (far_out, odd)):
        near = upward * (layers - 1)
        lines = [left[f, near, PAD - 1 : PAD, :] for f in range(4)]
        lines = [jnp.where(iy > 0, line, 0.0) for line in lines]
        others = [right[f, near, 0:1, :] for f in range(4)]
        lines += [jnp.where(iy < count_y - 1, line, 0.0) for line in others]
        lines.append(jnp.zeros((8, height), f32))
        out[start : start + 16, :] = jnp.concatenate(lines, axis=0).astype(bf16)


def stepper(wind, height):
    lane = lax.broadcasted_iota(jnp.int32, (8, height), 1)
    top = lane == height - 1
    bottom = lane == 0
    half = 0.5 * time_step
    wind_part = jnp.broadcast_to(wind[...] * half, (8, height))

    def step(get, factor, row, edge):
        def at(offset, low):
            return [get(f, offset, low) for f in range(4)]

        centre, ahead, behind = at(0, row), at(1, row), at(-1, row)
        lower = [pltpu.roll(c, 1, 0) for c in centre] if edge < 0 else at(0, row - 1)
        upper = [pltpu.roll(c, 7, 0) for c in centre] if edge > 0 else at(0, row + 1)
        above = [jnp.where(top, 0.0, pltpu.roll(c, height - 1, 1)) for c in centre]
        below = [jnp.where(bottom, 0.0, pltpu.roll(c, 1, 1)) for c in centre]
        factor = factor * time_step
        slopes = (ahead[3] - behind[3], upper[3] - lower[3], above[3] - below[3])
        result = []
        for i in range(3):
            around = (ahead[i] + behind[i]) + (upper[i] + lower[i]) + (above[i] + below[i])
            result.append(
                centre[i]
                + factor * (around - 6.0 * centre[i])
                - wind_part * (ahead[i] - behind[i])
                - half * slopes[i]
            )
        result.append(
            centre[3]
            - half * ((ahead[0] - behind[0]) + (upper[1] - lower[1]) + (above[2] - below[2]))
        )
        return result

    return step


def inner_kernel(
    count_y, vel, pre, vis, wind, left, right,
    vel_out, old_edge, mid_edge, visc_edge, pre_core,
    old, mid, visc, vel_core, sem, out_sem,
):
    layers, rows, height = pre.shape
    last = PAD + rows
    iy = lax.axis_index("gy")
    has_left = iy > 0
    has_right = iy < count_y - 1
    core = pl.ds(PAD, rows)
    copies = [
        pltpu.make_async_copy(vel.at[i], old.at[i, :, core], sem.at[i]) for i in range(3)
    ]
    copies.append(pltpu.make_async_copy(pre, old.at[3, :, core], sem.at[3]))
    copies.append(pltpu.make_async_copy(vis, visc.at[:, core], sem.at[4]))
    for place, (source, row) in enumerate(((left, 0), (right, last))):
        copies.append(
            pltpu.make_async_copy(
                source.at[pl.ds(0, 4)], old.at[:, :, pl.ds(row, PAD)], sem.at[5 + 2 * place]
            )
        )
        copies.append(
            pltpu.make_async_copy(
                source.at[4], visc.at[:, pl.ds(row, PAD)], sem.at[6 + 2 * place]
            )
        )
    for copy in copies:
        copy.start()
    for copy in copies:
        copy.wait()
    blank = jnp.zeros((4, layers, PAD, height), f32)

    @pl.when(jnp.logical_not(has_left))
    def _():
        old[:, :, 0:PAD, :] = blank
        mid[:, :, 0:PAD, :] = blank

    @pl.when(jnp.logical_not(has_right))
    def _():
        old[:, :, last : last + PAD, :] = blank
        mid[:, :, last : last + PAD, :] = blank

    step = stepper(wind, height)

    def advance(source, layer, row, edge=0):
        def get(f, offset, low):
            return source[f, layer + offset, pl.ds(low, 8), :]

        return step(get, visc[layer, pl.ds(row, 8), :], row, edge)

    def first(layer, row, edge=0):
        result = advance(old, layer, row, edge)
        for f in range(4):
            mid[f, layer, pl.ds(row, 8), :] = result[f]

    @pl.loop(1, layers - 1)
    def _(layer):
        for row in range(PAD, last, 8):
            first(layer, row)

    @pl.when(has_left)
    def _():
        @pl.loop(1, layers - 1)
        def _(layer):
            first(layer, 0, -1)

    @pl.when(has_right)
    def _():
        @pl.loop(1, layers - 1)
        def _(layer):
            first(layer, last, 1)

    @pl.loop(2, layers - 2)
    def _(layer):
        for row in range(PAD, last, 8):
            result = advance(mid, layer, row)
            for i in range(3):
                vel_core[i, layer - 2, row - PAD : row - PAD + 8, :] = result[i]
            pre_core[layer - 2, row - PAD : row - PAD + 8, :] = result[3]

    result = pltpu.make_async_copy(
        vel_core, vel_out.at[:, pl.ds(2, layers - 4)], out_sem
    )
    result.start()
    for side, first_old, place_old, first_mid, place_mid in (
        (0, 0, 2, 1, 3),
        (1, layers - 2, 1, layers - 3, 0),
    ):
        for depth in range(2):
            visc_edge[side, place_old + depth] = visc[first_old + depth]
            for f in range(4):
                old_edge[side, f, place_old + depth] = old[f, first_old + depth]
                mid_edge[side, f, place_mid + depth] = mid[f, first_mid + depth]
    result.wait()


def edge_kernel(
    count_x, count_y, near_message, far_message, wind, pick, weight, partial, pre_core,
    vel_in, old_in, mid_in, visc_in,
    vel_out, pre_out, payload, old, mid, visc,
    pre_full, vel_edge, out_sem,
):
    layers, rows, height = pre_full.shape
    last = PAD + rows
    ix = lax.axis_index("gx")
    iy = lax.axis_index("gy")
    has_left = iy > 0
    has_right = iy < count_y - 1
    has_before = ix > 0
    has_after = ix < count_x - 1
    odd = lax.rem(ix, 2)
    pre_full[2 : layers - 2] = pre_core[...]
    for message, side in ((near_message, 1 - odd), (far_message, odd)):
        near = 1 + 2 * side
        for field in range(4):
            for depth in range(2):
                start = (field * 2 + depth) * rows
                old[side, field, 3 * side + depth, PAD:last, :] = message[
                    start : start + rows, :
                ].astype(f32)
        visc[side, near, PAD:last, :] = message[8 * rows : 9 * rows, :].astype(f32)
        corner = message[9 * rows : 9 * rows + 16, :].astype(f32)
        for field in range(4):
            old[side, field, near, PAD - 1 : PAD, :] = corner[field : field + 1]
            old[side, field, near, last : last + 1, :] = corner[4 + field : 5 + field]

    step = stepper(wind, height)

    def advance(source, side, layer, row, edge=0):
        def get(f, offset, low):
            return source[side, f, layer + offset, pl.ds(low, 8), :]

        return step(get, visc[side, layer, pl.ds(row, 8), :], row, edge)

    def first(side, layer, row, edge=0):
        result = advance(old, side, layer, row, edge)
        for f in range(4):
            mid[side, f, layer, pl.ds(row, 8), :] = result[f]

    blank = jnp.zeros((4, PAD, height), f32)

    def vel_copy(side):
        return pltpu.make_async_copy(
            vel_edge.at[side], vel_out.at[:, pl.ds(side * (layers - 2), 2)], out_sem.at[side]
        )

    @pl.loop(0, 2)
    def _(side):
        there = jnp.where(side == 0, has_before, has_after)
        outside = 1 + 2 * side
        for row in range(PAD, last, 8):
            first(side, 2, row)

        @pl.when(has_left)
        def _():
            first(side, 2, 0, -1)

        @pl.when(jnp.logical_not(has_left))
        def _():
            mid[side, :, 2, 0:PAD, :] = blank

        @pl.when(has_right)
        def _():
            first(side, 2, last, 1)

        @pl.when(jnp.logical_not(has_right))
        def _():
            mid[side, :, 2, last : last + PAD, :] = blank

        @pl.when(there)
        def _():
            for row in range(PAD, last, 8):
                first(side, outside, row)

        @pl.when(jnp.logical_not(there))
        def _():
            mid[side, :, outside, PAD:last, :] = jnp.zeros((4, rows, height), f32)

        for row in range(PAD, last, 8):
            for layer, place in ((2, side), (3 - 2 * side, 1 - side)):
                result = advance(mid, side, layer, row)
                here = pl.ds(row - PAD, 8)
                for i in range(3):
                    vel_edge[side, i, place, here, :] = result[i]
                pre_full[side * (layers - 2) + place, here, :] = result[3]
        vel_copy(side).start()

    pre_copy = pltpu.make_async_copy(pre_full, pre_out, out_sem.at[2])
    pre_copy.start()
    flat = pre_full[...].reshape(layers * rows, height)
    found = jnp.zeros(weight.shape, f32)
    for part in parts_of(flat):
        found = found + jnp.dot(pick[...], part.astype(bf16), preferred_element_type=f32)
    loads = jnp.sum(weight[...] * found, axis=1, keepdims=True).astype(bf16).astype(f32)
    slots = weight.shape[0]
    same = lax.broadcasted_iota(jnp.int32, (LANES, LANES), 0) == lax.broadcasted_iota(
        jnp.int32, (LANES, LANES), 1
    )
    lines = []
    for start in range(0, slots, LANES):
        chosen = jnp.where(same, loads[start : start + LANES], 0.0)
        lines.append(jnp.sum(chosen, axis=0, keepdims=True))
    message = jnp.concatenate(lines + [partial[...]], axis=0)
    payload[...] = jnp.broadcast_to(message[None], payload.shape)
    pre_copy.wait()
    for side in range(2):
        vel_copy(side).wait()


def prepare_kernel(slot_count, damper_width, own_ids, cell, areas, nodes, modal, *refs):
    count_y = (len(refs) - 4) // 2
    smalls = refs[:count_y]
    shapes, partial, pick, weight = refs[count_y : count_y + 4]
    spreads = refs[count_y + 4 :]
    high_count = areas.shape[0]
    slots = own_ids.shape[1]
    cells, height = pick.shape[1], weight.shape[1]
    ids = own_ids[...]
    high = jnp.where(ids < 0, -1, ids // LANES)
    low = ids - high * LANES
    high_pick = lax.broadcasted_iota(jnp.int32, (high_count, slots), 0) == high
    low_pick = lax.broadcasted_iota(jnp.int32, (LANES, slots), 0) == low
    high_pick = high_pick.astype(f32).astype(bf16)
    spread = jnp.zeros((LANES, slots), f32)
    for part in parts_of(areas[...]):
        spread = spread + lax.dot_general(
            part.astype(bf16),
            high_pick,
            (((0,), (0,)), ((), ())),
            preferred_element_type=f32,
        )
    area = jnp.sum(jnp.where(low_pick, spread, 0.0), axis=0, keepdims=True)
    same = lax.broadcasted_iota(jnp.int32, (LANES, LANES), 0) == lax.broadcasted_iota(
        jnp.int32, (LANES, LANES), 1
    )

    def stand(row):
        lines = [
            jnp.sum(jnp.where(same, row[:, k : k + LANES], 0.0), axis=1, keepdims=True)
            for k in range(0, slots, LANES)
        ]
        return jnp.concatenate(lines, axis=0)

    place = cell[...]
    line = place // height
    level = place - line * height
    line, level = stand(line.astype(f32)), stand(level.astype(f32))
    rank = lax.broadcasted_iota(jnp.int32, (slots, cells), 1).astype(f32)
    pick[...] = (rank == line).astype(f32).astype(bf16)
    rank = lax.broadcasted_iota(jnp.int32, (slots, height), 1).astype(f32)
    weight[...] = jnp.where(rank == level, stand(area), 0.0)
    low_rank = lax.broadcasted_iota(jnp.int32, (LANES, slot_count), 0).astype(f32)
    node_rank = lax.broadcasted_iota(jnp.int32, (nodes.shape[0], damper_width), 0).astype(f32)
    table = nodes[...]
    for q, small in enumerate(smalls):
        numbers = small[:, :slot_count]
        numbers = numbers - jnp.floor(numbers * (1.0 / LANES)) * LANES
        spreads[q][...] = (low_rank == numbers).astype(f32).astype(bf16)
        lower = small[:, slot_count + 3 * damper_width : slot_count + 4 * damper_width]
        for end in range(2):
            picked = (node_rank == lower + (1.0 - end)).astype(f32).astype(bf16)
            rows = lax.dot_general(
                picked, table, (((0,), (0,)), ((), ())), preferred_element_type=f32
            )
            shapes[q, end] = rows.astype(bf16)
    state = modal[...]
    partial[...] = drift_times(state[0:1], state[1:2], shapes)


def respond(stretch, rate, hysteresis, viscous, hysteretic):
    hysteresis = hysteresis + modal_step * (
        rate
        - shape_beta * jnp.abs(rate) * hysteresis
        - shape_gamma * rate * jnp.abs(hysteresis)
    )
    force = -(viscous * rate + spring_rate * stretch + hysteretic * hysteresis)
    return hysteresis, force


def pulled(forces, shapes):
    sides = []
    for force in forces:
        three = jnp.concatenate(parts_of(force) + [jnp.zeros((13, force.shape[1]), f32)], axis=0)
        sides += [three, -three]
    left = jnp.concatenate(sides, axis=1).astype(bf16)
    right = shapes[...].reshape(-1, shapes.shape[-1])
    return jnp.sum(jnp.dot(left, right, preferred_element_type=f32), axis=0, keepdims=True)


def drift_times(displacement, velocity, shapes):
    pair = lax.dot_general(
        stacked(parts_of(displacement) + parts_of(velocity)),
        shapes[0].reshape(-1, shapes.shape[-1]),
        (((1,), (1,)), ((), ())),
        preferred_element_type=f32,
    )
    width = pair.shape[1] // 2
    drift = pair[:, :width] - pair[:, width:]
    return jnp.concatenate(
        [
            jnp.sum(drift[0:3], axis=0, keepdims=True),
            jnp.sum(drift[3:6], axis=0, keepdims=True),
        ],
        axis=0,
    )


def advance_modes(load, frequency, ratio, displacement, velocity):
    acceleration = (
        load
        - 2.0 * ratio * frequency * velocity
        - frequency * frequency * displacement
    )
    velocity = velocity + modal_step * acceleration
    return displacement + modal_step * velocity, velocity


def damper_rows(small, slot_count, width):
    return [small[:, slot_count + k * width : slot_count + (k + 1) * width] for k in range(3)]


def first_kernel(count_x, count_y, load_rows, *refs):
    received, shapes, modal, frequency, ratio = refs[:5]
    smalls = refs[5 : 5 + count_y]
    tables = refs[5 + count_y : 5 + 2 * count_y]
    spreads = refs[5 + 2 * count_y : 5 + 3 * count_y]
    payload, state, hysteresis_out = refs[5 + 3 * count_y :]
    iy = lax.axis_index("gy")
    panel_count = tables[0].shape[0]
    high_count = panel_count // LANES
    slot_count = count_x * load_rows * LANES
    width = payload.shape[-1]
    rank = lax.broadcasted_iota(jnp.int32, (high_count, LANES), 0).astype(f32)
    sides = []
    forces = []
    for q in range(count_y):
        piece = lax.rem(iy + q, count_y)
        ids = smalls[q][:, :slot_count]
        high = jnp.floor(ids * (1.0 / LANES))
        chunks = []
        for i in range(count_x):
            for r in range(load_rows):
                start = (i * load_rows + r) * LANES
                line = received[i, piece, r : r + 1, :]
                chunks.append(
                    jnp.where(rank == high[:, start : start + LANES], line, 0.0).astype(bf16)
                )
        sorted_loads = lax.dot_general(
            jnp.concatenate(chunks, axis=1),
            spreads[q][...],
            (((1,), (1,)), ((), ())),
            preferred_element_type=f32,
        )
        sides.append(
            jnp.concatenate(
                [jnp.where(rank == c, sorted_loads, 0.0).astype(bf16) for c in range(high_count)],
                axis=1,
            )
        )
        stretch = received[0, piece, load_rows : load_rows + 1, :]
        rate = received[0, piece, load_rows + 1 : load_rows + 2, :]
        for i in range(1, count_x):
            stretch = stretch + received[i, piece, load_rows : load_rows + 1, :]
            rate = rate + received[i, piece, load_rows + 1 : load_rows + 2, :]
        viscous, hysteretic, held_state = damper_rows(smalls[q], slot_count, width)
        hysteresis, force = respond(stretch, rate, held_state, viscous, hysteretic)
        hysteresis_out[q] = hysteresis
        forces.append(force)
    load = pulled(forces, shapes)
    rows = jnp.zeros((high_count, modal.shape[1]), f32)
    for q in range(count_y):
        rows = rows + jnp.dot(sides[q], tables[q][...], preferred_element_type=f32)
    panel_modal = jnp.sum(rows, axis=0, keepdims=True)
    displacement, velocity = advance_modes(
        panel_modal + load, frequency[...], ratio[...], modal[0:1, :], modal[1:2, :]
    )
    state[0:1, :] = displacement
    state[1:2, :] = velocity
    state[2:3, :] = panel_modal
    state[3:4, :] = panel_modal
    message = drift_times(displacement, velocity, shapes)
    payload[...] = jnp.broadcast_to(message[None], payload.shape)


def second_kernel(count_x, count_y, slot_count, *refs):
    received, shapes, frequency, ratio, state, held = refs[:6]
    smalls = refs[6 : 6 + count_y]
    modal, damper = refs[6 + count_y :]
    iy = lax.axis_index("gy")
    forces = []
    for q in range(count_y):
        piece = lax.rem(iy + q, count_y)
        stretch = received[0, piece, 0:1, :]
        rate = received[0, piece, 1:2, :]
        for i in range(1, count_x):
            stretch = stretch + received[i, piece, 0:1, :]
            rate = rate + received[i, piece, 1:2, :]
        viscous, hysteretic, _ = damper_rows(smalls[q], slot_count, stretch.shape[1])
        hysteresis, force = respond(stretch, rate, held[q], viscous, hysteretic)
        if q == 0:
            damper[...] = hysteresis[:, : damper.shape[1]]
        forces.append(force)
    load = state[2:3, :] + pulled(forces, shapes)
    displacement, velocity = advance_modes(
        load, frequency[...], ratio[...], state[0:1, :], state[1:2, :]
    )
    modal[0:1, :] = displacement
    modal[1:2, :] = velocity


def whole(space=pltpu.VMEM):
    return pl.BlockSpec(memory_space=space)


def body(
    velocity,
    pressure,
    viscosity,
    wind_profile,
    panel_area,
    slot_cell,
    slot_panel,
    panel_shapes,
    node_shapes,
    damper_node,
    damper_viscous,
    damper_hysteretic,
    frequency,
    damping_ratio,
    modal_state,
    damper_state,
):
    count_x = lax.axis_size("gx")
    count_y = lax.axis_size("gy")
    total = count_x * count_y
    both = ("gx", "gy")
    ix = lax.axis_index("gx")
    layers, rows, height = pressure.shape
    slots = slot_cell.shape[1]
    slots_padded = -(-slots // LANES) * LANES
    load_rows = slots_padded // LANES
    slot_count = count_x * slots_padded
    damper_count = damper_node.shape[0]
    damper_padded = -(-damper_count // LANES) * LANES
    mode_count = frequency.shape[0]
    params = pltpu.CompilerParams(vmem_limit_bytes=VMEM_BYTES)
    shape = jax.ShapeDtypeStruct

    raw = [
        pltpu.with_memory_space_constraint(value, pltpu.HBM)
        for value in (velocity, pressure, viscosity)
    ]
    starts = (None,) if count_y == 2 else (rows - PAD, 0)
    sides = pl.pallas_call(
        functools.partial(side_kernel, starts),
        out_shape=tuple(shape((5, layers, PAD, height), f32) for _ in starts),
        in_specs=[whole(pl.ANY)] * 3,
        out_specs=tuple(whole(pl.ANY) for _ in starts),
        scratch_shapes=[pltpu.SemaphoreType.DMA((len(starts), 3))],
        compiler_params=params,
        name="side",
    )(*raw)
    if count_y == 2:
        left = right = lax.ppermute(sides[0], "gy", [(0, 1), (1, 0)])
    else:
        left = lax.ppermute(sides[0], "gy", shifts(count_y, 1, False))
        right = lax.ppermute(sides[1], "gy", shifts(count_y, -1, False))

    message_shape = (9 * rows + 16, height)
    near_message, far_message = pl.pallas_call(
        pack_kernel,
        out_shape=(shape(message_shape, bf16), shape(message_shape, bf16)),
        in_specs=[whole(pl.ANY)] * 3,
        out_specs=(whole(), whole()),
        scratch_shapes=[
            pltpu.VMEM((2, 5, 2, rows, height), f32),
            pltpu.SemaphoreType.DMA((2, 3)),
        ],
        compiler_params=params,
        name="pack",
    )(*raw)
    near_message, far_message = pl.pallas_call(
        functools.partial(corner_kernel, count_y),
        out_shape=(shape(message_shape, bf16), shape(message_shape, bf16)),
        in_specs=[whole()] * 4,
        out_specs=(whole(), whole()),
        input_output_aliases={2: 0, 3: 1},
        compiler_params=params,
        name="corner",
    )(left, right, near_message, far_message)
    tied = lax.optimization_barrier(
        (
            near_message, far_message, left, right, panel_shapes, node_shapes, panel_area, slot_panel,
            damper_node, damper_viscous, damper_hysteretic, damper_state, modal_state,
        )
    )
    (
        near_message, far_message, left, right, panel_shapes, node_shapes, panel_area, slot_panel,
        damper_node, damper_viscous, damper_hysteretic, damper_state, modal_state,
    ) = tied
    near_message = lax.ppermute(near_message, "gx", pairs(count_x, 0))
    far_message = lax.ppermute(far_message, "gx", pairs(count_x, 1))

    def around(value):
        return [value] + [
            lax.ppermute(value, "gy", shifts(count_y, q, True)) for q in range(1, count_y)
        ]

    def damper_row(value, filler=0.0):
        extra = damper_padded - damper_count
        return jnp.pad(value, (0, extra), constant_values=filler)[None]

    tables = around(panel_shapes)
    ids = slot_panel
    if slots != slots_padded:
        ids = jnp.pad(
            ids.reshape(count_x, slots),
            ((0, 0), (0, slots_padded - slots)),
            constant_values=-1,
        ).reshape(1, slot_count)
    own_ids = lax.dynamic_slice_in_dim(ids, ix * slots_padded, slots_padded, axis=1)
    small = jnp.concatenate(
        [
            ids.astype(f32),
            damper_row(damper_viscous),
            damper_row(damper_hysteretic),
            damper_row(damper_state),
            damper_row(damper_node.astype(f32), -4.0),
        ],
        axis=1,
    )
    smalls = around(small)
    cell = jnp.pad(slot_cell, ((0, 0), (0, slots_padded - slots)))

    shapes, partial, pick, weight, *spreads = pl.pallas_call(
        functools.partial(prepare_kernel, slot_count, damper_padded),
        out_shape=(
            shape((count_y, 2, damper_padded, mode_count), bf16),
            shape((2, damper_padded), f32),
            shape((slots_padded, layers * rows), bf16),
            shape((slots_padded, height), f32),
        )
        + (shape((LANES, slot_count), bf16),) * count_y,
        in_specs=[whole()] * (5 + count_y),
        out_specs=(whole(),) * (4 + count_y),
        compiler_params=params,
        name="prepare",
    )(own_ids, cell, panel_area.reshape(-1, LANES), node_shapes, modal_state, *smalls)

    tall = rows + 2 * PAD
    wind = wind_profile[None, :]
    velocity_next, old, mid, visc, pre_core = pl.pallas_call(
        functools.partial(inner_kernel, count_y),
        out_shape=(
            shape(velocity.shape, f32),
            shape((2, 4, 5, tall, height), f32),
            shape((2, 4, 5, tall, height), f32),
            shape((2, 5, tall, height), f32),
            shape((layers - 4, rows, height), f32),
        ),
        in_specs=[whole(pl.ANY)] * 3 + [whole()] + [whole(pl.ANY)] * 2,
        out_specs=(whole(pl.ANY), whole(), whole(), whole(), whole()),
        scratch_shapes=[
            pltpu.VMEM((4, layers, tall, height), f32),
            pltpu.VMEM((4, layers, tall, height), f32),
            pltpu.VMEM((layers, tall, height), f32),
            pltpu.VMEM((3, layers - 4, rows, height), f32),
            pltpu.SemaphoreType.DMA((9,)),
            pltpu.SemaphoreType.DMA,
        ],
        compiler_params=params,
        name="inner",
    )(*raw, wind, left, right)

    velocity_next, pressure_next, payload, *_ = pl.pallas_call(
        functools.partial(edge_kernel, count_x, count_y),
        out_shape=(
            shape(velocity.shape, f32),
            shape(pressure.shape, f32),
            shape((total, load_rows + 2, LANES), f32),
            shape(old.shape, f32),
            shape(mid.shape, f32),
            shape(visc.shape, f32),
        ),
        in_specs=[whole()] * 7
        + [whole(pl.ANY)]
        + [whole()] * 3,
        out_specs=(whole(pl.ANY), whole(pl.ANY), whole(), whole(), whole(), whole()),
        input_output_aliases={7: 0, 8: 3, 9: 4, 10: 5},
        scratch_shapes=[
            pltpu.VMEM((layers, rows, height), f32),
            pltpu.VMEM((2, 3, 2, rows, height), f32),
            pltpu.SemaphoreType.DMA((3,)),
        ],
        compiler_params=params,
        name="edge",
    )(
        near_message, far_message, wind, pick, weight, partial, pre_core,
        velocity_next, old, mid, visc,
    )
    received = lax.all_to_all(payload, both, 0, 0, tiled=True)
    received = received.reshape(count_x, count_y, load_rows + 2, LANES)

    frequency = frequency[None]
    damping_ratio = damping_ratio[None]
    payload, state, hysteresis = pl.pallas_call(
        functools.partial(first_kernel, count_x, count_y, load_rows),
        out_shape=(
            shape((total, 2, damper_padded), f32),
            shape((4, mode_count), f32),
            shape((count_y, 1, damper_padded), f32),
        ),
        in_specs=[whole()] * (5 + 3 * count_y),
        out_specs=(whole(), whole(), whole()),
        compiler_params=params,
        name="first",
    )(received, shapes, modal_state, frequency, damping_ratio, *smalls, *tables, *spreads)
    received = lax.all_to_all(payload, both, 0, 0, tiled=True)
    received = received.reshape(count_x, count_y, 2, damper_padded)

    modal_next, damper_next = pl.pallas_call(
        functools.partial(second_kernel, count_x, count_y, slot_count),
        out_shape=(
            shape((2, mode_count), f32),
            shape((1, damper_count), f32),
        ),
        in_specs=[whole()] * (6 + count_y),
        out_specs=(whole(), whole()),
        compiler_params=params,
        name="second",
    )(received, shapes, frequency, damping_ratio, state, hysteresis, *smalls)
    return (velocity_next, pressure_next, modal_next, damper_next.reshape(damper_count))


def solution(mesh):
    placed = (
        P(None, "gx", "gy", None),
        P("gx", "gy", None),
        P("gx", "gy", None),
        P(),
        P("gy"),
        P("gy", "gx"),
        P("gy", None),
        P("gy", "gx"),
        P(None, "gx"),
        P("gy"),
        P("gy"),
        P("gy"),
        P("gx"),
        P("gx"),
        P(None, "gx"),
        P("gy"),
    )
    return jax.shard_map(
        body,
        mesh=mesh,
        in_specs=placed,
        out_specs=(P(None, "gx", "gy", None), P("gx", "gy", None), P(None, "gx"), P("gy")),
        check_vma=False,
    )
```

```python
import functools

import jax
import jax.numpy as jnp
from jax import lax
from jax.experimental import pallas as pl
from jax.experimental.pallas import tpu as pltpu
from jax.sharding import PartitionSpec as P

f32 = jnp.float32
bf16 = jnp.bfloat16
time_step = 0.1
modal_step = 0.5
shape_beta = 0.5
shape_gamma = 0.5
spring_rate = 0.5
LANES = 128
PAD = 8
VMEM_BYTES = 40 * 1024 * 1024


def shifts(size, step, cyclic):
    if cyclic:
        return [((i + step) % size, i) for i in range(size)]
    return [(i, i + step) for i in range(size) if 0 <= i + step < size]


def pairs(size, first):
    lower = range(first, size - 1, 2)
    return [(i, i + 1) for i in lower] + [(i + 1, i) for i in lower]


def parts_of(row):
    high = row.astype(bf16).astype(f32)
    rest = row - high
    middle = rest.astype(bf16).astype(f32)
    return [high, middle, rest - middle]


def stacked(rows):
    filler = jnp.zeros((16 - len(rows), rows[0].shape[1]), f32)
    return jnp.concatenate(rows + [filler], axis=0).astype(bf16)


def pack_kernel(starts, vel, pre, vis, near_out, far_out, *refs):
    sides, (stage, sem, side_sem) = refs[:-3], refs[-3:]
    layers, rows, height = pre.shape
    odd = lax.rem(lax.axis_index("gx"), 2)
    messages = ((near_out, 1 - odd), (far_out, odd))
    copies = []
    for place, (out, upward) in enumerate(messages):
        first = upward * (layers - 2)
        near = upward * (layers - 1)
        copies += [
            pltpu.make_async_copy(
                vel.at[:, pl.ds(first, 2)], stage.at[place, pl.ds(0, 3)], sem.at[place, 0]
            ),
            pltpu.make_async_copy(pre.at[pl.ds(first, 2)], stage.at[place, 3], sem.at[place, 1]),
            pltpu.make_async_copy(vis.at[near], stage.at[place, 4, 0], sem.at[place, 2]),
        ]
    more = []
    for place, (start, out) in enumerate(zip(starts, sides)):
        if start is None:
            start = jnp.where(lax.axis_index("gy") == 0, rows - PAD, 0)
        here = pl.ds(pl.multiple_of(start, PAD), PAD)
        more += [
            pltpu.make_async_copy(vel.at[:, :, here], out.at[pl.ds(0, 3)], side_sem.at[place, 0]),
            pltpu.make_async_copy(pre.at[:, here], out.at[3], side_sem.at[place, 1]),
            pltpu.make_async_copy(vis.at[:, here], out.at[4], side_sem.at[place, 2]),
        ]
    for copy in copies + more:
        copy.start()
    for copy in copies:
        copy.wait()
    for place, (out, _) in enumerate(messages):
        for field in range(4):
            for depth in range(2):
                start = (field * 2 + depth) * rows
                out[start : start + rows, :] = stage[place, field, depth].astype(bf16)
        out[8 * rows : 9 * rows, :] = stage[place, 4, 0].astype(bf16)
    for copy in more:
        copy.wait()


def corner_kernel(count_y, left, right, far_in, far_out):
    layers, height = left.shape[1], left.shape[3]
    start = far_out.shape[0] - 16
    iy = lax.axis_index("gy")
    near = lax.rem(lax.axis_index("gx"), 2) * (layers - 1)
    lines = [left[f, near, PAD - 1 : PAD, :] for f in range(4)]
    lines = [jnp.where(iy > 0, line, 0.0) for line in lines]
    others = [right[f, near, 0:1, :] for f in range(4)]
    lines += [jnp.where(iy < count_y - 1, line, 0.0) for line in others]
    lines.append(jnp.zeros((8, height), f32))
    far_out[start : start + 16, :] = jnp.concatenate(lines, axis=0).astype(bf16)


def line_kernel(rows, message, *outs):
    odd = lax.rem(lax.axis_index("gx"), 2)
    height = message.shape[1]

    def lines(row):
        low = row // 16 * 16
        found = []
        for field in range(4):
            pair = []
            for depth in range(2):
                start = (field * 2 + depth) * rows + low
                block = message[start : start + 16, :].astype(f32)
                pair.append(block[row - low : row - low + 1])
            found.append(jnp.where(odd == 1, pair[1], pair[0]))
        return jnp.concatenate(found + [jnp.zeros((4, height), f32)], axis=0)

    last, first = lines(rows - 1), lines(0)
    if len(outs) == 1:
        outs[0][...] = jnp.where(lax.axis_index("gy") == 0, last, first)
    else:
        outs[0][...] = last
        outs[1][...] = first


def stepper(wind, height):
    lane = lax.broadcasted_iota(jnp.int32, (8, height), 1)
    top = lane == height - 1
    bottom = lane == 0
    half = 0.5 * time_step
    wind_part = jnp.broadcast_to(wind[...] * half, (8, height))

    def step(get, factor, row, edge):
        def at(offset, low):
            return [get(f, offset, low) for f in range(4)]

        centre, ahead, behind = at(0, row), at(1, row), at(-1, row)
        lower = [pltpu.roll(c, 1, 0) for c in centre] if edge < 0 else at(0, row - 1)
        upper = [pltpu.roll(c, 7, 0) for c in centre] if edge > 0 else at(0, row + 1)
        above = [jnp.where(top, 0.0, pltpu.roll(c, height - 1, 1)) for c in centre]
        below = [jnp.where(bottom, 0.0, pltpu.roll(c, 1, 1)) for c in centre]
        factor = factor * time_step
        slopes = (ahead[3] - behind[3], upper[3] - lower[3], above[3] - below[3])
        result = []
        for i in range(3):
            around = (ahead[i] + behind[i]) + (upper[i] + lower[i]) + (above[i] + below[i])
            result.append(
                centre[i]
                + factor * (around - 6.0 * centre[i])
                - wind_part * (ahead[i] - behind[i])
                - half * slopes[i]
            )
        result.append(
            centre[3]
            - half * ((ahead[0] - behind[0]) + (upper[1] - lower[1]) + (above[2] - below[2]))
        )
        return result

    return step


def inner_kernel(
    count_y, vel, pre, vis, wind, left, right,
    vel_out, old_edge, mid_edge, visc_edge, pre_out,
    old, mid, visc, sem,
):
    layers, rows, height = pre.shape
    last = PAD + rows
    iy = lax.axis_index("gy")
    has_left = iy > 0
    has_right = iy < count_y - 1
    core = pl.ds(PAD, rows)
    copies = [
        pltpu.make_async_copy(vel.at[i], old.at[i, :, core], sem.at[i]) for i in range(3)
    ]
    copies.append(pltpu.make_async_copy(pre, old.at[3, :, core], sem.at[3]))
    copies.append(pltpu.make_async_copy(vis, visc.at[:, core], sem.at[4]))
    for place, (source, row) in enumerate(((left, 0), (right, last))):
        copies.append(
            pltpu.make_async_copy(
                source.at[pl.ds(0, 4)], old.at[:, :, pl.ds(row, PAD)], sem.at[5 + 2 * place]
            )
        )
        copies.append(
            pltpu.make_async_copy(
                source.at[4], visc.at[:, pl.ds(row, PAD)], sem.at[6 + 2 * place]
            )
        )
    for copy in copies:
        copy.start()
    for copy in copies:
        copy.wait()
    blank = jnp.zeros((4, layers, PAD, height), f32)

    @pl.when(jnp.logical_not(has_left))
    def _():
        old[:, :, 0:PAD, :] = blank
        mid[:, :, 0:PAD, :] = blank

    @pl.when(jnp.logical_not(has_right))
    def _():
        old[:, :, last : last + PAD, :] = blank
        mid[:, :, last : last + PAD, :] = blank

    step = stepper(wind, height)

    def advance(source, layer, row, edge=0):
        def get(f, offset, low):
            return source[f, layer + offset, pl.ds(low, 8), :]

        return step(get, visc[layer, pl.ds(row, 8), :], row, edge)

    def first(layer, row, edge=0):
        result = advance(old, layer, row, edge)
        for f in range(4):
            mid[f, layer, pl.ds(row, 8), :] = result[f]

    @pl.loop(1, layers - 1)
    def _(layer):
        for row in range(PAD, last, 8):
            first(layer, row)

    @pl.when(has_left)
    def _():
        @pl.loop(1, layers - 1)
        def _(layer):
            first(layer, 0, -1)

    @pl.when(has_right)
    def _():
        @pl.loop(1, layers - 1)
        def _(layer):
            first(layer, last, 1)

    @pl.loop(2, layers - 2)
    def _(layer):
        for row in range(PAD, last, 8):
            result = advance(mid, layer, row)
            for i in range(3):
                vel_out[i, layer, row - PAD : row - PAD + 8, :] = result[i]
            pre_out[layer, row - PAD : row - PAD + 8, :] = result[3]

    for side, first_old, place_old, first_mid, place_mid in (
        (0, 0, 2, 1, 3),
        (1, layers - 2, 1, layers - 3, 0),
    ):
        for depth in range(2):
            visc_edge[side, place_old + depth] = visc[first_old + depth]
            for f in range(4):
                old_edge[side, f, place_old + depth] = old[f, first_old + depth]
                mid_edge[side, f, place_mid + depth] = mid[f, first_mid + depth]


def edge_kernel(
    count_x, count_y, near_message, far_message, left_lines, right_lines, wind, pick, weight, found, partial,
    vel_in, pre_in, old_in, mid_in, visc_in,
    vel_out, pre_full, payload, old, mid, visc,
):
    layers, rows, height = pre_full.shape
    last = PAD + rows
    ix = lax.axis_index("gx")
    iy = lax.axis_index("gy")
    has_left = iy > 0
    has_right = iy < count_y - 1
    has_before = ix > 0
    has_after = ix < count_x - 1
    odd = lax.rem(ix, 2)
    for message, side in ((near_message, 1 - odd), (far_message, odd)):
        near = 1 + 2 * side
        for field in range(4):
            for depth in range(2):
                start = (field * 2 + depth) * rows
                old[side, field, 3 * side + depth, PAD:last, :] = message[
                    start : start + rows, :
                ].astype(f32)
        visc[side, near, PAD:last, :] = message[8 * rows : 9 * rows, :].astype(f32)
        if message is near_message:
            low = jnp.where(has_left, left_lines[...], 0.0)
            high = jnp.where(has_right, right_lines[...], 0.0)
        else:
            corner = message[9 * rows : 9 * rows + 16, :].astype(f32)
            low, high = corner[0:4], corner[4:8]
        for field in range(4):
            old[side, field, near, PAD - 1 : PAD, :] = low[field : field + 1]
            old[side, field, near, last : last + 1, :] = high[field : field + 1]

    step = stepper(wind, height)

    def advance(source, side, layer, row, edge=0):
        def get(f, offset, low):
            return source[side, f, layer + offset, pl.ds(low, 8), :]

        return step(get, visc[side, layer, pl.ds(row, 8), :], row, edge)

    def first(side, layer, row, edge=0):
        result = advance(old, side, layer, row, edge)
        for f in range(4):
            mid[side, f, layer, pl.ds(row, 8), :] = result[f]

    blank = jnp.zeros((4, PAD, height), f32)

    @pl.loop(0, 2)
    def _(side):
        there = jnp.where(side == 0, has_before, has_after)
        outside = 1 + 2 * side
        for row in range(PAD, last, 8):
            first(side, 2, row)

        @pl.when(has_left)
        def _():
            first(side, 2, 0, -1)

        @pl.when(jnp.logical_not(has_left))
        def _():
            mid[side, :, 2, 0:PAD, :] = blank

        @pl.when(has_right)
        def _():
            first(side, 2, last, 1)

        @pl.when(jnp.logical_not(has_right))
        def _():
            mid[side, :, 2, last : last + PAD, :] = blank

        @pl.when(there)
        def _():
            for row in range(PAD, last, 8):
                first(side, outside, row)

        @pl.when(jnp.logical_not(there))
        def _():
            mid[side, :, outside, PAD:last, :] = jnp.zeros((4, rows, height), f32)

        for row in range(PAD, last, 8):
            for layer, place in ((2, side), (3 - 2 * side, 1 - side)):
                result = advance(mid, side, layer, row)
                here = pl.ds(row - PAD, 8)
                target = side * (layers - 2) + place
                for i in range(3):
                    vel_out[i, target, here, :] = result[i]
                pre_full[target, here, :] = result[3]

    flat = [pre_full[start : start + 2].reshape(2 * rows, height) for start in (0, layers - 2)]
    total = found[...]
    for part in parts_of(jnp.concatenate(flat, axis=0)):
        total = total + jnp.dot(pick[...], part.astype(bf16), preferred_element_type=f32)
    loads = jnp.sum(weight[...] * total, axis=1, keepdims=True).astype(bf16).astype(f32)
    slots = weight.shape[0]
    same = lax.broadcasted_iota(jnp.int32, (LANES, LANES), 0) == lax.broadcasted_iota(
        jnp.int32, (LANES, LANES), 1
    )
    lines = []
    for start in range(0, slots, LANES):
        chosen = jnp.where(same, loads[start : start + LANES], 0.0)
        lines.append(jnp.sum(chosen, axis=0, keepdims=True))
    message = jnp.concatenate(lines + [partial[...]], axis=0)
    payload[...] = jnp.broadcast_to(message[None], payload.shape)


def prepare_kernel(slot_count, damper_width, own_ids, cell, areas, nodes, modal, pre, *refs):
    count_y = (len(refs) - 5) // 2
    smalls = refs[:count_y]
    shapes, partial, pick, weight, found = refs[count_y : count_y + 5]
    spreads = refs[count_y + 5 :]
    layers, rows = pre.shape[:2]
    high_count = areas.shape[0]
    slots = own_ids.shape[1]
    height = weight.shape[1]
    ids = own_ids[...]
    high = jnp.where(ids < 0, -1, ids // LANES)
    low = ids - high * LANES
    high_pick = lax.broadcasted_iota(jnp.int32, (high_count, slots), 0) == high
    low_pick = lax.broadcasted_iota(jnp.int32, (LANES, slots), 0) == low
    high_pick = high_pick.astype(f32).astype(bf16)
    spread = jnp.zeros((LANES, slots), f32)
    for part in parts_of(areas[...]):
        spread = spread + lax.dot_general(
            part.astype(bf16),
            high_pick,
            (((0,), (0,)), ((), ())),
            preferred_element_type=f32,
        )
    area = jnp.sum(jnp.where(low_pick, spread, 0.0), axis=0, keepdims=True)
    same = lax.broadcasted_iota(jnp.int32, (LANES, LANES), 0) == lax.broadcasted_iota(
        jnp.int32, (LANES, LANES), 1
    )

    def stand(row):
        lines = [
            jnp.sum(jnp.where(same, row[:, k : k + LANES], 0.0), axis=1, keepdims=True)
            for k in range(0, slots, LANES)
        ]
        return jnp.concatenate(lines, axis=0)

    place = cell[...]
    line = place // height
    level = place - line * height
    line, level = stand(line.astype(f32)), stand(level.astype(f32))
    rank = lax.broadcasted_iota(jnp.int32, (slots, 4 * rows), 1).astype(f32)
    shift = jnp.where(rank < 2 * rows, 0.0, float((layers - 4) * rows))
    pick[...] = (rank + shift == line).astype(f32).astype(bf16)
    inside = lax.broadcasted_iota(jnp.int32, (slots, (layers - 4) * rows), 1).astype(f32)
    inside = (inside + 2.0 * rows == line).astype(f32).astype(bf16)
    core = pre[2 : layers - 2].reshape((layers - 4) * rows, height)
    total = jnp.zeros((slots, height), f32)
    for part in parts_of(core):
        total = total + jnp.dot(inside, part.astype(bf16), preferred_element_type=f32)
    found[...] = total
    rank = lax.broadcasted_iota(jnp.int32, (slots, height), 1).astype(f32)
    weight[...] = jnp.where(rank == level, stand(area), 0.0)
    low_rank = lax.broadcasted_iota(jnp.int32, (LANES, slot_count), 0).astype(f32)
    node_rank = lax.broadcasted_iota(jnp.int32, (nodes.shape[0], damper_width), 0).astype(f32)
    table = nodes[...]
    for q, small in enumerate(smalls):
        numbers = small[:, :slot_count]
        numbers = numbers - jnp.floor(numbers * (1.0 / LANES)) * LANES
        spreads[q][...] = (low_rank == numbers).astype(f32).astype(bf16)
        lower = small[:, slot_count + 3 * damper_width : slot_count + 4 * damper_width]
        for end in range(2):
            picked = (node_rank == lower + (1.0 - end)).astype(f32).astype(bf16)
            rows = lax.dot_general(
                picked, table, (((0,), (0,)), ((), ())), preferred_element_type=f32
            )
            shapes[q, end] = rows.astype(bf16)
    state = modal[...]
    partial[...] = drift_times(state[0:1], state[1:2], shapes)


def respond(stretch, rate, hysteresis, viscous, hysteretic):
    hysteresis = hysteresis + modal_step * (
        rate
        - shape_beta * jnp.abs(rate) * hysteresis
        - shape_gamma * rate * jnp.abs(hysteresis)
    )
    force = -(viscous * rate + spring_rate * stretch + hysteretic * hysteresis)
    return hysteresis, force


def pulled(forces, shapes):
    sides = []
    for force in forces:
        three = jnp.concatenate(parts_of(force) + [jnp.zeros((13, force.shape[1]), f32)], axis=0)
        sides += [three, -three]
    left = jnp.concatenate(sides, axis=1).astype(bf16)
    right = shapes[...].reshape(-1, shapes.shape[-1])
    return jnp.sum(jnp.dot(left, right, preferred_element_type=f32), axis=0, keepdims=True)


def drift_times(displacement, velocity, shapes):
    pair = lax.dot_general(
        stacked(parts_of(displacement) + parts_of(velocity)),
        shapes[0].reshape(-1, shapes.shape[-1]),
        (((1,), (1,)), ((), ())),
        preferred_element_type=f32,
    )
    width = pair.shape[1] // 2
    drift = pair[:, :width] - pair[:, width:]
    return jnp.concatenate(
        [
            jnp.sum(drift[0:3], axis=0, keepdims=True),
            jnp.sum(drift[3:6], axis=0, keepdims=True),
        ],
        axis=0,
    )


def advance_modes(load, frequency, ratio, displacement, velocity):
    acceleration = (
        load
        - 2.0 * ratio * frequency * velocity
        - frequency * frequency * displacement
    )
    velocity = velocity + modal_step * acceleration
    return displacement + modal_step * velocity, velocity


def damper_rows(small, slot_count, width):
    return [small[:, slot_count + k * width : slot_count + (k + 1) * width] for k in range(3)]


def first_kernel(count_x, count_y, load_rows, *refs):
    received, shapes, modal, frequency, ratio = refs[:5]
    smalls = refs[5 : 5 + count_y]
    tables = refs[5 + count_y : 5 + 2 * count_y]
    spreads = refs[5 + 2 * count_y : 5 + 3 * count_y]
    vel, pre, payload, state, hysteresis_out, vel_out, pre_out, sem = refs[5 + 3 * count_y :]
    writes = [
        pltpu.make_async_copy(vel, vel_out, sem.at[0]),
        pltpu.make_async_copy(pre, pre_out, sem.at[1]),
    ]
    for write in writes:
        write.start()
    iy = lax.axis_index("gy")
    panel_count = tables[0].shape[0]
    high_count = panel_count // LANES
    slot_count = count_x * load_rows * LANES
    width = payload.shape[-1]
    rank = lax.broadcasted_iota(jnp.int32, (high_count, LANES), 0).astype(f32)
    sides = []
    forces = []
    for q in range(count_y):
        piece = lax.rem(iy + q, count_y)
        ids = smalls[q][:, :slot_count]
        high = jnp.floor(ids * (1.0 / LANES))
        chunks = []
        for i in range(count_x):
            for r in range(load_rows):
                start = (i * load_rows + r) * LANES
                line = received[i, piece, r : r + 1, :]
                chunks.append(
                    jnp.where(rank == high[:, start : start + LANES], line, 0.0).astype(bf16)
                )
        sorted_loads = lax.dot_general(
            jnp.concatenate(chunks, axis=1),
            spreads[q][...],
            (((1,), (1,)), ((), ())),
            preferred_element_type=f32,
        )
        sides.append(
            jnp.concatenate(
                [jnp.where(rank == c, sorted_loads, 0.0).astype(bf16) for c in range(high_count)],
                axis=1,
            )
        )
        stretch = received[0, piece, load_rows : load_rows + 1, :]
        rate = received[0, piece, load_rows + 1 : load_rows + 2, :]
        for i in range(1, count_x):
            stretch = stretch + received[i, piece, load_rows : load_rows + 1, :]
            rate = rate + received[i, piece, load_rows + 1 : load_rows + 2, :]
        viscous, hysteretic, held_state = damper_rows(smalls[q], slot_count, width)
        hysteresis, force = respond(stretch, rate, held_state, viscous, hysteretic)
        hysteresis_out[q] = hysteresis
        forces.append(force)
    load = pulled(forces, shapes)
    rows = jnp.zeros((high_count, modal.shape[1]), f32)
    for q in range(count_y):
        rows = rows + jnp.dot(sides[q], tables[q][...], preferred_element_type=f32)
    panel_modal = jnp.sum(rows, axis=0, keepdims=True)
    displacement, velocity = advance_modes(
        panel_modal + load, frequency[...], ratio[...], modal[0:1, :], modal[1:2, :]
    )
    state[0:1, :] = displacement
    state[1:2, :] = velocity
    state[2:3, :] = panel_modal
    state[3:4, :] = panel_modal
    message = drift_times(displacement, velocity, shapes)
    payload[...] = jnp.broadcast_to(message[None], payload.shape)
    for write in writes:
        write.wait()


def second_kernel(count_x, count_y, slot_count, *refs):
    received, shapes, frequency, ratio, state, held = refs[:6]
    smalls = refs[6 : 6 + count_y]
    modal, damper = refs[6 + count_y :]
    iy = lax.axis_index("gy")
    forces = []
    for q in range(count_y):
        piece = lax.rem(iy + q, count_y)
        stretch = received[0, piece, 0:1, :]
        rate = received[0, piece, 1:2, :]
        for i in range(1, count_x):
            stretch = stretch + received[i, piece, 0:1, :]
            rate = rate + received[i, piece, 1:2, :]
        viscous, hysteretic, _ = damper_rows(smalls[q], slot_count, stretch.shape[1])
        hysteresis, force = respond(stretch, rate, held[q], viscous, hysteretic)
        if q == 0:
            damper[...] = hysteresis[:, : damper.shape[1]]
        forces.append(force)
    load = state[2:3, :] + pulled(forces, shapes)
    displacement, velocity = advance_modes(
        load, frequency[...], ratio[...], state[0:1, :], state[1:2, :]
    )
    modal[0:1, :] = displacement
    modal[1:2, :] = velocity


def whole(space=pltpu.VMEM):
    return pl.BlockSpec(memory_space=space)


def body(
    velocity,
    pressure,
    viscosity,
    wind_profile,
    panel_area,
    slot_cell,
    slot_panel,
    panel_shapes,
    node_shapes,
    damper_node,
    damper_viscous,
    damper_hysteretic,
    frequency,
    damping_ratio,
    modal_state,
    damper_state,
):
    count_x = lax.axis_size("gx")
    count_y = lax.axis_size("gy")
    total = count_x * count_y
    both = ("gx", "gy")
    ix = lax.axis_index("gx")
    layers, rows, height = pressure.shape
    slots = slot_cell.shape[1]
    slots_padded = -(-slots // LANES) * LANES
    load_rows = slots_padded // LANES
    slot_count = count_x * slots_padded
    damper_count = damper_node.shape[0]
    damper_padded = -(-damper_count // LANES) * LANES
    mode_count = frequency.shape[0]
    params = pltpu.CompilerParams(vmem_limit_bytes=VMEM_BYTES)
    shape = jax.ShapeDtypeStruct

    raw = [
        pltpu.with_memory_space_constraint(value, pltpu.HBM)
        for value in (velocity, pressure, viscosity)
    ]
    starts = (None,) if count_y == 2 else (rows - PAD, 0)

    def swapped(values):
        if count_y == 2:
            value = lax.ppermute(values[0], "gy", [(0, 1), (1, 0)])
            return value, value
        return (
            lax.ppermute(values[0], "gy", shifts(count_y, 1, False)),
            lax.ppermute(values[1], "gy", shifts(count_y, -1, False)),
        )

    near_shape, far_shape = (9 * rows, height), (9 * rows + 16, height)
    near_message, far_message, *sides = pl.pallas_call(
        functools.partial(pack_kernel, starts),
        out_shape=(pltpu.VMEM(near_shape, bf16), pltpu.VMEM(far_shape, bf16))
        + tuple(shape((5, layers, PAD, height), f32) for _ in starts),
        in_specs=[whole(pl.ANY)] * 3,
        out_specs=(whole(),) * 2 + (whole(pl.ANY),) * len(starts),
        scratch_shapes=[
            pltpu.VMEM((2, 5, 2, rows, height), f32),
            pltpu.SemaphoreType.DMA((2, 3)),
            pltpu.SemaphoreType.DMA((len(starts), 3)),
        ],
        compiler_params=params,
        name="pack",
    )(*raw)
    near_message = lax.ppermute(near_message, "gx", pairs(count_x, 0))
    left, right = swapped(sides)
    far_message = pl.pallas_call(
        functools.partial(corner_kernel, count_y),
        out_shape=pltpu.VMEM(far_shape, bf16),
        in_specs=[whole()] * 3,
        out_specs=whole(),
        input_output_aliases={2: 0},
        compiler_params=params,
        name="corner",
    )(left, right, far_message)
    tied = lax.optimization_barrier(
        (
            far_message, left, right, panel_shapes, node_shapes, panel_area, slot_panel,
            damper_node, damper_viscous, damper_hysteretic, damper_state, modal_state,
        )
    )
    (
        far_message, left, right, panel_shapes, node_shapes, panel_area, slot_panel,
        damper_node, damper_viscous, damper_hysteretic, damper_state, modal_state,
    ) = tied
    far_message = lax.ppermute(far_message, "gx", pairs(count_x, 1))

    def around(value):
        return [value] + [
            lax.ppermute(value, "gy", shifts(count_y, q, True)) for q in range(1, count_y)
        ]

    def damper_row(value, filler=0.0):
        extra = damper_padded - damper_count
        return jnp.pad(value, (0, extra), constant_values=filler)[None]

    tables = around(panel_shapes)
    ids = slot_panel
    if slots != slots_padded:
        ids = jnp.pad(
            ids.reshape(count_x, slots),
            ((0, 0), (0, slots_padded - slots)),
            constant_values=-1,
        ).reshape(1, slot_count)
    own_ids = lax.dynamic_slice_in_dim(ids, ix * slots_padded, slots_padded, axis=1)
    small = jnp.concatenate(
        [
            ids.astype(f32),
            damper_row(damper_viscous),
            damper_row(damper_hysteretic),
            damper_row(damper_state),
            damper_row(damper_node.astype(f32), -4.0),
        ],
        axis=1,
    )
    smalls = around(small)
    cell = jnp.pad(slot_cell, ((0, 0), (0, slots_padded - slots)))

    tall = rows + 2 * PAD
    wind = wind_profile[None, :]
    velocity_next, old, mid, visc, pressure_next = pl.pallas_call(
        functools.partial(inner_kernel, count_y),
        out_shape=(
            pltpu.VMEM(velocity.shape, f32),
            shape((2, 4, 5, tall, height), f32),
            shape((2, 4, 5, tall, height), f32),
            shape((2, 5, tall, height), f32),
            pltpu.VMEM(pressure.shape, f32),
        ),
        in_specs=[whole(pl.ANY)] * 3 + [whole()] + [whole(pl.ANY)] * 2,
        out_specs=(whole(), whole(), whole(), whole(), whole()),
        scratch_shapes=[
            pltpu.VMEM((4, layers, tall, height), f32),
            pltpu.VMEM((4, layers, tall, height), f32),
            pltpu.VMEM((layers, tall, height), f32),
            pltpu.SemaphoreType.DMA((9,)),
        ],
        compiler_params=params,
        name="inner",
    )(*raw, wind, left, right)

    shapes, partial, pick, weight, found, *spreads = pl.pallas_call(
        functools.partial(prepare_kernel, slot_count, damper_padded),
        out_shape=(
            shape((count_y, 2, damper_padded, mode_count), bf16),
            shape((2, damper_padded), f32),
            shape((slots_padded, 4 * rows), bf16),
            shape((slots_padded, height), f32),
            shape((slots_padded, height), f32),
        )
        + (shape((LANES, slot_count), bf16),) * count_y,
        in_specs=[whole()] * (6 + count_y),
        out_specs=(whole(),) * (5 + count_y),
        compiler_params=params,
        name="prepare",
    )(
        own_ids, cell, panel_area.reshape(-1, LANES), node_shapes, modal_state,
        pressure_next, *smalls,
    )

    near_message, pressure_next = lax.optimization_barrier((near_message, pressure_next))
    lines = pl.pallas_call(
        functools.partial(line_kernel, rows),
        out_shape=tuple(shape((8, height), f32) for _ in starts),
        in_specs=[whole()],
        out_specs=tuple(whole() for _ in starts),
        compiler_params=params,
        name="lines",
    )(near_message)
    left_lines, right_lines = swapped(lines)
    velocity_next, pressure_next, payload, *_ = pl.pallas_call(
        functools.partial(edge_kernel, count_x, count_y),
        out_shape=(
            pltpu.VMEM(velocity.shape, f32),
            pltpu.VMEM(pressure.shape, f32),
            shape((total, load_rows + 2, LANES), f32),
            shape(old.shape, f32),
            shape(mid.shape, f32),
            shape(visc.shape, f32),
        ),
        in_specs=[whole()] * 14,
        out_specs=(whole(),) * 6,
        input_output_aliases={9: 0, 10: 1, 11: 3, 12: 4, 13: 5},
        compiler_params=params,
        name="edge",
    )(
        near_message, far_message, left_lines, right_lines,
        wind, pick, weight, found, partial,
        velocity_next, pressure_next, old, mid, visc,
    )
    received = lax.all_to_all(payload, both, 0, 0, tiled=True)
    received = received.reshape(count_x, count_y, load_rows + 2, LANES)

    frequency = frequency[None]
    damping_ratio = damping_ratio[None]
    payload, state, hysteresis, velocity_next, pressure_next = pl.pallas_call(
        functools.partial(first_kernel, count_x, count_y, load_rows),
        out_shape=(
            shape((total, 2, damper_padded), f32),
            shape((4, mode_count), f32),
            shape((count_y, 1, damper_padded), f32),
            shape(velocity.shape, f32),
            shape(pressure.shape, f32),
        ),
        in_specs=[whole()] * (7 + 3 * count_y),
        out_specs=(whole(),) * 3 + (whole(pl.ANY),) * 2,
        scratch_shapes=[pltpu.SemaphoreType.DMA((2,))],
        compiler_params=params,
        name="first",
    )(
        received, shapes, modal_state, frequency, damping_ratio,
        *smalls, *tables, *spreads, velocity_next, pressure_next,
    )
    received = lax.all_to_all(payload, both, 0, 0, tiled=True)
    received = received.reshape(count_x, count_y, 2, damper_padded)

    modal_next, damper_next = pl.pallas_call(
        functools.partial(second_kernel, count_x, count_y, slot_count),
        out_shape=(
            shape((2, mode_count), f32),
            shape((1, damper_count), f32),
        ),
        in_specs=[whole()] * (6 + count_y),
        out_specs=(whole(), whole()),
        compiler_params=params,
        name="second",
    )(received, shapes, frequency, damping_ratio, state, hysteresis, *smalls)
    return (velocity_next, pressure_next, modal_next, damper_next.reshape(damper_count))


def solution(mesh):
    placed = (
        P(None, "gx", "gy", None),
        P("gx", "gy", None),
        P("gx", "gy", None),
        P(),
        P("gy"),
        P("gy", "gx"),
        P("gy", None),
        P("gy", "gx"),
        P(None, "gx"),
        P("gy"),
        P("gy"),
        P("gy"),
        P("gx"),
        P("gx"),
        P(None, "gx"),
        P("gy"),
    )
    return jax.shard_map(
        body,
        mesh=mesh,
        in_specs=placed,
        out_specs=(P(None, "gx", "gy", None), P("gx", "gy", None), P(None, "gx"), P("gy")),
        check_vma=False,
    )
```

```python
import functools

import jax
import jax.numpy as jnp
from jax import lax
from jax.experimental import pallas as pl
from jax.experimental.pallas import tpu as pltpu
from jax.sharding import PartitionSpec as P

f32 = jnp.float32
bf16 = jnp.bfloat16
time_step = 0.1
modal_step = 0.5
shape_beta = 0.5
shape_gamma = 0.5
spring_rate = 0.5
LANES = 128
PAD = 8
VMEM_BYTES = 40 * 1024 * 1024


def shifts(size, step, cyclic):
    if cyclic:
        return [((i + step) % size, i) for i in range(size)]
    return [(i, i + step) for i in range(size) if 0 <= i + step < size]


def pairs(size, first):
    lower = range(first, size - 1, 2)
    return [(i, i + 1) for i in lower] + [(i + 1, i) for i in lower]


def parts_of(row):
    high = row.astype(bf16).astype(f32)
    rest = row - high
    middle = rest.astype(bf16).astype(f32)
    return [high, middle, rest - middle]


def stacked(rows):
    filler = jnp.zeros((16 - len(rows), rows[0].shape[1]), f32)
    return jnp.concatenate(rows + [filler], axis=0).astype(bf16)


def pack_kernel(starts, vel, pre, vis, near_out, far_out, *refs):
    sides, lines = refs[: len(starts)], refs[len(starts) : -3]
    stage, sem, side_sem = refs[-3:]
    layers, rows, height = pre.shape
    odd = lax.rem(lax.axis_index("gx"), 2)
    messages = ((near_out, 1 - odd), (far_out, odd))
    copies = []
    for place, (out, upward) in enumerate(messages):
        first = upward * (layers - 2)
        near = upward * (layers - 1)
        copies += [
            pltpu.make_async_copy(
                vel.at[:, pl.ds(first, 2)], stage.at[place, pl.ds(0, 3)], sem.at[place, 0]
            ),
            pltpu.make_async_copy(pre.at[pl.ds(first, 2)], stage.at[place, 3], sem.at[place, 1]),
            pltpu.make_async_copy(vis.at[near], stage.at[place, 4, 0], sem.at[place, 2]),
        ]
    more = []
    for place, (start, out) in enumerate(zip(starts, sides)):
        if start is None:
            start = jnp.where(lax.axis_index("gy") == 0, rows - PAD, 0)
        here = pl.ds(pl.multiple_of(start, PAD), PAD)
        more += [
            pltpu.make_async_copy(vel.at[:, :, here], out.at[pl.ds(0, 3)], side_sem.at[place, 0]),
            pltpu.make_async_copy(pre.at[:, here], out.at[3], side_sem.at[place, 1]),
            pltpu.make_async_copy(vis.at[:, here], out.at[4], side_sem.at[place, 2]),
        ]
    for copy in copies + more:
        copy.start()
    for copy in copies:
        copy.wait()
    for place, (out, _) in enumerate(messages):
        for field in range(4):
            for depth in range(2):
                start = (field * 2 + depth) * rows
                out[start : start + rows, :] = stage[place, field, depth].astype(bf16)
        out[8 * rows : 9 * rows, :] = stage[place, 4, 0].astype(bf16)
    last = [stage[0, f, 1 - odd, rows - 1 : rows, :] for f in range(4)]
    first = [stage[0, f, 1 - odd, 0:1, :] for f in range(4)]
    filler = [jnp.zeros((12, height), f32)]
    last = jnp.concatenate(last + filler, axis=0)
    first = jnp.concatenate(first + filler, axis=0)
    if len(lines) == 1:
        lines[0][...] = jnp.where(lax.axis_index("gy") == 0, last, first).astype(bf16)
    else:
        lines[0][...] = last.astype(bf16)
        lines[1][...] = first.astype(bf16)
    for copy in more:
        copy.wait()


def corner_kernel(count_y, left, right, far_in, far_out):
    layers, height = left.shape[1], left.shape[3]
    start = far_out.shape[0] - 16
    iy = lax.axis_index("gy")
    near = lax.rem(lax.axis_index("gx"), 2) * (layers - 1)
    lines = [left[f, near, PAD - 1 : PAD, :] for f in range(4)]
    lines = [jnp.where(iy > 0, line, 0.0) for line in lines]
    others = [right[f, near, 0:1, :] for f in range(4)]
    lines += [jnp.where(iy < count_y - 1, line, 0.0) for line in others]
    lines.append(jnp.zeros((8, height), f32))
    far_out[start : start + 16, :] = jnp.concatenate(lines, axis=0).astype(bf16)


def stepper(wind, height):
    lane = lax.broadcasted_iota(jnp.int32, (8, height), 1)
    top = lane == height - 1
    bottom = lane == 0
    half = 0.5 * time_step
    wind_part = jnp.broadcast_to(wind[...] * half, (8, height))

    def step(get, factor, row, edge):
        def at(offset, low):
            return [get(f, offset, low) for f in range(4)]

        centre, ahead, behind = at(0, row), at(1, row), at(-1, row)
        lower = [pltpu.roll(c, 1, 0) for c in centre] if edge < 0 else at(0, row - 1)
        upper = [pltpu.roll(c, 7, 0) for c in centre] if edge > 0 else at(0, row + 1)
        above = [jnp.where(top, 0.0, pltpu.roll(c, height - 1, 1)) for c in centre]
        below = [jnp.where(bottom, 0.0, pltpu.roll(c, 1, 1)) for c in centre]
        factor = factor * time_step
        slopes = (ahead[3] - behind[3], upper[3] - lower[3], above[3] - below[3])
        result = []
        for i in range(3):
            around = (ahead[i] + behind[i]) + (upper[i] + lower[i]) + (above[i] + below[i])
            result.append(
                centre[i]
                + factor * (around - 6.0 * centre[i])
                - wind_part * (ahead[i] - behind[i])
                - half * slopes[i]
            )
        result.append(
            centre[3]
            - half * ((ahead[0] - behind[0]) + (upper[1] - lower[1]) + (above[2] - below[2]))
        )
        return result

    return step


def inner_kernel(
    count_y, vel, pre, vis, wind, left, right,
    vel_out, old_edge, mid_edge, visc_edge, pre_out,
    old, mid, visc, sem,
):
    layers, rows, height = pre.shape
    last = PAD + rows
    iy = lax.axis_index("gy")
    has_left = iy > 0
    has_right = iy < count_y - 1
    core = pl.ds(PAD, rows)
    copies = [
        pltpu.make_async_copy(vel.at[i], old.at[i, :, core], sem.at[i]) for i in range(3)
    ]
    copies.append(pltpu.make_async_copy(pre, old.at[3, :, core], sem.at[3]))
    copies.append(pltpu.make_async_copy(vis, visc.at[:, core], sem.at[4]))
    for place, (source, row) in enumerate(((left, 0), (right, last))):
        copies.append(
            pltpu.make_async_copy(
                source.at[pl.ds(0, 4)], old.at[:, :, pl.ds(row, PAD)], sem.at[5 + 2 * place]
            )
        )
        copies.append(
            pltpu.make_async_copy(
                source.at[4], visc.at[:, pl.ds(row, PAD)], sem.at[6 + 2 * place]
            )
        )
    for copy in copies:
        copy.start()
    for copy in copies:
        copy.wait()
    blank = jnp.zeros((4, layers, PAD, height), f32)

    @pl.when(jnp.logical_not(has_left))
    def _():
        old[:, :, 0:PAD, :] = blank
        mid[:, :, 0:PAD, :] = blank

    @pl.when(jnp.logical_not(has_right))
    def _():
        old[:, :, last : last + PAD, :] = blank
        mid[:, :, last : last + PAD, :] = blank

    step = stepper(wind, height)

    def advance(source, layer, row, edge=0):
        def get(f, offset, low):
            return source[f, layer + offset, pl.ds(low, 8), :]

        return step(get, visc[layer, pl.ds(row, 8), :], row, edge)

    def first(layer, row, edge=0):
        result = advance(old, layer, row, edge)
        for f in range(4):
            mid[f, layer, pl.ds(row, 8), :] = result[f]

    @pl.loop(1, layers - 1)
    def _(layer):
        for row in range(PAD, last, 8):
            first(layer, row)

    @pl.when(has_left)
    def _():
        @pl.loop(1, layers - 1)
        def _(layer):
            first(layer, 0, -1)

    @pl.when(has_right)
    def _():
        @pl.loop(1, layers - 1)
        def _(layer):
            first(layer, last, 1)

    @pl.loop(2, layers - 2)
    def _(layer):
        for row in range(PAD, last, 8):
            result = advance(mid, layer, row)
            for i in range(3):
                vel_out[i, layer, row - PAD : row - PAD + 8, :] = result[i]
            pre_out[layer, row - PAD : row - PAD + 8, :] = result[3]

    for side, first_old, place_old, first_mid, place_mid in (
        (0, 0, 2, 1, 3),
        (1, layers - 2, 1, layers - 3, 0),
    ):
        for depth in range(2):
            visc_edge[side, place_old + depth] = visc[first_old + depth]
            for f in range(4):
                old_edge[side, f, place_old + depth] = old[f, first_old + depth]
                mid_edge[side, f, place_mid + depth] = mid[f, first_mid + depth]


def edge_kernel(count_x, count_y, is_near, message, *refs):
    if is_near:
        left_lines, right_lines = refs[:2]
        wind, pick, found = refs[2:5]
        vel_out, pre_out, found_out, old, mid, visc = refs[10:]
    else:
        wind, pick, found, weight, partial = refs[:5]
        vel_out, pre_out, payload, old, mid, visc = refs[10:]
    layers, rows, height = pre_out.shape
    last = PAD + rows
    ix = lax.axis_index("gx")
    iy = lax.axis_index("gy")
    has_left = iy > 0
    has_right = iy < count_y - 1
    odd = lax.rem(ix, 2)
    side = 1 - odd if is_near else odd
    there = jnp.where(side == 0, ix > 0, ix < count_x - 1)
    outside = 1 + 2 * side
    for field in range(4):
        for depth in range(2):
            start = (field * 2 + depth) * rows
            old[side, field, 3 * side + depth, PAD:last, :] = message[
                start : start + rows, :
            ].astype(f32)
    visc[side, outside, PAD:last, :] = message[8 * rows : 9 * rows, :].astype(f32)
    if is_near:
        low = jnp.where(has_left, left_lines[...].astype(f32), 0.0)
        high = jnp.where(has_right, right_lines[...].astype(f32), 0.0)
    else:
        corner = message[9 * rows : 9 * rows + 16, :].astype(f32)
        low, high = corner[0:4], corner[4:8]
    for field in range(4):
        old[side, field, outside, PAD - 1 : PAD, :] = low[field : field + 1]
        old[side, field, outside, last : last + 1, :] = high[field : field + 1]

    step = stepper(wind, height)

    def advance(source, layer, row, edge=0):
        def get(f, offset, low):
            return source[side, f, layer + offset, pl.ds(low, 8), :]

        return step(get, visc[side, layer, pl.ds(row, 8), :], row, edge)

    def first(layer, row, edge=0):
        result = advance(old, layer, row, edge)
        for f in range(4):
            mid[side, f, layer, pl.ds(row, 8), :] = result[f]

    blank = jnp.zeros((4, PAD, height), f32)
    for row in range(PAD, last, 8):
        first(2, row)

    @pl.when(has_left)
    def _():
        first(2, 0, -1)

    @pl.when(jnp.logical_not(has_left))
    def _():
        mid[side, :, 2, 0:PAD, :] = blank

    @pl.when(has_right)
    def _():
        first(2, last, 1)

    @pl.when(jnp.logical_not(has_right))
    def _():
        mid[side, :, 2, last : last + PAD, :] = blank

    @pl.when(there)
    def _():
        for row in range(PAD, last, 8):
            first(outside, row)

    @pl.when(jnp.logical_not(there))
    def _():
        mid[side, :, outside, PAD:last, :] = jnp.zeros((4, rows, height), f32)

    for row in range(PAD, last, 8):
        for layer, place in ((2, side), (3 - 2 * side, 1 - side)):
            result = advance(mid, layer, row)
            here = pl.ds(row - PAD, 8)
            target = side * (layers - 2) + place
            for i in range(3):
                vel_out[i, target, here, :] = result[i]
            pre_out[target, here, :] = result[3]

    flat = pre_out[pl.ds(side * (layers - 2), 2)].reshape(2 * rows, height)
    total = found[...]
    for part in parts_of(flat):
        total = total + jnp.dot(pick[side], part.astype(bf16), preferred_element_type=f32)
    if is_near:
        found_out[...] = total
        return
    loads = jnp.sum(weight[...] * total, axis=1, keepdims=True).astype(bf16).astype(f32)
    slots = weight.shape[0]
    same = lax.broadcasted_iota(jnp.int32, (LANES, LANES), 0) == lax.broadcasted_iota(
        jnp.int32, (LANES, LANES), 1
    )
    lines = []
    for start in range(0, slots, LANES):
        chosen = jnp.where(same, loads[start : start + LANES], 0.0)
        lines.append(jnp.sum(chosen, axis=0, keepdims=True))
    message = jnp.concatenate(lines + [partial[...]], axis=0)
    payload[...] = jnp.broadcast_to(message[None], payload.shape)


def prepare_kernel(slot_count, damper_width, own_ids, cell, areas, nodes, modal, pre, *refs):
    count_y = (len(refs) - 5) // 2
    smalls = refs[:count_y]
    shapes, partial, pick, weight, found = refs[count_y : count_y + 5]
    spreads = refs[count_y + 5 :]
    layers, rows = pre.shape[:2]
    high_count = areas.shape[0]
    slots = own_ids.shape[1]
    height = weight.shape[1]
    ids = own_ids[...]
    high = jnp.where(ids < 0, -1, ids // LANES)
    low = ids - high * LANES
    high_pick = lax.broadcasted_iota(jnp.int32, (high_count, slots), 0) == high
    low_pick = lax.broadcasted_iota(jnp.int32, (LANES, slots), 0) == low
    high_pick = high_pick.astype(f32).astype(bf16)
    spread = jnp.zeros((LANES, slots), f32)
    for part in parts_of(areas[...]):
        spread = spread + lax.dot_general(
            part.astype(bf16),
            high_pick,
            (((0,), (0,)), ((), ())),
            preferred_element_type=f32,
        )
    area = jnp.sum(jnp.where(low_pick, spread, 0.0), axis=0, keepdims=True)
    same = lax.broadcasted_iota(jnp.int32, (LANES, LANES), 0) == lax.broadcasted_iota(
        jnp.int32, (LANES, LANES), 1
    )

    def stand(row):
        lines = [
            jnp.sum(jnp.where(same, row[:, k : k + LANES], 0.0), axis=1, keepdims=True)
            for k in range(0, slots, LANES)
        ]
        return jnp.concatenate(lines, axis=0)

    place = cell[...]
    line = place // height
    level = place - line * height
    line, level = stand(line.astype(f32)), stand(level.astype(f32))
    rank = lax.broadcasted_iota(jnp.int32, (slots, 2 * rows), 1).astype(f32)
    for side in range(2):
        start = float(side * (layers - 2) * rows)
        pick[side] = (rank + start == line).astype(f32).astype(bf16)
    inside = lax.broadcasted_iota(jnp.int32, (slots, (layers - 4) * rows), 1).astype(f32)
    inside = (inside + 2.0 * rows == line).astype(f32).astype(bf16)
    core = pre[2 : layers - 2].reshape((layers - 4) * rows, height)
    total = jnp.zeros((slots, height), f32)
    for part in parts_of(core):
        total = total + jnp.dot(inside, part.astype(bf16), preferred_element_type=f32)
    found[...] = total
    rank = lax.broadcasted_iota(jnp.int32, (slots, height), 1).astype(f32)
    weight[...] = jnp.where(rank == level, stand(area), 0.0)
    low_rank = lax.broadcasted_iota(jnp.int32, (LANES, slot_count), 0).astype(f32)
    node_rank = lax.broadcasted_iota(jnp.int32, (nodes.shape[0], damper_width), 0).astype(f32)
    table = nodes[...]
    for q, small in enumerate(smalls):
        numbers = small[:, :slot_count]
        numbers = numbers - jnp.floor(numbers * (1.0 / LANES)) * LANES
        spreads[q][...] = (low_rank == numbers).astype(f32).astype(bf16)
        lower = small[:, slot_count + 3 * damper_width : slot_count + 4 * damper_width]
        for end in range(2):
            picked = (node_rank == lower + (1.0 - end)).astype(f32).astype(bf16)
            rows = lax.dot_general(
                picked, table, (((0,), (0,)), ((), ())), preferred_element_type=f32
            )
            shapes[q, end] = rows.astype(bf16)
    state = modal[...]
    partial[...] = drift_times(state[0:1], state[1:2], shapes)


def respond(stretch, rate, hysteresis, viscous, hysteretic):
    hysteresis = hysteresis + modal_step * (
        rate
        - shape_beta * jnp.abs(rate) * hysteresis
        - shape_gamma * rate * jnp.abs(hysteresis)
    )
    force = -(viscous * rate + spring_rate * stretch + hysteretic * hysteresis)
    return hysteresis, force


def pulled(forces, shapes):
    sides = []
    for force in forces:
        three = jnp.concatenate(parts_of(force) + [jnp.zeros((13, force.shape[1]), f32)], axis=0)
        sides += [three, -three]
    left = jnp.concatenate(sides, axis=1).astype(bf16)
    right = shapes[...].reshape(-1, shapes.shape[-1])
    return jnp.sum(jnp.dot(left, right, preferred_element_type=f32), axis=0, keepdims=True)


def drift_times(displacement, velocity, shapes):
    pair = lax.dot_general(
        stacked(parts_of(displacement) + parts_of(velocity)),
        shapes[0].reshape(-1, shapes.shape[-1]),
        (((1,), (1,)), ((), ())),
        preferred_element_type=f32,
    )
    width = pair.shape[1] // 2
    drift = pair[:, :width] - pair[:, width:]
    return jnp.concatenate(
        [
            jnp.sum(drift[0:3], axis=0, keepdims=True),
            jnp.sum(drift[3:6], axis=0, keepdims=True),
        ],
        axis=0,
    )


def advance_modes(load, frequency, ratio, displacement, velocity):
    acceleration = (
        load
        - 2.0 * ratio * frequency * velocity
        - frequency * frequency * displacement
    )
    velocity = velocity + modal_step * acceleration
    return displacement + modal_step * velocity, velocity


def damper_rows(small, slot_count, width):
    return [small[:, slot_count + k * width : slot_count + (k + 1) * width] for k in range(3)]


def first_kernel(count_x, count_y, load_rows, *refs):
    received, shapes, modal, frequency, ratio = refs[:5]
    smalls = refs[5 : 5 + count_y]
    tables = refs[5 + count_y : 5 + 2 * count_y]
    spreads = refs[5 + 2 * count_y : 5 + 3 * count_y]
    vel, pre, payload, state, hysteresis_out, vel_out, pre_out, sem = refs[5 + 3 * count_y :]
    writes = [
        pltpu.make_async_copy(vel, vel_out, sem.at[0]),
        pltpu.make_async_copy(pre, pre_out, sem.at[1]),
    ]
    for write in writes:
        write.start()
    iy = lax.axis_index("gy")
    panel_count = tables[0].shape[0]
    high_count = panel_count // LANES
    slot_count = count_x * load_rows * LANES
    width = payload.shape[-1]
    rank = lax.broadcasted_iota(jnp.int32, (high_count, LANES), 0).astype(f32)
    sides = []
    forces = []
    for q in range(count_y):
        piece = lax.rem(iy + q, count_y)
        ids = smalls[q][:, :slot_count]
        high = jnp.floor(ids * (1.0 / LANES))
        chunks = []
        for i in range(count_x):
            for r in range(load_rows):
                start = (i * load_rows + r) * LANES
                line = received[i, piece, r : r + 1, :]
                chunks.append(
                    jnp.where(rank == high[:, start : start + LANES], line, 0.0).astype(bf16)
                )
        sorted_loads = lax.dot_general(
            jnp.concatenate(chunks, axis=1),
            spreads[q][...],
            (((1,), (1,)), ((), ())),
            preferred_element_type=f32,
        )
        sides.append(
            jnp.concatenate(
                [jnp.where(rank == c, sorted_loads, 0.0).astype(bf16) for c in range(high_count)],
                axis=1,
            )
        )
        stretch = received[0, piece, load_rows : load_rows + 1, :]
        rate = received[0, piece, load_rows + 1 : load_rows + 2, :]
        for i in range(1, count_x):
            stretch = stretch + received[i, piece, load_rows : load_rows + 1, :]
            rate = rate + received[i, piece, load_rows + 1 : load_rows + 2, :]
        viscous, hysteretic, held_state = damper_rows(smalls[q], slot_count, width)
        hysteresis, force = respond(stretch, rate, held_state, viscous, hysteretic)
        hysteresis_out[q] = hysteresis
        forces.append(force)
    load = pulled(forces, shapes)
    rows = jnp.zeros((high_count, modal.shape[1]), f32)
    for q in range(count_y):
        rows = rows + jnp.dot(sides[q], tables[q][...], preferred_element_type=f32)
    panel_modal = jnp.sum(rows, axis=0, keepdims=True)
    displacement, velocity = advance_modes(
        panel_modal + load, frequency[...], ratio[...], modal[0:1, :], modal[1:2, :]
    )
    state[0:1, :] = displacement
    state[1:2, :] = velocity
    state[2:3, :] = panel_modal
    state[3:4, :] = panel_modal
    message = drift_times(displacement, velocity, shapes)
    payload[...] = jnp.broadcast_to(message[None], payload.shape)
    for write in writes:
        write.wait()


def second_kernel(count_x, count_y, slot_count, *refs):
    received, shapes, frequency, ratio, state, held = refs[:6]
    smalls = refs[6 : 6 + count_y]
    modal, damper = refs[6 + count_y :]
    iy = lax.axis_index("gy")
    forces = []
    for q in range(count_y):
        piece = lax.rem(iy + q, count_y)
        stretch = received[0, piece, 0:1, :]
        rate = received[0, piece, 1:2, :]
        for i in range(1, count_x):
            stretch = stretch + received[i, piece, 0:1, :]
            rate = rate + received[i, piece, 1:2, :]
        viscous, hysteretic, _ = damper_rows(smalls[q], slot_count, stretch.shape[1])
        hysteresis, force = respond(stretch, rate, held[q], viscous, hysteretic)
        if q == 0:
            damper[...] = hysteresis[:, : damper.shape[1]]
        forces.append(force)
    load = state[2:3, :] + pulled(forces, shapes)
    displacement, velocity = advance_modes(
        load, frequency[...], ratio[...], state[0:1, :], state[1:2, :]
    )
    modal[0:1, :] = displacement
    modal[1:2, :] = velocity


def whole(space=pltpu.VMEM):
    return pl.BlockSpec(memory_space=space)


def body(
    velocity,
    pressure,
    viscosity,
    wind_profile,
    panel_area,
    slot_cell,
    slot_panel,
    panel_shapes,
    node_shapes,
    damper_node,
    damper_viscous,
    damper_hysteretic,
    frequency,
    damping_ratio,
    modal_state,
    damper_state,
):
    count_x = lax.axis_size("gx")
    count_y = lax.axis_size("gy")
    total = count_x * count_y
    both = ("gx", "gy")
    ix = lax.axis_index("gx")
    layers, rows, height = pressure.shape
    slots = slot_cell.shape[1]
    slots_padded = -(-slots // LANES) * LANES
    load_rows = slots_padded // LANES
    slot_count = count_x * slots_padded
    damper_count = damper_node.shape[0]
    damper_padded = -(-damper_count // LANES) * LANES
    mode_count = frequency.shape[0]
    params = pltpu.CompilerParams(vmem_limit_bytes=VMEM_BYTES)
    shape = jax.ShapeDtypeStruct

    raw = [
        pltpu.with_memory_space_constraint(value, pltpu.HBM)
        for value in (velocity, pressure, viscosity)
    ]
    starts = (None,) if count_y == 2 else (rows - PAD, 0)

    def swapped(values):
        if count_y == 2:
            value = lax.ppermute(values[0], "gy", [(0, 1), (1, 0)])
            return value, value
        return (
            lax.ppermute(values[0], "gy", shifts(count_y, 1, False)),
            lax.ppermute(values[1], "gy", shifts(count_y, -1, False)),
        )

    near_shape, far_shape = (9 * rows, height), (9 * rows + 16, height)
    near_message, far_message, *rest = pl.pallas_call(
        functools.partial(pack_kernel, starts),
        out_shape=(pltpu.VMEM(near_shape, bf16), pltpu.VMEM(far_shape, bf16))
        + tuple(shape((5, layers, PAD, height), f32) for _ in starts)
        + tuple(pltpu.VMEM((16, height), bf16) for _ in starts),
        in_specs=[whole(pl.ANY)] * 3,
        out_specs=(whole(),) * 2 + (whole(pl.ANY),) * len(starts) + (whole(),) * len(starts),
        scratch_shapes=[
            pltpu.VMEM((2, 5, 2, rows, height), f32),
            pltpu.SemaphoreType.DMA((2, 3)),
            pltpu.SemaphoreType.DMA((len(starts), 3)),
        ],
        compiler_params=params,
        name="pack",
    )(*raw)
    near_message = lax.ppermute(near_message, "gx", pairs(count_x, 0))
    left, right = swapped(rest[: len(starts)])
    lines = rest[len(starts) :]
    far_message = pl.pallas_call(
        functools.partial(corner_kernel, count_y),
        out_shape=pltpu.VMEM(far_shape, bf16),
        in_specs=[whole()] * 3,
        out_specs=whole(),
        input_output_aliases={2: 0},
        compiler_params=params,
        name="corner",
    )(left, right, far_message)
    tied = lax.optimization_barrier(
        (
            far_message, left, right, panel_shapes, node_shapes, panel_area, slot_panel,
            damper_node, damper_viscous, damper_hysteretic, damper_state, modal_state,
        )
    )
    (
        far_message, left, right, panel_shapes, node_shapes, panel_area, slot_panel,
        damper_node, damper_viscous, damper_hysteretic, damper_state, modal_state,
    ) = tied
    far_message = lax.ppermute(far_message, "gx", pairs(count_x, 1))
    across = [
        [
            (i * count_y + k, j * count_y + k + step)
            for i, j in pairs(count_x, 0)
            for k in range(count_y)
            if 0 <= k + step < count_y
        ]
        for step in (1, -1)
    ]
    if count_y == 2:
        left_lines = right_lines = lax.ppermute(lines[0], both, across[0] + across[1])
    else:
        left_lines = lax.ppermute(lines[0], both, across[0])
        right_lines = lax.ppermute(lines[1], both, across[1])

    def around(value):
        return [value] + [
            lax.ppermute(value, "gy", shifts(count_y, q, True)) for q in range(1, count_y)
        ]

    def damper_row(value, filler=0.0):
        extra = damper_padded - damper_count
        return jnp.pad(value, (0, extra), constant_values=filler)[None]

    tables = around(panel_shapes)
    ids = slot_panel
    if slots != slots_padded:
        ids = jnp.pad(
            ids.reshape(count_x, slots),
            ((0, 0), (0, slots_padded - slots)),
            constant_values=-1,
        ).reshape(1, slot_count)
    own_ids = lax.dynamic_slice_in_dim(ids, ix * slots_padded, slots_padded, axis=1)
    small = jnp.concatenate(
        [
            ids.astype(f32),
            damper_row(damper_viscous),
            damper_row(damper_hysteretic),
            damper_row(damper_state),
            damper_row(damper_node.astype(f32), -4.0),
        ],
        axis=1,
    )
    smalls = around(small)
    cell = jnp.pad(slot_cell, ((0, 0), (0, slots_padded - slots)))

    tall = rows + 2 * PAD
    wind = wind_profile[None, :]
    velocity_next, old, mid, visc, pressure_next = pl.pallas_call(
        functools.partial(inner_kernel, count_y),
        out_shape=(
            pltpu.VMEM(velocity.shape, f32),
            shape((2, 4, 5, tall, height), f32),
            shape((2, 4, 5, tall, height), f32),
            shape((2, 5, tall, height), f32),
            pltpu.VMEM(pressure.shape, f32),
        ),
        in_specs=[whole(pl.ANY)] * 3 + [whole()] + [whole(pl.ANY)] * 2,
        out_specs=(whole(), whole(), whole(), whole(), whole()),
        scratch_shapes=[
            pltpu.VMEM((4, layers, tall, height), f32),
            pltpu.VMEM((4, layers, tall, height), f32),
            pltpu.VMEM((layers, tall, height), f32),
            pltpu.SemaphoreType.DMA((9,)),
        ],
        compiler_params=params,
        name="inner",
    )(*raw, wind, left, right)

    shapes, partial, pick, weight, found, *spreads = pl.pallas_call(
        functools.partial(prepare_kernel, slot_count, damper_padded),
        out_shape=(
            shape((count_y, 2, damper_padded, mode_count), bf16),
            shape((2, damper_padded), f32),
            shape((2, slots_padded, 2 * rows), bf16),
            shape((slots_padded, height), f32),
            shape((slots_padded, height), f32),
        )
        + (shape((LANES, slot_count), bf16),) * count_y,
        in_specs=[whole()] * (6 + count_y),
        out_specs=(whole(),) * (5 + count_y),
        compiler_params=params,
        name="prepare",
    )(
        own_ids, cell, panel_area.reshape(-1, LANES), node_shapes, modal_state,
        pressure_next, *smalls,
    )

    def edge(is_near, result, *operands):
        kept = (velocity_next, pressure_next, old, mid, visc)
        base = len(operands)
        return pl.pallas_call(
            functools.partial(edge_kernel, count_x, count_y, is_near),
            out_shape=(
                pltpu.VMEM(velocity.shape, f32),
                pltpu.VMEM(pressure.shape, f32),
                result,
                pltpu.VMEM(old.shape, f32),
                pltpu.VMEM(mid.shape, f32),
                pltpu.VMEM(visc.shape, f32),
            ),
            in_specs=[whole()] * (base + 5),
            out_specs=(whole(),) * 6,
            input_output_aliases={base: 0, base + 1: 1, base + 2: 3, base + 3: 4, base + 4: 5},
            compiler_params=params,
            name="near" if is_near else "far",
        )(*operands, *kept)

    velocity_next, pressure_next, found, old, mid, visc = edge(
        True,
        pltpu.VMEM(found.shape, f32),
        near_message,
        left_lines,
        right_lines,
        wind,
        pick,
        found,
    )
    velocity_next, pressure_next, payload, *_ = edge(
        False,
        shape((total, load_rows + 2, LANES), f32),
        far_message,
        wind,
        pick,
        found,
        weight,
        partial,
    )
    received = lax.all_to_all(payload, both, 0, 0, tiled=True)
    received = received.reshape(count_x, count_y, load_rows + 2, LANES)

    frequency = frequency[None]
    damping_ratio = damping_ratio[None]
    payload, state, hysteresis, velocity_next, pressure_next = pl.pallas_call(
        functools.partial(first_kernel, count_x, count_y, load_rows),
        out_shape=(
            shape((total, 2, damper_padded), f32),
            shape((4, mode_count), f32),
            shape((count_y, 1, damper_padded), f32),
            shape(velocity.shape, f32),
            shape(pressure.shape, f32),
        ),
        in_specs=[whole()] * (7 + 3 * count_y),
        out_specs=(whole(),) * 3 + (whole(pl.ANY),) * 2,
        scratch_shapes=[pltpu.SemaphoreType.DMA((2,))],
        compiler_params=params,
        name="first",
    )(
        received, shapes, modal_state, frequency, damping_ratio,
        *smalls, *tables, *spreads, velocity_next, pressure_next,
    )
    received = lax.all_to_all(payload, both, 0, 0, tiled=True)
    received = received.reshape(count_x, count_y, 2, damper_padded)

    modal_next, damper_next = pl.pallas_call(
        functools.partial(second_kernel, count_x, count_y, slot_count),
        out_shape=(
            shape((2, mode_count), f32),
            shape((1, damper_count), f32),
        ),
        in_specs=[whole()] * (6 + count_y),
        out_specs=(whole(), whole()),
        compiler_params=params,
        name="second",
    )(received, shapes, frequency, damping_ratio, state, hysteresis, *smalls)
    return (velocity_next, pressure_next, modal_next, damper_next.reshape(damper_count))


def solution(mesh):
    placed = (
        P(None, "gx", "gy", None),
        P("gx", "gy", None),
        P("gx", "gy", None),
        P(),
        P("gy"),
        P("gy", "gx"),
        P("gy", None),
        P("gy", "gx"),
        P(None, "gx"),
        P("gy"),
        P("gy"),
        P("gy"),
        P("gx"),
        P("gx"),
        P(None, "gx"),
        P("gy"),
    )
    return jax.shard_map(
        body,
        mesh=mesh,
        in_specs=placed,
        out_specs=(P(None, "gx", "gy", None), P("gx", "gy", None), P(None, "gx"), P("gy")),
        check_vma=False,
    )
```

```python
import functools

import jax
import jax.numpy as jnp
from jax import lax
from jax.experimental import pallas as pl
from jax.experimental.pallas import tpu as pltpu
from jax.sharding import PartitionSpec as P

f32 = jnp.float32
bf16 = jnp.bfloat16
time_step = 0.1
modal_step = 0.5
shape_beta = 0.5
shape_gamma = 0.5
spring_rate = 0.5
LANES = 128
PAD = 8
VMEM_BYTES = 40 * 1024 * 1024


def shifts(size, step, cyclic):
    if cyclic:
        return [((i + step) % size, i) for i in range(size)]
    return [(i, i + step) for i in range(size) if 0 <= i + step < size]


def pairs(size, first):
    lower = range(first, size - 1, 2)
    return [(i, i + 1) for i in lower] + [(i + 1, i) for i in lower]


def parts_of(row):
    high = row.astype(bf16).astype(f32)
    rest = row - high
    middle = rest.astype(bf16).astype(f32)
    return [high, middle, rest - middle]


def stacked(rows):
    filler = jnp.zeros((16 - len(rows), rows[0].shape[1]), f32)
    return jnp.concatenate(rows + [filler], axis=0).astype(bf16)


def pack_kernel(starts, vel, pre, vis, near_out, far_out, *refs):
    sides, lines = refs[: len(starts)], refs[len(starts) : -3]
    stage, sem, side_sem = refs[-3:]
    layers, rows, height = pre.shape
    odd = lax.rem(lax.axis_index("gx"), 2)
    messages = ((near_out, 1 - odd), (far_out, odd))
    copies = []
    for place, (out, upward) in enumerate(messages):
        first = upward * (layers - 2)
        near = upward * (layers - 1)
        copies += [
            pltpu.make_async_copy(
                vel.at[:, pl.ds(first, 2)], stage.at[place, pl.ds(0, 3)], sem.at[place, 0]
            ),
            pltpu.make_async_copy(pre.at[pl.ds(first, 2)], stage.at[place, 3], sem.at[place, 1]),
            pltpu.make_async_copy(vis.at[near], stage.at[place, 4, 0], sem.at[place, 2]),
        ]
    more = []
    for place, (start, out) in enumerate(zip(starts, sides)):
        if start is None:
            start = jnp.where(lax.axis_index("gy") == 0, rows - PAD, 0)
        here = pl.ds(pl.multiple_of(start, PAD), PAD)
        more += [
            pltpu.make_async_copy(vel.at[:, :, here], out.at[pl.ds(0, 3)], side_sem.at[place, 0]),
            pltpu.make_async_copy(pre.at[:, here], out.at[3], side_sem.at[place, 1]),
            pltpu.make_async_copy(vis.at[:, here], out.at[4], side_sem.at[place, 2]),
        ]
    for copy in copies + more:
        copy.start()
    for copy in copies:
        copy.wait()
    for place, (out, _) in enumerate(messages):
        for field in range(4):
            for depth in range(2):
                start = (field * 2 + depth) * rows
                out[start : start + rows, :] = stage[place, field, depth].astype(bf16)
        out[8 * rows : 9 * rows, :] = stage[place, 4, 0].astype(bf16)
    last = [stage[0, f, 1 - odd, rows - 1 : rows, :] for f in range(4)]
    first = [stage[0, f, 1 - odd, 0:1, :] for f in range(4)]
    filler = [jnp.zeros((12, height), f32)]
    last = jnp.concatenate(last + filler, axis=0)
    first = jnp.concatenate(first + filler, axis=0)
    if len(lines) == 1:
        lines[0][...] = jnp.where(lax.axis_index("gy") == 0, last, first).astype(bf16)
    else:
        lines[0][...] = last.astype(bf16)
        lines[1][...] = first.astype(bf16)
    for copy in more:
        copy.wait()


def corner_kernel(count_y, left, right, far_in, far_out):
    layers, height = left.shape[1], left.shape[3]
    start = far_out.shape[0] - 16
    iy = lax.axis_index("gy")
    near = lax.rem(lax.axis_index("gx"), 2) * (layers - 1)
    lines = [left[f, near, PAD - 1 : PAD, :] for f in range(4)]
    lines = [jnp.where(iy > 0, line, 0.0) for line in lines]
    others = [right[f, near, 0:1, :] for f in range(4)]
    lines += [jnp.where(iy < count_y - 1, line, 0.0) for line in others]
    lines.append(jnp.zeros((8, height), f32))
    far_out[start : start + 16, :] = jnp.concatenate(lines, axis=0).astype(bf16)


def stepper(wind, height):
    lane = lax.broadcasted_iota(jnp.int32, (8, height), 1)
    top = lane == height - 1
    bottom = lane == 0
    half = 0.5 * time_step
    wind_part = jnp.broadcast_to(wind[...] * half, (8, height))

    def step(get, factor, row, edge):
        def at(offset, low):
            return [get(f, offset, low) for f in range(4)]

        centre, ahead, behind = at(0, row), at(1, row), at(-1, row)
        lower = [pltpu.roll(c, 1, 0) for c in centre] if edge < 0 else at(0, row - 1)
        upper = [pltpu.roll(c, 7, 0) for c in centre] if edge > 0 else at(0, row + 1)
        above = [jnp.where(top, 0.0, pltpu.roll(c, height - 1, 1)) for c in centre]
        below = [jnp.where(bottom, 0.0, pltpu.roll(c, 1, 1)) for c in centre]
        factor = factor * time_step
        slopes = (ahead[3] - behind[3], upper[3] - lower[3], above[3] - below[3])
        result = []
        for i in range(3):
            around = (ahead[i] + behind[i]) + (upper[i] + lower[i]) + (above[i] + below[i])
            result.append(
                centre[i]
                + factor * (around - 6.0 * centre[i])
                - wind_part * (ahead[i] - behind[i])
                - half * slopes[i]
            )
        result.append(
            centre[3]
            - half * ((ahead[0] - behind[0]) + (upper[1] - lower[1]) + (above[2] - below[2]))
        )
        return result

    return step


def inner_kernel(
    count_y, vel, pre, vis, wind, left, right,
    vel_out, old_edge, mid_edge, visc_edge, pre_out,
    old, mid, visc, sem,
):
    layers, rows, height = pre.shape
    last = PAD + rows
    iy = lax.axis_index("gy")
    has_left = iy > 0
    has_right = iy < count_y - 1
    core = pl.ds(PAD, rows)
    copies = [
        pltpu.make_async_copy(vel.at[i], old.at[i, :, core], sem.at[i]) for i in range(3)
    ]
    copies.append(pltpu.make_async_copy(pre, old.at[3, :, core], sem.at[3]))
    copies.append(pltpu.make_async_copy(vis, visc.at[:, core], sem.at[4]))
    for place, (source, row) in enumerate(((left, 0), (right, last))):
        copies.append(
            pltpu.make_async_copy(
                source.at[pl.ds(0, 4)], old.at[:, :, pl.ds(row, PAD)], sem.at[5 + 2 * place]
            )
        )
        copies.append(
            pltpu.make_async_copy(
                source.at[4], visc.at[:, pl.ds(row, PAD)], sem.at[6 + 2 * place]
            )
        )
    for copy in copies:
        copy.start()
    for copy in copies:
        copy.wait()
    blank = jnp.zeros((4, layers, PAD, height), f32)

    @pl.when(jnp.logical_not(has_left))
    def _():
        old[:, :, 0:PAD, :] = blank
        mid[:, :, 0:PAD, :] = blank

    @pl.when(jnp.logical_not(has_right))
    def _():
        old[:, :, last : last + PAD, :] = blank
        mid[:, :, last : last + PAD, :] = blank

    step = stepper(wind, height)

    nothing = jnp.zeros((8, height), f32)

    def advance(source, layer, row, edge=0, missing=0):
        def get(f, offset, low):
            if missing and offset == missing:
                return nothing
            return source[f, layer + offset, pl.ds(low, 8), :]

        return step(get, visc[layer, pl.ds(row, 8), :], row, edge)

    def first(layer, row, edge=0):
        result = advance(old, layer, row, edge)
        for f in range(4):
            mid[f, layer, pl.ds(row, 8), :] = result[f]

    @pl.loop(1, layers - 1)
    def _(layer):
        for row in range(PAD, last, 8):
            first(layer, row)

    @pl.when(has_left)
    def _():
        @pl.loop(1, layers - 1)
        def _(layer):
            first(layer, 0, -1)

    @pl.when(has_right)
    def _():
        @pl.loop(1, layers - 1)
        def _(layer):
            first(layer, last, 1)

    @pl.loop(2, layers - 2)
    def _(layer):
        for row in range(PAD, last, 8):
            result = advance(mid, layer, row)
            for i in range(3):
                vel_out[i, layer, row - PAD : row - PAD + 8, :] = result[i]
            pre_out[layer, row - PAD : row - PAD + 8, :] = result[3]

    for side, own, inside, place, missing in (
        (0, 0, 1, 3, -1),
        (1, layers - 1, layers - 2, 1, 1),
    ):

        def begin(row, edge, side=side, own=own, missing=missing):
            result = advance(old, own, row, edge, missing)
            for f in range(4):
                mid_edge[side, f, 2, row : row + 8, :] = result[f]

        for row in range(PAD, last, 8):
            begin(row, 0)
            result = advance(mid, inside, row, 0, missing)
            here = slice(row - PAD, row - PAD + 8)
            for i in range(3):
                vel_out[i, inside, here, :] = result[i]
            pre_out[inside, here, :] = result[3]
        for there, row, edge in ((has_left, 0, -1), (has_right, last, 1)):

            @pl.when(there)
            def _(begin=begin, row=row, edge=edge):
                begin(row, edge)

            @pl.when(jnp.logical_not(there))
            def _(side=side, row=row):
                mid_edge[side, :, 2, row : row + PAD, :] = jnp.zeros((4, PAD, height), f32)

        visc_edge[side, 2] = visc[own]
        visc_edge[side, place] = visc[inside]
        for f in range(4):
            old_edge[side, f, 2] = old[f, own]
            mid_edge[side, f, place] = mid[f, inside]


def edge_kernel(count_x, count_y, is_near, message, *refs):
    if is_near:
        left_lines, right_lines = refs[:2]
        wind, pick, found = refs[2:5]
        vel_out, pre_out, found_out, old, mid, visc = refs[10:]
    else:
        wind, pick, found, weight, partial = refs[:5]
        vel_out, pre_out, payload, old, mid, visc = refs[10:]
    layers, rows, height = pre_out.shape
    last = PAD + rows
    ix = lax.axis_index("gx")
    iy = lax.axis_index("gy")
    has_left = iy > 0
    has_right = iy < count_y - 1
    odd = lax.rem(ix, 2)
    side = 1 - odd if is_near else odd
    there = jnp.where(side == 0, ix > 0, ix < count_x - 1)
    outside = 1 + 2 * side
    for field in range(4):
        for depth in range(2):
            start = (field * 2 + depth) * rows
            old[side, field, 3 * side + depth, PAD:last, :] = message[
                start : start + rows, :
            ].astype(f32)
    visc[side, outside, PAD:last, :] = message[8 * rows : 9 * rows, :].astype(f32)
    if is_near:
        low = jnp.where(has_left, left_lines[...].astype(f32), 0.0)
        high = jnp.where(has_right, right_lines[...].astype(f32), 0.0)
    else:
        corner = message[9 * rows : 9 * rows + 16, :].astype(f32)
        low, high = corner[0:4], corner[4:8]
    for field in range(4):
        old[side, field, outside, PAD - 1 : PAD, :] = low[field : field + 1]
        old[side, field, outside, last : last + 1, :] = high[field : field + 1]

    step = stepper(wind, height)

    def advance(source, layer, row, edge=0):
        def get(f, offset, low):
            return source[side, f, layer + offset, pl.ds(low, 8), :]

        return step(get, visc[side, layer, pl.ds(row, 8), :], row, edge)

    def first(layer, row, edge=0, keep=None):
        result = advance(old, layer, row, edge)
        for f in range(4):
            value = result[f] if keep is None else jnp.where(keep, result[f], 0.0)
            mid[side, f, layer, pl.ds(row, 8), :] = value

    sign = 1.0 - 2.0 * side.astype(f32)
    windy = jnp.broadcast_to(wind[...] * (0.5 * time_step), (8, height)) * sign
    pull = sign * (0.5 * time_step)

    def light(source, layer, other, row, write):
        here = pl.ds(row, 8)
        o = [source[side, f, other, here, :] for f in range(4)]
        c = visc[side, layer, here, :] * time_step + windy
        write(0, c * o[0] + pull * o[3])
        write(1, c * o[1])
        write(2, c * o[2])
        write(3, pull * o[0])

    for row in range(0, last + PAD, 8):
        def write(f, value, row=row):
            mid[side, f, 2, pl.ds(row, 8), :] += value
        light(old, 2, outside, row, write)
    for row in range(PAD, last, 8):
        first(outside, row, 0, there)

    for row in range(PAD, last, 8):
        result = advance(mid, 2, row)
        here = pl.ds(row - PAD, 8)
        target = side * (layers - 1)
        for i in range(3):
            vel_out[i, target, here, :] = result[i]
        pre_out[target, here, :] = result[3]
        target = 1 + side * (layers - 3)

        def write(f, value, here=here, target=target):
            if f < 3:
                vel_out[f, target, here, :] += value
            else:
                pre_out[target, here, :] += value

        light(mid, 3 - 2 * side, 2, row, write)

    flat = pre_out[pl.ds(side * (layers - 2), 2)].reshape(2 * rows, height)
    total = found[...]
    for part in parts_of(flat):
        total = total + jnp.dot(pick[side], part.astype(bf16), preferred_element_type=f32)
    if is_near:
        found_out[...] = total
        return
    loads = jnp.sum(weight[...] * total, axis=1, keepdims=True).astype(bf16).astype(f32)
    slots = weight.shape[0]
    same = lax.broadcasted_iota(jnp.int32, (LANES, LANES), 0) == lax.broadcasted_iota(
        jnp.int32, (LANES, LANES), 1
    )
    lines = []
    for start in range(0, slots, LANES):
        chosen = jnp.where(same, loads[start : start + LANES], 0.0)
        lines.append(jnp.sum(chosen, axis=0, keepdims=True))
    message = jnp.concatenate(lines + [partial[...]], axis=0)
    payload[...] = jnp.broadcast_to(message[None], payload.shape)


def prepare_kernel(slot_count, damper_width, own_ids, cell, areas, nodes, modal, pre, *refs):
    count_y = (len(refs) - 5) // 2
    smalls = refs[:count_y]
    shapes, partial, pick, weight, found = refs[count_y : count_y + 5]
    spreads = refs[count_y + 5 :]
    layers, rows = pre.shape[:2]
    high_count = areas.shape[0]
    slots = own_ids.shape[1]
    height = weight.shape[1]
    ids = own_ids[...]
    high = jnp.where(ids < 0, -1, ids // LANES)
    low = ids - high * LANES
    high_pick = lax.broadcasted_iota(jnp.int32, (high_count, slots), 0) == high
    low_pick = lax.broadcasted_iota(jnp.int32, (LANES, slots), 0) == low
    high_pick = high_pick.astype(f32).astype(bf16)
    spread = jnp.zeros((LANES, slots), f32)
    for part in parts_of(areas[...]):
        spread = spread + lax.dot_general(
            part.astype(bf16),
            high_pick,
            (((0,), (0,)), ((), ())),
            preferred_element_type=f32,
        )
    area = jnp.sum(jnp.where(low_pick, spread, 0.0), axis=0, keepdims=True)
    same = lax.broadcasted_iota(jnp.int32, (LANES, LANES), 0) == lax.broadcasted_iota(
        jnp.int32, (LANES, LANES), 1
    )

    def stand(row):
        lines = [
            jnp.sum(jnp.where(same, row[:, k : k + LANES], 0.0), axis=1, keepdims=True)
            for k in range(0, slots, LANES)
        ]
        return jnp.concatenate(lines, axis=0)

    place = cell[...]
    line = place // height
    level = place - line * height
    line, level = stand(line.astype(f32)), stand(level.astype(f32))
    rank = lax.broadcasted_iota(jnp.int32, (slots, 2 * rows), 1).astype(f32)
    for side in range(2):
        start = float(side * (layers - 2) * rows)
        pick[side] = (rank + start == line).astype(f32).astype(bf16)
    inside = lax.broadcasted_iota(jnp.int32, (slots, (layers - 4) * rows), 1).astype(f32)
    inside = (inside + 2.0 * rows == line).astype(f32).astype(bf16)
    core = pre[2 : layers - 2].reshape((layers - 4) * rows, height)
    total = jnp.zeros((slots, height), f32)
    for part in parts_of(core):
        total = total + jnp.dot(inside, part.astype(bf16), preferred_element_type=f32)
    found[...] = total
    rank = lax.broadcasted_iota(jnp.int32, (slots, height), 1).astype(f32)
    weight[...] = jnp.where(rank == level, stand(area), 0.0)
    low_rank = lax.broadcasted_iota(jnp.int32, (LANES, slot_count), 0).astype(f32)
    node_rank = lax.broadcasted_iota(jnp.int32, (nodes.shape[0], damper_width), 0).astype(f32)
    table = nodes[...]
    for q, small in enumerate(smalls):
        numbers = small[:, :slot_count]
        numbers = numbers - jnp.floor(numbers * (1.0 / LANES)) * LANES
        spreads[q][...] = (low_rank == numbers).astype(f32).astype(bf16)
        lower = small[:, slot_count + 3 * damper_width : slot_count + 4 * damper_width]
        for end in range(2):
            picked = (node_rank == lower + (1.0 - end)).astype(f32).astype(bf16)
            rows = lax.dot_general(
                picked, table, (((0,), (0,)), ((), ())), preferred_element_type=f32
            )
            shapes[q, end] = rows.astype(bf16)
    state = modal[...]
    partial[...] = drift_times(state[0:1], state[1:2], shapes)


def respond(stretch, rate, hysteresis, viscous, hysteretic):
    hysteresis = hysteresis + modal_step * (
        rate
        - shape_beta * jnp.abs(rate) * hysteresis
        - shape_gamma * rate * jnp.abs(hysteresis)
    )
    force = -(viscous * rate + spring_rate * stretch + hysteretic * hysteresis)
    return hysteresis, force


def pulled(forces, shapes):
    sides = []
    for force in forces:
        three = jnp.concatenate(parts_of(force) + [jnp.zeros((13, force.shape[1]), f32)], axis=0)
        sides += [three, -three]
    left = jnp.concatenate(sides, axis=1).astype(bf16)
    right = shapes[...].reshape(-1, shapes.shape[-1])
    return jnp.sum(jnp.dot(left, right, preferred_element_type=f32), axis=0, keepdims=True)


def drift_times(displacement, velocity, shapes):
    pair = lax.dot_general(
        stacked(parts_of(displacement) + parts_of(velocity)),
        shapes[0].reshape(-1, shapes.shape[-1]),
        (((1,), (1,)), ((), ())),
        preferred_element_type=f32,
    )
    width = pair.shape[1] // 2
    drift = pair[:, :width] - pair[:, width:]
    return jnp.concatenate(
        [
            jnp.sum(drift[0:3], axis=0, keepdims=True),
            jnp.sum(drift[3:6], axis=0, keepdims=True),
        ],
        axis=0,
    )


def advance_modes(load, frequency, ratio, displacement, velocity):
    acceleration = (
        load
        - 2.0 * ratio * frequency * velocity
        - frequency * frequency * displacement
    )
    velocity = velocity + modal_step * acceleration
    return displacement + modal_step * velocity, velocity


def damper_rows(small, slot_count, width):
    return [small[:, slot_count + k * width : slot_count + (k + 1) * width] for k in range(3)]


def first_kernel(count_x, count_y, load_rows, *refs):
    received, shapes, modal, frequency, ratio = refs[:5]
    smalls = refs[5 : 5 + count_y]
    tables = refs[5 + count_y : 5 + 2 * count_y]
    spreads = refs[5 + 2 * count_y : 5 + 3 * count_y]
    vel, pre, payload, state, hysteresis_out, vel_out, pre_out, sem = refs[5 + 3 * count_y :]
    writes = [
        pltpu.make_async_copy(vel, vel_out, sem.at[0]),
        pltpu.make_async_copy(pre, pre_out, sem.at[1]),
    ]
    for write in writes:
        write.start()
    iy = lax.axis_index("gy")
    panel_count = tables[0].shape[0]
    high_count = panel_count // LANES
    slot_count = count_x * load_rows * LANES
    width = payload.shape[-1]
    rank = lax.broadcasted_iota(jnp.int32, (high_count, LANES), 0).astype(f32)
    sides = []
    forces = []
    for q in range(count_y):
        piece = lax.rem(iy + q, count_y)
        ids = smalls[q][:, :slot_count]
        high = jnp.floor(ids * (1.0 / LANES))
        chunks = []
        for i in range(count_x):
            for r in range(load_rows):
                start = (i * load_rows + r) * LANES
                line = received[i, piece, r : r + 1, :]
                chunks.append(
                    jnp.where(rank == high[:, start : start + LANES], line, 0.0).astype(bf16)
                )
        sorted_loads = lax.dot_general(
            jnp.concatenate(chunks, axis=1),
            spreads[q][...],
            (((1,), (1,)), ((), ())),
            preferred_element_type=f32,
        )
        sides.append(
            jnp.concatenate(
                [jnp.where(rank == c, sorted_loads, 0.0).astype(bf16) for c in range(high_count)],
                axis=1,
            )
        )
        stretch = received[0, piece, load_rows : load_rows + 1, :]
        rate = received[0, piece, load_rows + 1 : load_rows + 2, :]
        for i in range(1, count_x):
            stretch = stretch + received[i, piece, load_rows : load_rows + 1, :]
            rate = rate + received[i, piece, load_rows + 1 : load_rows + 2, :]
        viscous, hysteretic, held_state = damper_rows(smalls[q], slot_count, width)
        hysteresis, force = respond(stretch, rate, held_state, viscous, hysteretic)
        hysteresis_out[q] = hysteresis
        forces.append(force)
    load = pulled(forces, shapes)
    rows = jnp.zeros((high_count, modal.shape[1]), f32)
    for q in range(count_y):
        rows = rows + jnp.dot(sides[q], tables[q][...], preferred_element_type=f32)
    panel_modal = jnp.sum(rows, axis=0, keepdims=True)
    displacement, velocity = advance_modes(
        panel_modal + load, frequency[...], ratio[...], modal[0:1, :], modal[1:2, :]
    )
    state[0:1, :] = displacement
    state[1:2, :] = velocity
    state[2:3, :] = panel_modal
    state[3:4, :] = panel_modal
    message = drift_times(displacement, velocity, shapes)
    payload[...] = jnp.broadcast_to(message[None], payload.shape)
    for write in writes:
        write.wait()


def second_kernel(count_x, count_y, slot_count, *refs):
    received, shapes, frequency, ratio, state, held = refs[:6]
    smalls = refs[6 : 6 + count_y]
    modal, damper = refs[6 + count_y :]
    iy = lax.axis_index("gy")
    forces = []
    for q in range(count_y):
        piece = lax.rem(iy + q, count_y)
        stretch = received[0, piece, 0:1, :]
        rate = received[0, piece, 1:2, :]
        for i in range(1, count_x):
            stretch = stretch + received[i, piece, 0:1, :]
            rate = rate + received[i, piece, 1:2, :]
        viscous, hysteretic, _ = damper_rows(smalls[q], slot_count, stretch.shape[1])
        hysteresis, force = respond(stretch, rate, held[q], viscous, hysteretic)
        if q == 0:
            damper[...] = hysteresis[:, : damper.shape[1]]
        forces.append(force)
    load = state[2:3, :] + pulled(forces, shapes)
    displacement, velocity = advance_modes(
        load, frequency[...], ratio[...], state[0:1, :], state[1:2, :]
    )
    modal[0:1, :] = displacement
    modal[1:2, :] = velocity


def whole(space=pltpu.VMEM):
    return pl.BlockSpec(memory_space=space)


def body(
    velocity,
    pressure,
    viscosity,
    wind_profile,
    panel_area,
    slot_cell,
    slot_panel,
    panel_shapes,
    node_shapes,
    damper_node,
    damper_viscous,
    damper_hysteretic,
    frequency,
    damping_ratio,
    modal_state,
    damper_state,
):
    count_x = lax.axis_size("gx")
    count_y = lax.axis_size("gy")
    total = count_x * count_y
    both = ("gx", "gy")
    ix = lax.axis_index("gx")
    layers, rows, height = pressure.shape
    slots = slot_cell.shape[1]
    slots_padded = -(-slots // LANES) * LANES
    load_rows = slots_padded // LANES
    slot_count = count_x * slots_padded
    damper_count = damper_node.shape[0]
    damper_padded = -(-damper_count // LANES) * LANES
    mode_count = frequency.shape[0]
    params = pltpu.CompilerParams(vmem_limit_bytes=VMEM_BYTES)
    shape = jax.ShapeDtypeStruct

    raw = [
        pltpu.with_memory_space_constraint(value, pltpu.HBM)
        for value in (velocity, pressure, viscosity)
    ]
    starts = (None,) if count_y == 2 else (rows - PAD, 0)

    def swapped(values):
        if count_y == 2:
            value = lax.ppermute(values[0], "gy", [(0, 1), (1, 0)])
            return value, value
        return (
            lax.ppermute(values[0], "gy", shifts(count_y, 1, False)),
            lax.ppermute(values[1], "gy", shifts(count_y, -1, False)),
        )

    near_shape, far_shape = (9 * rows, height), (9 * rows + 16, height)
    near_message, far_message, *rest = pl.pallas_call(
        functools.partial(pack_kernel, starts),
        out_shape=(pltpu.VMEM(near_shape, bf16), pltpu.VMEM(far_shape, bf16))
        + tuple(shape((5, layers, PAD, height), f32) for _ in starts)
        + tuple(pltpu.VMEM((16, height), bf16) for _ in starts),
        in_specs=[whole(pl.ANY)] * 3,
        out_specs=(whole(),) * 2 + (whole(pl.ANY),) * len(starts) + (whole(),) * len(starts),
        scratch_shapes=[
            pltpu.VMEM((2, 5, 2, rows, height), f32),
            pltpu.SemaphoreType.DMA((2, 3)),
            pltpu.SemaphoreType.DMA((len(starts), 3)),
        ],
        compiler_params=params,
        name="pack",
    )(*raw)
    near_message = lax.ppermute(near_message, "gx", pairs(count_x, 0))
    left, right = swapped(rest[: len(starts)])
    lines = rest[len(starts) :]
    far_message = pl.pallas_call(
        functools.partial(corner_kernel, count_y),
        out_shape=pltpu.VMEM(far_shape, bf16),
        in_specs=[whole()] * 3,
        out_specs=whole(),
        input_output_aliases={2: 0},
        compiler_params=params,
        name="corner",
    )(left, right, far_message)
    tied = lax.optimization_barrier(
        (
            far_message, left, right, panel_shapes, node_shapes, panel_area, slot_panel,
            damper_node, damper_viscous, damper_hysteretic, damper_state, modal_state,
        )
    )
    (
        far_message, left, right, panel_shapes, node_shapes, panel_area, slot_panel,
        damper_node, damper_viscous, damper_hysteretic, damper_state, modal_state,
    ) = tied
    far_message = lax.ppermute(far_message, "gx", pairs(count_x, 1))
    across = [
        [
            (i * count_y + k, j * count_y + k + step)
            for i, j in pairs(count_x, 0)
            for k in range(count_y)
            if 0 <= k + step < count_y
        ]
        for step in (1, -1)
    ]
    if count_y == 2:
        left_lines = right_lines = lax.ppermute(lines[0], both, across[0] + across[1])
    else:
        left_lines = lax.ppermute(lines[0], both, across[0])
        right_lines = lax.ppermute(lines[1], both, across[1])

    def around(value):
        return [value] + [
            lax.ppermute(value, "gy", shifts(count_y, q, True)) for q in range(1, count_y)
        ]

    def damper_row(value, filler=0.0):
        extra = damper_padded - damper_count
        return jnp.pad(value, (0, extra), constant_values=filler)[None]

    tables = around(panel_shapes)
    ids = slot_panel
    if slots != slots_padded:
        ids = jnp.pad(
            ids.reshape(count_x, slots),
            ((0, 0), (0, slots_padded - slots)),
            constant_values=-1,
        ).reshape(1, slot_count)
    own_ids = lax.dynamic_slice_in_dim(ids, ix * slots_padded, slots_padded, axis=1)
    small = jnp.concatenate(
        [
            ids.astype(f32),
            damper_row(damper_viscous),
            damper_row(damper_hysteretic),
            damper_row(damper_state),
            damper_row(damper_node.astype(f32), -4.0),
        ],
        axis=1,
    )
    smalls = around(small)
    cell = jnp.pad(slot_cell, ((0, 0), (0, slots_padded - slots)))

    tall = rows + 2 * PAD
    wind = wind_profile[None, :]
    velocity_next, old, mid, visc, pressure_next = pl.pallas_call(
        functools.partial(inner_kernel, count_y),
        out_shape=(
            pltpu.VMEM(velocity.shape, f32),
            shape((2, 4, 5, tall, height), f32),
            shape((2, 4, 5, tall, height), f32),
            shape((2, 5, tall, height), f32),
            pltpu.VMEM(pressure.shape, f32),
        ),
        in_specs=[whole(pl.ANY)] * 3 + [whole()] + [whole(pl.ANY)] * 2,
        out_specs=(whole(), whole(), whole(), whole(), whole()),
        scratch_shapes=[
            pltpu.VMEM((4, layers, tall, height), f32),
            pltpu.VMEM((4, layers, tall, height), f32),
            pltpu.VMEM((layers, tall, height), f32),
            pltpu.SemaphoreType.DMA((9,)),
        ],
        compiler_params=params,
        name="inner",
    )(*raw, wind, left, right)

    shapes, partial, pick, weight, found, *spreads = pl.pallas_call(
        functools.partial(prepare_kernel, slot_count, damper_padded),
        out_shape=(
            shape((count_y, 2, damper_padded, mode_count), bf16),
            shape((2, damper_padded), f32),
            shape((2, slots_padded, 2 * rows), bf16),
            shape((slots_padded, height), f32),
            shape((slots_padded, height), f32),
        )
        + (shape((LANES, slot_count), bf16),) * count_y,
        in_specs=[whole()] * (6 + count_y),
        out_specs=(whole(),) * (5 + count_y),
        compiler_params=params,
        name="prepare",
    )(
        own_ids, cell, panel_area.reshape(-1, LANES), node_shapes, modal_state,
        pressure_next, *smalls,
    )

    def edge(is_near, result, *operands):
        kept = (velocity_next, pressure_next, old, mid, visc)
        base = len(operands)
        return pl.pallas_call(
            functools.partial(edge_kernel, count_x, count_y, is_near),
            out_shape=(
                pltpu.VMEM(velocity.shape, f32),
                pltpu.VMEM(pressure.shape, f32),
                result,
                pltpu.VMEM(old.shape, f32),
                pltpu.VMEM(mid.shape, f32),
                pltpu.VMEM(visc.shape, f32),
            ),
            in_specs=[whole()] * (base + 5),
            out_specs=(whole(),) * 6,
            input_output_aliases={base: 0, base + 1: 1, base + 2: 3, base + 3: 4, base + 4: 5},
            compiler_params=params,
            name="near" if is_near else "far",
        )(*operands, *kept)

    velocity_next, pressure_next, found, old, mid, visc = edge(
        True,
        pltpu.VMEM(found.shape, f32),
        near_message,
        left_lines,
        right_lines,
        wind,
        pick,
        found,
    )
    velocity_next, pressure_next, payload, *_ = edge(
        False,
        shape((total, load_rows + 2, LANES), f32),
        far_message,
        wind,
        pick,
        found,
        weight,
        partial,
    )
    received = lax.all_to_all(payload, both, 0, 0, tiled=True)
    received = received.reshape(count_x, count_y, load_rows + 2, LANES)

    frequency = frequency[None]
    damping_ratio = damping_ratio[None]
    payload, state, hysteresis, velocity_next, pressure_next = pl.pallas_call(
        functools.partial(first_kernel, count_x, count_y, load_rows),
        out_shape=(
            shape((total, 2, damper_padded), f32),
            shape((4, mode_count), f32),
            shape((count_y, 1, damper_padded), f32),
            shape(velocity.shape, f32),
            shape(pressure.shape, f32),
        ),
        in_specs=[whole()] * (7 + 3 * count_y),
        out_specs=(whole(),) * 3 + (whole(pl.ANY),) * 2,
        scratch_shapes=[pltpu.SemaphoreType.DMA((2,))],
        compiler_params=params,
        name="first",
    )(
        received, shapes, modal_state, frequency, damping_ratio,
        *smalls, *tables, *spreads, velocity_next, pressure_next,
    )
    received = lax.all_to_all(payload, both, 0, 0, tiled=True)
    received = received.reshape(count_x, count_y, 2, damper_padded)

    modal_next, damper_next = pl.pallas_call(
        functools.partial(second_kernel, count_x, count_y, slot_count),
        out_shape=(
            shape((2, mode_count), f32),
            shape((1, damper_count), f32),
        ),
        in_specs=[whole()] * (6 + count_y),
        out_specs=(whole(), whole()),
        compiler_params=params,
        name="second",
    )(received, shapes, frequency, damping_ratio, state, hysteresis, *smalls)
    return (velocity_next, pressure_next, modal_next, damper_next.reshape(damper_count))


def solution(mesh):
    placed = (
        P(None, "gx", "gy", None),
        P("gx", "gy", None),
        P("gx", "gy", None),
        P(),
        P("gy"),
        P("gy", "gx"),
        P("gy", None),
        P("gy", "gx"),
        P(None, "gx"),
        P("gy"),
        P("gy"),
        P("gy"),
        P("gx"),
        P("gx"),
        P(None, "gx"),
        P("gy"),
    )
    return jax.shard_map(
        body,
        mesh=mesh,
        in_specs=placed,
        out_specs=(P(None, "gx", "gy", None), P("gx", "gy", None), P(None, "gx"), P("gy")),
        check_vma=False,
    )
```

```python
import functools

import jax
import jax.numpy as jnp
from jax import lax
from jax.experimental import pallas as pl
from jax.experimental.pallas import tpu as pltpu
from jax.sharding import PartitionSpec as P

f32 = jnp.float32
bf16 = jnp.bfloat16
time_step = 0.1
modal_step = 0.5
shape_beta = 0.5
shape_gamma = 0.5
spring_rate = 0.5
LANES = 128
PAD = 8
VMEM_BYTES = 40 * 1024 * 1024


def shifts(size, step, cyclic):
    if cyclic:
        return [((i + step) % size, i) for i in range(size)]
    return [(i, i + step) for i in range(size) if 0 <= i + step < size]


def pairs(size, first):
    lower = range(first, size - 1, 2)
    return [(i, i + 1) for i in lower] + [(i + 1, i) for i in lower]


def parts_of(row):
    high = row.astype(bf16).astype(f32)
    rest = row - high
    middle = rest.astype(bf16).astype(f32)
    return [high, middle, rest - middle]


def stacked(rows):
    filler = jnp.zeros((16 - len(rows), rows[0].shape[1]), f32)
    return jnp.concatenate(rows + [filler], axis=0).astype(bf16)


def pack_kernel(starts, vel, pre, vis, near_out, far_out, *refs):
    sides, lines = refs[: len(starts)], refs[len(starts) : -3]
    stage, sem, side_sem = refs[-3:]
    layers, rows, height = pre.shape
    odd = lax.rem(lax.axis_index("gx"), 2)
    messages = ((near_out, 1 - odd), (far_out, odd))
    copies = []
    for place, (out, upward) in enumerate(messages):
        first = upward * (layers - 2)
        near = upward * (layers - 1)
        copies += [
            pltpu.make_async_copy(
                vel.at[:, pl.ds(first, 2)], stage.at[place, pl.ds(0, 3)], sem.at[place, 0]
            ),
            pltpu.make_async_copy(pre.at[pl.ds(first, 2)], stage.at[place, 3], sem.at[place, 1]),
            pltpu.make_async_copy(vis.at[near], stage.at[place, 4, 0], sem.at[place, 2]),
        ]
    more = []
    for place, (start, out) in enumerate(zip(starts, sides)):
        if start is None:
            start = jnp.where(lax.axis_index("gy") == 0, rows - PAD, 0)
        here = pl.ds(pl.multiple_of(start, PAD), PAD)
        more += [
            pltpu.make_async_copy(vel.at[:, :, here], out.at[pl.ds(0, 3)], side_sem.at[place, 0]),
            pltpu.make_async_copy(pre.at[:, here], out.at[3], side_sem.at[place, 1]),
            pltpu.make_async_copy(vis.at[:, here], out.at[4], side_sem.at[place, 2]),
        ]
    for copy in copies + more:
        copy.start()
    for copy in copies:
        copy.wait()
    for place, (out, _) in enumerate(messages):
        for field in range(4):
            for depth in range(2):
                start = (field * 2 + depth) * rows
                out[start : start + rows, :] = stage[place, field, depth].astype(bf16)
        out[8 * rows : 9 * rows, :] = stage[place, 4, 0].astype(bf16)
    last = [stage[0, f, 1 - odd, rows - 1 : rows, :] for f in range(4)]
    first = [stage[0, f, 1 - odd, 0:1, :] for f in range(4)]
    filler = [jnp.zeros((12, height), f32)]
    last = jnp.concatenate(last + filler, axis=0)
    first = jnp.concatenate(first + filler, axis=0)
    if len(lines) == 1:
        lines[0][...] = jnp.where(lax.axis_index("gy") == 0, last, first).astype(bf16)
    else:
        lines[0][...] = last.astype(bf16)
        lines[1][...] = first.astype(bf16)
    for copy in more:
        copy.wait()


def corner_kernel(count_y, left, right, far_in, far_out):
    layers, height = left.shape[1], left.shape[3]
    start = far_out.shape[0] - 16
    iy = lax.axis_index("gy")
    near = lax.rem(lax.axis_index("gx"), 2) * (layers - 1)
    lines = [left[f, near, PAD - 1 : PAD, :] for f in range(4)]
    lines = [jnp.where(iy > 0, line, 0.0) for line in lines]
    others = [right[f, near, 0:1, :] for f in range(4)]
    lines += [jnp.where(iy < count_y - 1, line, 0.0) for line in others]
    lines.append(jnp.zeros((8, height), f32))
    far_out[start : start + 16, :] = jnp.concatenate(lines, axis=0).astype(bf16)


def stepper(wind, height):
    lane = lax.broadcasted_iota(jnp.int32, (8, height), 1)
    top = lane == height - 1
    bottom = lane == 0
    half = 0.5 * time_step
    wind_part = jnp.broadcast_to(wind[...] * half, (8, height))

    def step(get, factor, row, edge):
        def at(offset, low):
            return [get(f, offset, low) for f in range(4)]

        centre, ahead, behind = at(0, row), at(1, row), at(-1, row)
        lower = [pltpu.roll(c, 1, 0) for c in centre] if edge < 0 else at(0, row - 1)
        upper = [pltpu.roll(c, 7, 0) for c in centre] if edge > 0 else at(0, row + 1)
        above = [jnp.where(top, 0.0, pltpu.roll(c, height - 1, 1)) for c in centre]
        below = [jnp.where(bottom, 0.0, pltpu.roll(c, 1, 1)) for c in centre]
        factor = factor * time_step
        slopes = (ahead[3] - behind[3], upper[3] - lower[3], above[3] - below[3])
        result = []
        for i in range(3):
            around = (ahead[i] + behind[i]) + (upper[i] + lower[i]) + (above[i] + below[i])
            result.append(
                centre[i]
                + factor * (around - 6.0 * centre[i])
                - wind_part * (ahead[i] - behind[i])
                - half * slopes[i]
            )
        result.append(
            centre[3]
            - half * ((ahead[0] - behind[0]) + (upper[1] - lower[1]) + (above[2] - below[2]))
        )
        return result

    return step


def inner_kernel(
    count_y, vel, pre, vis, wind, left, right,
    vel_out, old_edge, mid_edge, visc_edge, pre_out,
    old, mid, visc, sem,
):
    layers, rows, height = pre.shape
    last = PAD + rows
    iy = lax.axis_index("gy")
    has_left = iy > 0
    has_right = iy < count_y - 1
    core = pl.ds(PAD, rows)
    copies = [
        pltpu.make_async_copy(vel.at[i], old.at[i, :, core], sem.at[i]) for i in range(3)
    ]
    copies.append(pltpu.make_async_copy(pre, old.at[3, :, core], sem.at[3]))
    copies.append(pltpu.make_async_copy(vis, visc.at[:, core], sem.at[4]))
    for place, (source, row) in enumerate(((left, 0), (right, last))):
        copies.append(
            pltpu.make_async_copy(
                source.at[pl.ds(0, 4)], old.at[:, :, pl.ds(row, PAD)], sem.at[5 + 2 * place]
            )
        )
        copies.append(
            pltpu.make_async_copy(
                source.at[4], visc.at[:, pl.ds(row, PAD)], sem.at[6 + 2 * place]
            )
        )
    for copy in copies:
        copy.start()
    for copy in copies:
        copy.wait()
    blank = jnp.zeros((4, layers, PAD, height), f32)

    @pl.when(jnp.logical_not(has_left))
    def _():
        old[:, :, 0:PAD, :] = blank
        mid[:, :, 0:PAD, :] = blank

    @pl.when(jnp.logical_not(has_right))
    def _():
        old[:, :, last : last + PAD, :] = blank
        mid[:, :, last : last + PAD, :] = blank

    step = stepper(wind, height)

    nothing = jnp.zeros((8, height), f32)

    def advance(source, layer, row, edge=0, missing=0):
        def get(f, offset, low):
            if missing and offset == missing:
                return nothing
            return source[f, layer + offset, pl.ds(low, 8), :]

        return step(get, visc[layer, pl.ds(row, 8), :], row, edge)

    def first(layer, row, edge=0):
        result = advance(old, layer, row, edge)
        for f in range(4):
            mid[f, layer, pl.ds(row, 8), :] = result[f]

    @pl.loop(1, layers - 1)
    def _(layer):
        for row in range(PAD, last, 8):
            first(layer, row)

    @pl.when(has_left)
    def _():
        @pl.loop(1, layers - 1)
        def _(layer):
            first(layer, 0, -1)

    @pl.when(has_right)
    def _():
        @pl.loop(1, layers - 1)
        def _(layer):
            first(layer, last, 1)

    @pl.loop(2, layers - 2)
    def _(layer):
        for row in range(PAD, last, 8):
            result = advance(mid, layer, row)
            for i in range(3):
                vel_out[i, layer, row - PAD : row - PAD + 8, :] = result[i]
            pre_out[layer, row - PAD : row - PAD + 8, :] = result[3]

    for side, own, inside, place, missing in (
        (0, 0, 1, 3, -1),
        (1, layers - 1, layers - 2, 1, 1),
    ):

        def begin(row, edge, side=side, own=own, missing=missing):
            result = advance(old, own, row, edge, missing)
            for f in range(4):
                mid_edge[side, f, 2, row : row + 8, :] = result[f]

        for row in range(PAD, last, 8):
            begin(row, 0)
            result = advance(mid, inside, row, 0, missing)
            here = slice(row - PAD, row - PAD + 8)
            for i in range(3):
                vel_out[i, inside, here, :] = result[i]
            pre_out[inside, here, :] = result[3]
        for there, row, edge in ((has_left, 0, -1), (has_right, last, 1)):

            @pl.when(there)
            def _(begin=begin, row=row, edge=edge):
                begin(row, edge)

            @pl.when(jnp.logical_not(there))
            def _(side=side, row=row):
                mid_edge[side, :, 2, row : row + PAD, :] = jnp.zeros((4, PAD, height), f32)

        visc_edge[side, 2] = visc[own]
        visc_edge[side, place] = visc[inside]
        for f in range(4):
            old_edge[side, f, 2] = old[f, own]
            mid_edge[side, f, place] = mid[f, inside]


def edge_kernel(count_x, count_y, damper_count, is_near, message, *refs):
    if is_near:
        left_lines, right_lines = refs[:2]
        wind, pick, found = refs[2:5]
        vel_out, pre_out, found_out, old, mid, visc = refs[10:]
    else:
        wind, pick, found, weight, partial = refs[:5]
        vel_out, pre_out, payload, old, mid, visc = refs[10:]
    layers, rows, height = pre_out.shape
    last = PAD + rows
    ix = lax.axis_index("gx")
    iy = lax.axis_index("gy")
    has_left = iy > 0
    has_right = iy < count_y - 1
    odd = lax.rem(ix, 2)
    side = 1 - odd if is_near else odd
    there = jnp.where(side == 0, ix > 0, ix < count_x - 1)
    outside = 1 + 2 * side
    for field in range(4):
        for depth in range(2):
            start = (field * 2 + depth) * rows
            old[side, field, 3 * side + depth, PAD:last, :] = message[
                start : start + rows, :
            ].astype(f32)
    visc[side, outside, PAD:last, :] = message[8 * rows : 9 * rows, :].astype(f32)
    if is_near:
        low = jnp.where(has_left, left_lines[...].astype(f32), 0.0)
        high = jnp.where(has_right, right_lines[...].astype(f32), 0.0)
    else:
        corner = message[9 * rows : 9 * rows + 16, :].astype(f32)
        low, high = corner[0:4], corner[4:8]
    for field in range(4):
        old[side, field, outside, PAD - 1 : PAD, :] = low[field : field + 1]
        old[side, field, outside, last : last + 1, :] = high[field : field + 1]

    step = stepper(wind, height)

    def advance(source, layer, row, edge=0):
        def get(f, offset, low):
            return source[side, f, layer + offset, pl.ds(low, 8), :]

        return step(get, visc[side, layer, pl.ds(row, 8), :], row, edge)

    def first(layer, row, edge=0, keep=None):
        result = advance(old, layer, row, edge)
        for f in range(4):
            value = result[f] if keep is None else jnp.where(keep, result[f], 0.0)
            mid[side, f, layer, pl.ds(row, 8), :] = value

    sign = 1.0 - 2.0 * side.astype(f32)
    windy = jnp.broadcast_to(wind[...] * (0.5 * time_step), (8, height)) * sign
    pull = sign * (0.5 * time_step)

    def light(source, layer, other, row, write):
        here = pl.ds(row, 8)
        o = [source[side, f, other, here, :] for f in range(4)]
        c = visc[side, layer, here, :] * time_step + windy
        write(0, c * o[0] + pull * o[3])
        write(1, c * o[1])
        write(2, c * o[2])
        write(3, pull * o[0])

    for row in range(0, last + PAD, 8):
        def write(f, value, row=row):
            mid[side, f, 2, pl.ds(row, 8), :] += value
        light(old, 2, outside, row, write)
    for row in range(PAD, last, 8):
        first(outside, row, 0, there)

    for row in range(PAD, last, 8):
        result = advance(mid, 2, row)
        here = pl.ds(row - PAD, 8)
        target = side * (layers - 1)
        for i in range(3):
            vel_out[i, target, here, :] = result[i]
        pre_out[target, here, :] = result[3]
        target = 1 + side * (layers - 3)

        def write(f, value, here=here, target=target):
            if f < 3:
                vel_out[f, target, here, :] += value
            else:
                pre_out[target, here, :] += value

        light(mid, 3 - 2 * side, 2, row, write)

    flat = pre_out[pl.ds(side * (layers - 2), 2)].reshape(2 * rows, height)
    total = found[...]
    for part in parts_of(flat):
        total = total + jnp.dot(pick[side], part.astype(bf16), preferred_element_type=f32)
    if is_near:
        found_out[...] = total
        return
    loads = jnp.sum(weight[...] * total, axis=1, keepdims=True).astype(bf16).astype(f32)
    slots = weight.shape[0]
    same = lax.broadcasted_iota(jnp.int32, (LANES, LANES), 0) == lax.broadcasted_iota(
        jnp.int32, (LANES, LANES), 1
    )
    lines = []
    for start in range(0, slots, LANES):
        chosen = jnp.where(same, loads[start : start + LANES], 0.0)
        lines.append(jnp.sum(chosen, axis=0, keepdims=True))
    pair = folded(partial[...], damper_count)
    high = pair.astype(bf16).astype(f32)
    message = jnp.concatenate(lines + [high, pair - high], axis=0).astype(bf16)
    payload[...] = jnp.broadcast_to(message[None], payload.shape)


def prepare_kernel(slot_count, damper_width, own_ids, cell, areas, nodes, modal, pre, *refs):
    count_y = (len(refs) - 5) // 2
    smalls = refs[:count_y]
    shapes, partial, pick, weight, found = refs[count_y : count_y + 5]
    spreads = refs[count_y + 5 :]
    layers, rows = pre.shape[:2]
    high_count = areas.shape[0]
    slots = own_ids.shape[1]
    height = weight.shape[1]
    ids = own_ids[...]
    high = jnp.where(ids < 0, -1, ids // LANES)
    low = ids - high * LANES
    high_pick = lax.broadcasted_iota(jnp.int32, (high_count, slots), 0) == high
    low_pick = lax.broadcasted_iota(jnp.int32, (LANES, slots), 0) == low
    high_pick = high_pick.astype(f32).astype(bf16)
    spread = jnp.zeros((LANES, slots), f32)
    for part in parts_of(areas[...]):
        spread = spread + lax.dot_general(
            part.astype(bf16),
            high_pick,
            (((0,), (0,)), ((), ())),
            preferred_element_type=f32,
        )
    area = jnp.sum(jnp.where(low_pick, spread, 0.0), axis=0, keepdims=True)
    same = lax.broadcasted_iota(jnp.int32, (LANES, LANES), 0) == lax.broadcasted_iota(
        jnp.int32, (LANES, LANES), 1
    )

    def stand(row):
        lines = [
            jnp.sum(jnp.where(same, row[:, k : k + LANES], 0.0), axis=1, keepdims=True)
            for k in range(0, slots, LANES)
        ]
        return jnp.concatenate(lines, axis=0)

    place = cell[...]
    line = place // height
    level = place - line * height
    line, level = stand(line.astype(f32)), stand(level.astype(f32))
    rank = lax.broadcasted_iota(jnp.int32, (slots, 2 * rows), 1).astype(f32)
    for side in range(2):
        start = float(side * (layers - 2) * rows)
        pick[side] = (rank + start == line).astype(f32).astype(bf16)
    inside = lax.broadcasted_iota(jnp.int32, (slots, (layers - 4) * rows), 1).astype(f32)
    inside = (inside + 2.0 * rows == line).astype(f32).astype(bf16)
    core = pre[2 : layers - 2].reshape((layers - 4) * rows, height)
    total = jnp.zeros((slots, height), f32)
    for part in parts_of(core):
        total = total + jnp.dot(inside, part.astype(bf16), preferred_element_type=f32)
    found[...] = total
    rank = lax.broadcasted_iota(jnp.int32, (slots, height), 1).astype(f32)
    weight[...] = jnp.where(rank == level, stand(area), 0.0)
    low_rank = lax.broadcasted_iota(jnp.int32, (LANES, slot_count), 0).astype(f32)
    node_rank = lax.broadcasted_iota(jnp.int32, (nodes.shape[0], damper_width), 0).astype(f32)
    table = nodes[...]
    for q, small in enumerate(smalls):
        numbers = small[:, :slot_count]
        numbers = numbers - jnp.floor(numbers * (1.0 / LANES)) * LANES
        spreads[q][...] = (low_rank == numbers).astype(f32).astype(bf16)
        lower = small[:, slot_count + 3 * damper_width : slot_count + 4 * damper_width]
        for end in range(2):
            picked = (node_rank == lower + (1.0 - end)).astype(f32).astype(bf16)
            rows = lax.dot_general(
                picked, table, (((0,), (0,)), ((), ())), preferred_element_type=f32
            )
            shapes[q, end] = rows.astype(bf16)
    state = modal[...]
    partial[...] = drift_times(state[0:1], state[1:2], shapes)


def folded(pair, count):
    width = pair.shape[1]
    if 2 * count > width:
        return pair
    return pair[0:1] + pltpu.roll(pair[1:2], count, 1)


def unfolded(rows, count):
    width = rows.shape[1]
    if 2 * count > width:
        return rows[0:1], rows[1:2]
    low = lax.broadcasted_iota(jnp.int32, rows.shape, 1) < count
    return jnp.where(low, rows, 0.0), jnp.where(low, pltpu.roll(rows, width - count, 1), 0.0)


def respond(stretch, rate, hysteresis, viscous, hysteretic):
    hysteresis = hysteresis + modal_step * (
        rate
        - shape_beta * jnp.abs(rate) * hysteresis
        - shape_gamma * rate * jnp.abs(hysteresis)
    )
    force = -(viscous * rate + spring_rate * stretch + hysteretic * hysteresis)
    return hysteresis, force


def pulled(forces, shapes):
    sides = []
    for force in forces:
        three = jnp.concatenate(parts_of(force) + [jnp.zeros((13, force.shape[1]), f32)], axis=0)
        sides += [three, -three]
    left = jnp.concatenate(sides, axis=1).astype(bf16)
    right = shapes[...].reshape(-1, shapes.shape[-1])
    return jnp.sum(jnp.dot(left, right, preferred_element_type=f32), axis=0, keepdims=True)


def drift_times(displacement, velocity, shapes):
    pair = lax.dot_general(
        stacked(parts_of(displacement) + parts_of(velocity)),
        shapes[0].reshape(-1, shapes.shape[-1]),
        (((1,), (1,)), ((), ())),
        preferred_element_type=f32,
    )
    width = pair.shape[1] // 2
    drift = pair[:, :width] - pair[:, width:]
    return jnp.concatenate(
        [
            jnp.sum(drift[0:3], axis=0, keepdims=True),
            jnp.sum(drift[3:6], axis=0, keepdims=True),
        ],
        axis=0,
    )


def advance_modes(load, frequency, ratio, displacement, velocity):
    acceleration = (
        load
        - 2.0 * ratio * frequency * velocity
        - frequency * frequency * displacement
    )
    velocity = velocity + modal_step * acceleration
    return displacement + modal_step * velocity, velocity


def damper_rows(small, slot_count, width):
    return [small[:, slot_count + k * width : slot_count + (k + 1) * width] for k in range(3)]


def first_kernel(count_x, count_y, load_rows, damper_count, *refs):
    arrived, shapes, modal, frequency, ratio = refs[:5]
    smalls = refs[5 : 5 + count_y]
    tables = refs[5 + count_y : 5 + 2 * count_y]
    spreads = refs[5 + 2 * count_y : 5 + 3 * count_y]
    vel, pre, payload, state, hysteresis_out, vel_out, pre_out, received, sem = refs[5 + 3 * count_y :]
    writes = [
        pltpu.make_async_copy(vel, vel_out, sem.at[0]),
        pltpu.make_async_copy(pre, pre_out, sem.at[1]),
    ]
    for write in writes:
        write.start()
    iy = lax.axis_index("gy")
    received[...] = arrived[...].astype(f32)
    kept = (arrived.shape[2] - load_rows) // 2
    panel_count = tables[0].shape[0]
    high_count = panel_count // LANES
    slot_count = count_x * load_rows * LANES
    width = payload.shape[-1]
    rank = lax.broadcasted_iota(jnp.int32, (high_count, LANES), 0).astype(f32)
    sides = []
    forces = []
    for q in range(count_y):
        piece = lax.rem(iy + q, count_y)
        ids = smalls[q][:, :slot_count]
        high = jnp.floor(ids * (1.0 / LANES))
        chunks = []
        for i in range(count_x):
            for r in range(load_rows):
                start = (i * load_rows + r) * LANES
                line = received[i, piece, r : r + 1, :]
                chunks.append(
                    jnp.where(rank == high[:, start : start + LANES], line, 0.0).astype(bf16)
                )
        sorted_loads = lax.dot_general(
            jnp.concatenate(chunks, axis=1),
            spreads[q][...],
            (((1,), (1,)), ((), ())),
            preferred_element_type=f32,
        )
        sides.append(
            jnp.concatenate(
                [jnp.where(rank == c, sorted_loads, 0.0).astype(bf16) for c in range(high_count)],
                axis=1,
            )
        )
        sums = received[0, piece, load_rows:, :]
        for i in range(1, count_x):
            sums = sums + received[i, piece, load_rows:, :]
        stretch, rate = unfolded(sums[:kept] + sums[kept:], damper_count)
        viscous, hysteretic, held_state = damper_rows(smalls[q], slot_count, width)
        hysteresis, force = respond(stretch, rate, held_state, viscous, hysteretic)
        hysteresis_out[q] = hysteresis
        forces.append(force)
    load = pulled(forces, shapes)
    rows = jnp.zeros((high_count, modal.shape[1]), f32)
    for q in range(count_y):
        rows = rows + jnp.dot(sides[q], tables[q][...], preferred_element_type=f32)
    panel_modal = jnp.sum(rows, axis=0, keepdims=True)
    displacement, velocity = advance_modes(
        panel_modal + load, frequency[...], ratio[...], modal[0:1, :], modal[1:2, :]
    )
    state[0:1, :] = displacement
    state[1:2, :] = velocity
    state[2:3, :] = panel_modal
    state[3:4, :] = panel_modal
    message = folded(drift_times(displacement, velocity, shapes), damper_count)
    payload[...] = jnp.broadcast_to(message[None], payload.shape)
    for write in writes:
        write.wait()


def second_kernel(count_x, count_y, slot_count, damper_count, *refs):
    received, shapes, frequency, ratio, state, held = refs[:6]
    smalls = refs[6 : 6 + count_y]
    modal, damper = refs[6 + count_y :]
    iy = lax.axis_index("gy")
    forces = []
    for q in range(count_y):
        piece = lax.rem(iy + q, count_y)
        sums = received[0, piece]
        for i in range(1, count_x):
            sums = sums + received[i, piece]
        stretch, rate = unfolded(sums, damper_count)
        viscous, hysteretic, _ = damper_rows(smalls[q], slot_count, stretch.shape[1])
        hysteresis, force = respond(stretch, rate, held[q], viscous, hysteretic)
        if q == 0:
            damper[...] = hysteresis[:, : damper.shape[1]]
        forces.append(force)
    load = state[2:3, :] + pulled(forces, shapes)
    displacement, velocity = advance_modes(
        load, frequency[...], ratio[...], state[0:1, :], state[1:2, :]
    )
    modal[0:1, :] = displacement
    modal[1:2, :] = velocity


def whole(space=pltpu.VMEM):
    return pl.BlockSpec(memory_space=space)


def body(
    velocity,
    pressure,
    viscosity,
    wind_profile,
    panel_area,
    slot_cell,
    slot_panel,
    panel_shapes,
    node_shapes,
    damper_node,
    damper_viscous,
    damper_hysteretic,
    frequency,
    damping_ratio,
    modal_state,
    damper_state,
):
    count_x = lax.axis_size("gx")
    count_y = lax.axis_size("gy")
    total = count_x * count_y
    both = ("gx", "gy")
    ix = lax.axis_index("gx")
    layers, rows, height = pressure.shape
    slots = slot_cell.shape[1]
    slots_padded = -(-slots // LANES) * LANES
    load_rows = slots_padded // LANES
    slot_count = count_x * slots_padded
    damper_count = damper_node.shape[0]
    damper_padded = -(-damper_count // LANES) * LANES
    mode_count = frequency.shape[0]
    params = pltpu.CompilerParams(vmem_limit_bytes=VMEM_BYTES)
    shape = jax.ShapeDtypeStruct

    raw = [
        pltpu.with_memory_space_constraint(value, pltpu.HBM)
        for value in (velocity, pressure, viscosity)
    ]
    starts = (None,) if count_y == 2 else (rows - PAD, 0)

    def swapped(values):
        if count_y == 2:
            value = lax.ppermute(values[0], "gy", [(0, 1), (1, 0)])
            return value, value
        return (
            lax.ppermute(values[0], "gy", shifts(count_y, 1, False)),
            lax.ppermute(values[1], "gy", shifts(count_y, -1, False)),
        )

    near_shape, far_shape = (9 * rows, height), (9 * rows + 16, height)
    near_message, far_message, *rest = pl.pallas_call(
        functools.partial(pack_kernel, starts),
        out_shape=(pltpu.VMEM(near_shape, bf16), pltpu.VMEM(far_shape, bf16))
        + tuple(shape((5, layers, PAD, height), f32) for _ in starts)
        + tuple(pltpu.VMEM((16, height), bf16) for _ in starts),
        in_specs=[whole(pl.ANY)] * 3,
        out_specs=(whole(),) * 2 + (whole(pl.ANY),) * len(starts) + (whole(),) * len(starts),
        scratch_shapes=[
            pltpu.VMEM((2, 5, 2, rows, height), f32),
            pltpu.SemaphoreType.DMA((2, 3)),
            pltpu.SemaphoreType.DMA((len(starts), 3)),
        ],
        compiler_params=params,
        name="pack",
    )(*raw)
    near_message = lax.ppermute(near_message, "gx", pairs(count_x, 0))
    left, right = swapped(rest[: len(starts)])
    lines = rest[len(starts) :]
    far_message = pl.pallas_call(
        functools.partial(corner_kernel, count_y),
        out_shape=pltpu.VMEM(far_shape, bf16),
        in_specs=[whole()] * 3,
        out_specs=whole(),
        input_output_aliases={2: 0},
        compiler_params=params,
        name="corner",
    )(left, right, far_message)
    tied = lax.optimization_barrier(
        (
            far_message, left, right, panel_shapes, node_shapes, panel_area, slot_panel,
            damper_node, damper_viscous, damper_hysteretic, damper_state, modal_state,
        )
    )
    (
        far_message, left, right, panel_shapes, node_shapes, panel_area, slot_panel,
        damper_node, damper_viscous, damper_hysteretic, damper_state, modal_state,
    ) = tied
    far_message = lax.ppermute(far_message, "gx", pairs(count_x, 1))
    across = [
        [
            (i * count_y + k, j * count_y + k + step)
            for i, j in pairs(count_x, 0)
            for k in range(count_y)
            if 0 <= k + step < count_y
        ]
        for step in (1, -1)
    ]
    if count_y == 2:
        left_lines = right_lines = lax.ppermute(lines[0], both, across[0] + across[1])
    else:
        left_lines = lax.ppermute(lines[0], both, across[0])
        right_lines = lax.ppermute(lines[1], both, across[1])

    def around(value):
        return [value] + [
            lax.ppermute(value, "gy", shifts(count_y, q, True)) for q in range(1, count_y)
        ]

    def damper_row(value, filler=0.0):
        extra = damper_padded - damper_count
        return jnp.pad(value, (0, extra), constant_values=filler)[None]

    tables = around(panel_shapes)
    ids = slot_panel
    if slots != slots_padded:
        ids = jnp.pad(
            ids.reshape(count_x, slots),
            ((0, 0), (0, slots_padded - slots)),
            constant_values=-1,
        ).reshape(1, slot_count)
    own_ids = lax.dynamic_slice_in_dim(ids, ix * slots_padded, slots_padded, axis=1)
    small = jnp.concatenate(
        [
            ids.astype(f32),
            damper_row(damper_viscous),
            damper_row(damper_hysteretic),
            damper_row(damper_state),
            damper_row(damper_node.astype(f32), -4.0),
        ],
        axis=1,
    )
    smalls = around(small)
    cell = jnp.pad(slot_cell, ((0, 0), (0, slots_padded - slots)))

    tall = rows + 2 * PAD
    wind = wind_profile[None, :]
    velocity_next, old, mid, visc, pressure_next = pl.pallas_call(
        functools.partial(inner_kernel, count_y),
        out_shape=(
            pltpu.VMEM(velocity.shape, f32),
            shape((2, 4, 5, tall, height), f32),
            shape((2, 4, 5, tall, height), f32),
            shape((2, 5, tall, height), f32),
            pltpu.VMEM(pressure.shape, f32),
        ),
        in_specs=[whole(pl.ANY)] * 3 + [whole()] + [whole(pl.ANY)] * 2,
        out_specs=(whole(), whole(), whole(), whole(), whole()),
        scratch_shapes=[
            pltpu.VMEM((4, layers, tall, height), f32),
            pltpu.VMEM((4, layers, tall, height), f32),
            pltpu.VMEM((layers, tall, height), f32),
            pltpu.SemaphoreType.DMA((9,)),
        ],
        compiler_params=params,
        name="inner",
    )(*raw, wind, left, right)

    shapes, partial, pick, weight, found, *spreads = pl.pallas_call(
        functools.partial(prepare_kernel, slot_count, damper_padded),
        out_shape=(
            shape((count_y, 2, damper_padded, mode_count), bf16),
            shape((2, damper_padded), f32),
            shape((2, slots_padded, 2 * rows), bf16),
            shape((slots_padded, height), f32),
            shape((slots_padded, height), f32),
        )
        + (shape((LANES, slot_count), bf16),) * count_y,
        in_specs=[whole()] * (6 + count_y),
        out_specs=(whole(),) * (5 + count_y),
        compiler_params=params,
        name="prepare",
    )(
        own_ids, cell, panel_area.reshape(-1, LANES), node_shapes, modal_state,
        pressure_next, *smalls,
    )

    kept = 1 if 2 * damper_count <= damper_padded else 2

    def edge(is_near, result, *operands):
        kept = (velocity_next, pressure_next, old, mid, visc)
        base = len(operands)
        return pl.pallas_call(
            functools.partial(edge_kernel, count_x, count_y, damper_count, is_near),
            out_shape=(
                pltpu.VMEM(velocity.shape, f32),
                pltpu.VMEM(pressure.shape, f32),
                result,
                pltpu.VMEM(old.shape, f32),
                pltpu.VMEM(mid.shape, f32),
                pltpu.VMEM(visc.shape, f32),
            ),
            in_specs=[whole()] * (base + 5),
            out_specs=(whole(),) * 6,
            input_output_aliases={base: 0, base + 1: 1, base + 2: 3, base + 3: 4, base + 4: 5},
            compiler_params=params,
            name="near" if is_near else "far",
        )(*operands, *kept)

    velocity_next, pressure_next, found, old, mid, visc = edge(
        True,
        pltpu.VMEM(found.shape, f32),
        near_message,
        left_lines,
        right_lines,
        wind,
        pick,
        found,
    )
    velocity_next, pressure_next, payload, *_ = edge(
        False,
        shape((total, load_rows + 2 * kept, LANES), bf16),
        far_message,
        wind,
        pick,
        found,
        weight,
        partial,
    )
    received = lax.all_to_all(payload, both, 0, 0, tiled=True)
    received = received.reshape(count_x, count_y, load_rows + 2 * kept, LANES)

    frequency = frequency[None]
    damping_ratio = damping_ratio[None]
    payload, state, hysteresis, velocity_next, pressure_next = pl.pallas_call(
        functools.partial(first_kernel, count_x, count_y, load_rows, damper_count),
        out_shape=(
            shape((total, kept, damper_padded), f32),
            shape((4, mode_count), f32),
            shape((count_y, 1, damper_padded), f32),
            shape(velocity.shape, f32),
            shape(pressure.shape, f32),
        ),
        in_specs=[whole()] * (7 + 3 * count_y),
        out_specs=(whole(),) * 3 + (whole(pl.ANY),) * 2,
        scratch_shapes=[
            pltpu.VMEM((count_x, count_y, load_rows + 2 * kept, LANES), f32),
            pltpu.SemaphoreType.DMA((2,)),
        ],
        compiler_params=params,
        name="first",
    )(
        received, shapes, modal_state, frequency, damping_ratio,
        *smalls, *tables, *spreads, velocity_next, pressure_next,
    )
    received = lax.all_to_all(payload, both, 0, 0, tiled=True)
    received = received.reshape(count_x, count_y, kept, damper_padded)

    modal_next, damper_next = pl.pallas_call(
        functools.partial(second_kernel, count_x, count_y, slot_count, damper_count),
        out_shape=(
            shape((2, mode_count), f32),
            shape((1, damper_count), f32),
        ),
        in_specs=[whole()] * (6 + count_y),
        out_specs=(whole(), whole()),
        compiler_params=params,
        name="second",
    )(received, shapes, frequency, damping_ratio, state, hysteresis, *smalls)
    return (velocity_next, pressure_next, modal_next, damper_next.reshape(damper_count))


def solution(mesh):
    placed = (
        P(None, "gx", "gy", None),
        P("gx", "gy", None),
        P("gx", "gy", None),
        P(),
        P("gy"),
        P("gy", "gx"),
        P("gy", None),
        P("gy", "gx"),
        P(None, "gx"),
        P("gy"),
        P("gy"),
        P("gy"),
        P("gx"),
        P("gx"),
        P(None, "gx"),
        P("gy"),
    )
    return jax.shard_map(
        body,
        mesh=mesh,
        in_specs=placed,
        out_specs=(P(None, "gx", "gy", None), P("gx", "gy", None), P(None, "gx"), P("gy")),
        check_vma=False,
    )
```

```python
import functools

import jax
import jax.numpy as jnp
from jax import lax
from jax.experimental import pallas as pl
from jax.experimental.pallas import tpu as pltpu
from jax.sharding import PartitionSpec as P

f32 = jnp.float32
bf16 = jnp.bfloat16
time_step = 0.1
modal_step = 0.5
shape_beta = 0.5
shape_gamma = 0.5
spring_rate = 0.5
LANES = 128
PAD = 8
VMEM_BYTES = 40 * 1024 * 1024


def shifts(size, step, cyclic):
    if cyclic:
        return [((i + step) % size, i) for i in range(size)]
    return [(i, i + step) for i in range(size) if 0 <= i + step < size]


def pairs(size, first):
    lower = range(first, size - 1, 2)
    return [(i, i + 1) for i in lower] + [(i + 1, i) for i in lower]


def parts_of(row):
    high = row.astype(bf16).astype(f32)
    rest = row - high
    middle = rest.astype(bf16).astype(f32)
    return [high, middle, rest - middle]


def stacked(rows):
    filler = jnp.zeros((16 - len(rows), rows[0].shape[1]), f32)
    return jnp.concatenate(rows + [filler], axis=0).astype(bf16)


def pack_kernel(starts, vel, pre, vis, near_out, far_out, *refs):
    sides, lines = refs[: len(starts)], refs[len(starts) : -3]
    stage, sem, side_sem = refs[-3:]
    layers, rows, height = pre.shape
    odd = lax.rem(lax.axis_index("gx"), 2)
    messages = ((near_out, 1 - odd), (far_out, odd))
    copies = []
    for place, (out, upward) in enumerate(messages):
        first = upward * (layers - 2)
        near = upward * (layers - 1)
        copies += [
            pltpu.make_async_copy(
                vel.at[:, pl.ds(first, 2)], stage.at[place, pl.ds(0, 3)], sem.at[place, 0]
            ),
            pltpu.make_async_copy(pre.at[pl.ds(first, 2)], stage.at[place, 3], sem.at[place, 1]),
            pltpu.make_async_copy(vis.at[near], stage.at[place, 4, 0], sem.at[place, 2]),
        ]
    more = []
    for place, (start, out) in enumerate(zip(starts, sides)):
        if start is None:
            start = jnp.where(lax.axis_index("gy") == 0, rows - PAD, 0)
        here = pl.ds(pl.multiple_of(start, PAD), PAD)
        more += [
            pltpu.make_async_copy(vel.at[:, :, here], out.at[pl.ds(0, 3)], side_sem.at[place, 0]),
            pltpu.make_async_copy(pre.at[:, here], out.at[3], side_sem.at[place, 1]),
            pltpu.make_async_copy(vis.at[:, here], out.at[4], side_sem.at[place, 2]),
        ]
    for copy in copies + more:
        copy.start()
    for copy in copies:
        copy.wait()
    for place, (out, _) in enumerate(messages):
        for field in range(4):
            for depth in range(2):
                start = (field * 2 + depth) * rows
                out[start : start + rows, :] = stage[place, field, depth].astype(bf16)
        out[8 * rows : 9 * rows, :] = stage[place, 4, 0].astype(bf16)
    last = [stage[0, f, 1 - odd, rows - 1 : rows, :] for f in range(4)]
    first = [stage[0, f, 1 - odd, 0:1, :] for f in range(4)]
    filler = [jnp.zeros((12, height), f32)]
    last = jnp.concatenate(last + filler, axis=0)
    first = jnp.concatenate(first + filler, axis=0)
    if len(lines) == 1:
        lines[0][...] = jnp.where(lax.axis_index("gy") == 0, last, first).astype(bf16)
    else:
        lines[0][...] = last.astype(bf16)
        lines[1][...] = first.astype(bf16)
    for copy in more:
        copy.wait()


def corner_kernel(count_y, left, right, far_in, far_out):
    layers, height = left.shape[1], left.shape[3]
    start = far_out.shape[0] - 16
    iy = lax.axis_index("gy")
    near = lax.rem(lax.axis_index("gx"), 2) * (layers - 1)
    lines = [left[f, near, PAD - 1 : PAD, :] for f in range(4)]
    lines = [jnp.where(iy > 0, line, 0.0) for line in lines]
    others = [right[f, near, 0:1, :] for f in range(4)]
    lines += [jnp.where(iy < count_y - 1, line, 0.0) for line in others]
    lines.append(jnp.zeros((8, height), f32))
    far_out[start : start + 16, :] = jnp.concatenate(lines, axis=0).astype(bf16)


def stepper(wind, height):
    lane = lax.broadcasted_iota(jnp.int32, (8, height), 1)
    top = lane == height - 1
    bottom = lane == 0
    half = 0.5 * time_step
    wind_part = jnp.broadcast_to(wind[...] * half, (8, height))

    def step(get, factor, row, edge):
        def at(offset, low):
            return [get(f, offset, low) for f in range(4)]

        centre, ahead, behind = at(0, row), at(1, row), at(-1, row)
        lower = [pltpu.roll(c, 1, 0) for c in centre] if edge < 0 else at(0, row - 1)
        upper = [pltpu.roll(c, 7, 0) for c in centre] if edge > 0 else at(0, row + 1)
        above = [jnp.where(top, 0.0, pltpu.roll(c, height - 1, 1)) for c in centre]
        below = [jnp.where(bottom, 0.0, pltpu.roll(c, 1, 1)) for c in centre]
        factor = factor * time_step
        slopes = (ahead[3] - behind[3], upper[3] - lower[3], above[3] - below[3])
        result = []
        for i in range(3):
            around = (ahead[i] + behind[i]) + (upper[i] + lower[i]) + (above[i] + below[i])
            result.append(
                centre[i]
                + factor * (around - 6.0 * centre[i])
                - wind_part * (ahead[i] - behind[i])
                - half * slopes[i]
            )
        result.append(
            centre[3]
            - half * ((ahead[0] - behind[0]) + (upper[1] - lower[1]) + (above[2] - below[2]))
        )
        return result

    return step


def inner_kernel(
    count_y, vel, pre, vis, wind, left, right,
    vel_out, old_edge, mid_edge, visc_edge, pre_out,
    old, mid, visc, sem,
):
    layers, rows, height = pre.shape
    last = PAD + rows
    iy = lax.axis_index("gy")
    has_left = iy > 0
    has_right = iy < count_y - 1
    core = pl.ds(PAD, rows)
    copies = [
        pltpu.make_async_copy(vel.at[i], old.at[i, :, core], sem.at[i]) for i in range(3)
    ]
    copies.append(pltpu.make_async_copy(pre, old.at[3, :, core], sem.at[3]))
    copies.append(pltpu.make_async_copy(vis, visc.at[:, core], sem.at[4]))
    for place, (source, row) in enumerate(((left, 0), (right, last))):
        copies.append(
            pltpu.make_async_copy(
                source.at[pl.ds(0, 4)], old.at[:, :, pl.ds(row, PAD)], sem.at[5 + 2 * place]
            )
        )
        copies.append(
            pltpu.make_async_copy(
                source.at[4], visc.at[:, pl.ds(row, PAD)], sem.at[6 + 2 * place]
            )
        )
    for copy in copies:
        copy.start()
    for copy in copies:
        copy.wait()
    blank = jnp.zeros((4, layers, PAD, height), f32)

    @pl.when(jnp.logical_not(has_left))
    def _():
        old[:, :, 0:PAD, :] = blank
        mid[:, :, 0:PAD, :] = blank

    @pl.when(jnp.logical_not(has_right))
    def _():
        old[:, :, last : last + PAD, :] = blank
        mid[:, :, last : last + PAD, :] = blank

    step = stepper(wind, height)

    nothing = jnp.zeros((8, height), f32)

    def advance(source, layer, row, edge=0, missing=0):
        def get(f, offset, low):
            if missing and offset == missing:
                return nothing
            return source[f, layer + offset, pl.ds(low, 8), :]

        return step(get, visc[layer, pl.ds(row, 8), :], row, edge)

    def first(layer, row, edge=0):
        result = advance(old, layer, row, edge)
        for f in range(4):
            mid[f, layer, pl.ds(row, 8), :] = result[f]

    @pl.loop(1, layers - 1)
    def _(layer):
        for row in range(PAD, last, 8):
            first(layer, row)

    @pl.when(has_left)
    def _():
        @pl.loop(1, layers - 1)
        def _(layer):
            first(layer, 0, -1)

    @pl.when(has_right)
    def _():
        @pl.loop(1, layers - 1)
        def _(layer):
            first(layer, last, 1)

    @pl.loop(2, layers - 2)
    def _(layer):
        for row in range(PAD, last, 8):
            result = advance(mid, layer, row)
            for i in range(3):
                vel_out[i, layer, row - PAD : row - PAD + 8, :] = result[i]
            pre_out[layer, row - PAD : row - PAD + 8, :] = result[3]

    for side, own, inside, place, missing in (
        (0, 0, 1, 3, -1),
        (1, layers - 1, layers - 2, 1, 1),
    ):

        def begin(row, edge, side=side, own=own, missing=missing):
            result = advance(old, own, row, edge, missing)
            for f in range(4):
                mid_edge[side, f, 2, row : row + 8, :] = result[f]

        for row in range(PAD, last, 8):
            begin(row, 0)
            result = advance(mid, inside, row, 0, missing)
            here = slice(row - PAD, row - PAD + 8)
            for i in range(3):
                vel_out[i, inside, here, :] = result[i]
            pre_out[inside, here, :] = result[3]
        for there, row, edge in ((has_left, 0, -1), (has_right, last, 1)):

            @pl.when(there)
            def _(begin=begin, row=row, edge=edge):
                begin(row, edge)

            @pl.when(jnp.logical_not(there))
            def _(side=side, row=row):
                mid_edge[side, :, 2, row : row + PAD, :] = jnp.zeros((4, PAD, height), f32)

        visc_edge[side, 2] = visc[own]
        visc_edge[side, place] = visc[inside]
        for f in range(4):
            old_edge[side, f, 2] = old[f, own]
            mid_edge[side, f, place] = mid[f, inside]


def edge_kernel(count_x, count_y, damper_count, is_near, message, *refs):
    if is_near:
        left_lines, right_lines = refs[:2]
        wind, pick, found = refs[2:5]
        vel_out, pre_out, found_out, old, mid, visc = refs[10:]
    else:
        wind, pick, found, weight, partial = refs[:5]
        vel_out, pre_out, payload, old, mid, visc = refs[10:]
    layers, rows, height = pre_out.shape
    last = PAD + rows
    ix = lax.axis_index("gx")
    iy = lax.axis_index("gy")
    has_left = iy > 0
    has_right = iy < count_y - 1
    odd = lax.rem(ix, 2)
    side = 1 - odd if is_near else odd
    there = jnp.where(side == 0, ix > 0, ix < count_x - 1)
    outside = 1 + 2 * side
    for field in range(4):
        for depth in range(2):
            start = (field * 2 + depth) * rows
            old[side, field, 3 * side + depth, PAD:last, :] = message[
                start : start + rows, :
            ].astype(f32)
    visc[side, outside, PAD:last, :] = message[8 * rows : 9 * rows, :].astype(f32)
    if is_near:
        low = jnp.where(has_left, left_lines[...].astype(f32), 0.0)
        high = jnp.where(has_right, right_lines[...].astype(f32), 0.0)
    else:
        corner = message[9 * rows : 9 * rows + 16, :].astype(f32)
        low, high = corner[0:4], corner[4:8]
    for field in range(4):
        old[side, field, outside, PAD - 1 : PAD, :] = low[field : field + 1]
        old[side, field, outside, last : last + 1, :] = high[field : field + 1]

    step = stepper(wind, height)

    def advance(source, layer, row, edge=0):
        def get(f, offset, low):
            return source[side, f, layer + offset, pl.ds(low, 8), :]

        return step(get, visc[side, layer, pl.ds(row, 8), :], row, edge)

    def first(layer, row, edge=0, keep=None):
        result = advance(old, layer, row, edge)
        for f in range(4):
            value = result[f] if keep is None else jnp.where(keep, result[f], 0.0)
            mid[side, f, layer, pl.ds(row, 8), :] = value

    sign = 1.0 - 2.0 * side.astype(f32)
    windy = jnp.broadcast_to(wind[...] * (0.5 * time_step), (8, height)) * sign
    pull = sign * (0.5 * time_step)

    def light(source, layer, other, row, write):
        here = pl.ds(row, 8)
        o = [source[side, f, other, here, :] for f in range(4)]
        c = visc[side, layer, here, :] * time_step + windy
        write(0, c * o[0] + pull * o[3])
        write(1, c * o[1])
        write(2, c * o[2])
        write(3, pull * o[0])

    for row in range(0, last + PAD, 8):
        def write(f, value, row=row):
            mid[side, f, 2, pl.ds(row, 8), :] += value
        light(old, 2, outside, row, write)
    for row in range(PAD, last, 8):
        first(outside, row, 0, there)

    for row in range(PAD, last, 8):
        result = advance(mid, 2, row)
        here = pl.ds(row - PAD, 8)
        target = side * (layers - 1)
        for i in range(3):
            vel_out[i, target, here, :] = result[i]
        pre_out[target, here, :] = result[3]
        target = 1 + side * (layers - 3)

        def write(f, value, here=here, target=target):
            if f < 3:
                vel_out[f, target, here, :] += value
            else:
                pre_out[target, here, :] += value

        light(mid, 3 - 2 * side, 2, row, write)

    flat = pre_out[pl.ds(side * (layers - 2), 2)].reshape(2 * rows, height)
    total = found[...]
    for part in parts_of(flat)[:2]:
        total = total + jnp.dot(pick[side], part.astype(bf16), preferred_element_type=f32)
    if is_near:
        found_out[...] = total
        return
    loads = jnp.sum(weight[...] * total, axis=1, keepdims=True).astype(bf16).astype(f32)
    slots = weight.shape[0]
    same = lax.broadcasted_iota(jnp.int32, (LANES, LANES), 0) == lax.broadcasted_iota(
        jnp.int32, (LANES, LANES), 1
    )
    lines = []
    for start in range(0, slots, LANES):
        chosen = jnp.where(same, loads[start : start + LANES], 0.0)
        lines.append(jnp.sum(chosen, axis=0, keepdims=True))
    pair = folded(partial[...], damper_count)
    high = pair.astype(bf16).astype(f32)
    message = jnp.concatenate(lines + [high, pair - high], axis=0).astype(bf16)
    payload[...] = jnp.broadcast_to(message[None], payload.shape)


def prepare_kernel(slot_count, damper_width, own_ids, cell, areas, nodes, modal, pre, *refs):
    count_y = (len(refs) - 5) // 2
    smalls = refs[:count_y]
    shapes, partial, pick, weight, found = refs[count_y : count_y + 5]
    spreads = refs[count_y + 5 :]
    layers, rows = pre.shape[:2]
    high_count = areas.shape[0]
    slots = own_ids.shape[1]
    height = weight.shape[1]
    ids = own_ids[...]
    high = jnp.where(ids < 0, -1, ids // LANES)
    low = ids - high * LANES
    high_pick = lax.broadcasted_iota(jnp.int32, (high_count, slots), 0) == high
    low_pick = lax.broadcasted_iota(jnp.int32, (LANES, slots), 0) == low
    high_pick = high_pick.astype(f32).astype(bf16)
    spread = jnp.zeros((LANES, slots), f32)
    for part in parts_of(areas[...]):
        spread = spread + lax.dot_general(
            part.astype(bf16),
            high_pick,
            (((0,), (0,)), ((), ())),
            preferred_element_type=f32,
        )
    area = jnp.sum(jnp.where(low_pick, spread, 0.0), axis=0, keepdims=True)
    same = lax.broadcasted_iota(jnp.int32, (LANES, LANES), 0) == lax.broadcasted_iota(
        jnp.int32, (LANES, LANES), 1
    )

    def stand(row):
        lines = [
            jnp.sum(jnp.where(same, row[:, k : k + LANES], 0.0), axis=1, keepdims=True)
            for k in range(0, slots, LANES)
        ]
        return jnp.concatenate(lines, axis=0)

    place = cell[...]
    line = place // height
    level = place - line * height
    line, level = stand(line.astype(f32)), stand(level.astype(f32))
    rank = lax.broadcasted_iota(jnp.int32, (slots, 2 * rows), 1).astype(f32)
    for side in range(2):
        start = float(side * (layers - 2) * rows)
        pick[side] = (rank + start == line).astype(f32).astype(bf16)
    inside = lax.broadcasted_iota(jnp.int32, (slots, (layers - 4) * rows), 1).astype(f32)
    inside = (inside + 2.0 * rows == line).astype(f32).astype(bf16)
    core = pre[2 : layers - 2].reshape((layers - 4) * rows, height)
    total = jnp.zeros((slots, height), f32)
    for part in parts_of(core):
        total = total + jnp.dot(inside, part.astype(bf16), preferred_element_type=f32)
    found[...] = total
    rank = lax.broadcasted_iota(jnp.int32, (slots, height), 1).astype(f32)
    weight[...] = jnp.where(rank == level, stand(area), 0.0)
    low_rank = lax.broadcasted_iota(jnp.int32, (LANES, slot_count), 0).astype(f32)
    node_rank = lax.broadcasted_iota(jnp.int32, (nodes.shape[0], damper_width), 0).astype(f32)
    table = nodes[...]
    for q, small in enumerate(smalls):
        numbers = small[:, :slot_count]
        numbers = numbers - jnp.floor(numbers * (1.0 / LANES)) * LANES
        spreads[q][...] = (low_rank == numbers).astype(f32).astype(bf16)
        lower = small[:, slot_count + 3 * damper_width : slot_count + 4 * damper_width]
        for end in range(2):
            picked = (node_rank == lower + (1.0 - end)).astype(f32).astype(bf16)
            rows = lax.dot_general(
                picked, table, (((0,), (0,)), ((), ())), preferred_element_type=f32
            )
            shapes[q, end] = rows.astype(bf16)
    state = modal[...]
    partial[...] = drift_times(state[0:1], state[1:2], shapes)


def folded(pair, count):
    width = pair.shape[1]
    if 2 * count > width:
        return pair
    return pair[0:1] + pltpu.roll(pair[1:2], count, 1)


def unfolded(rows, count):
    width = rows.shape[1]
    if 2 * count > width:
        return rows[0:1], rows[1:2]
    low = lax.broadcasted_iota(jnp.int32, rows.shape, 1) < count
    return jnp.where(low, rows, 0.0), jnp.where(low, pltpu.roll(rows, width - count, 1), 0.0)


def respond(stretch, rate, hysteresis, viscous, hysteretic):
    hysteresis = hysteresis + modal_step * (
        rate
        - shape_beta * jnp.abs(rate) * hysteresis
        - shape_gamma * rate * jnp.abs(hysteresis)
    )
    force = -(viscous * rate + spring_rate * stretch + hysteretic * hysteresis)
    return hysteresis, force


def pulled(forces, shapes):
    sides = []
    for force in forces:
        three = jnp.concatenate(parts_of(force) + [jnp.zeros((13, force.shape[1]), f32)], axis=0)
        sides += [three, -three]
    left = jnp.concatenate(sides, axis=1).astype(bf16)
    right = shapes[...].reshape(-1, shapes.shape[-1])
    return jnp.sum(jnp.dot(left, right, preferred_element_type=f32), axis=0, keepdims=True)


def drift_times(displacement, velocity, shapes):
    pair = lax.dot_general(
        stacked(parts_of(displacement) + parts_of(velocity)),
        shapes[0].reshape(-1, shapes.shape[-1]),
        (((1,), (1,)), ((), ())),
        preferred_element_type=f32,
    )
    width = pair.shape[1] // 2
    drift = pair[:, :width] - pair[:, width:]
    return jnp.concatenate(
        [
            jnp.sum(drift[0:3], axis=0, keepdims=True),
            jnp.sum(drift[3:6], axis=0, keepdims=True),
        ],
        axis=0,
    )


def advance_modes(load, frequency, ratio, displacement, velocity):
    acceleration = (
        load
        - 2.0 * ratio * frequency * velocity
        - frequency * frequency * displacement
    )
    velocity = velocity + modal_step * acceleration
    return displacement + modal_step * velocity, velocity


def damper_rows(small, slot_count, width):
    return [small[:, slot_count + k * width : slot_count + (k + 1) * width] for k in range(3)]


def first_kernel(count_x, count_y, load_rows, damper_count, *refs):
    arrived, shapes, modal, frequency, ratio = refs[:5]
    smalls = refs[5 : 5 + count_y]
    tables = refs[5 + count_y : 5 + 2 * count_y]
    spreads = refs[5 + 2 * count_y : 5 + 3 * count_y]
    vel, pre, payload, state, hysteresis_out, vel_out, pre_out, received, sem = refs[5 + 3 * count_y :]
    writes = [
        pltpu.make_async_copy(vel, vel_out, sem.at[0]),
        pltpu.make_async_copy(pre, pre_out, sem.at[1]),
    ]
    for write in writes:
        write.start()
    iy = lax.axis_index("gy")
    received[...] = arrived[...].astype(f32)
    kept = (arrived.shape[2] - load_rows) // 2
    panel_count = tables[0].shape[0]
    high_count = panel_count // LANES
    slot_count = count_x * load_rows * LANES
    width = payload.shape[-1]
    rank = lax.broadcasted_iota(jnp.int32, (high_count, LANES), 0).astype(f32)
    sides = []
    forces = []
    for q in range(count_y):
        piece = lax.rem(iy + q, count_y)
        ids = smalls[q][:, :slot_count]
        high = jnp.floor(ids * (1.0 / LANES))
        chunks = []
        for i in range(count_x):
            for r in range(load_rows):
                start = (i * load_rows + r) * LANES
                line = received[i, piece, r : r + 1, :]
                chunks.append(
                    jnp.where(rank == high[:, start : start + LANES], line, 0.0).astype(bf16)
                )
        sorted_loads = lax.dot_general(
            jnp.concatenate(chunks, axis=1),
            spreads[q][...],
            (((1,), (1,)), ((), ())),
            preferred_element_type=f32,
        )
        sides.append(
            jnp.concatenate(
                [jnp.where(rank == c, sorted_loads, 0.0).astype(bf16) for c in range(high_count)],
                axis=1,
            )
        )
        sums = received[0, piece, load_rows:, :]
        for i in range(1, count_x):
            sums = sums + received[i, piece, load_rows:, :]
        stretch, rate = unfolded(sums[:kept] + sums[kept:], damper_count)
        viscous, hysteretic, held_state = damper_rows(smalls[q], slot_count, width)
        hysteresis, force = respond(stretch, rate, held_state, viscous, hysteretic)
        hysteresis_out[q] = hysteresis
        forces.append(force)
    load = pulled(forces, shapes)
    rows = jnp.zeros((high_count, modal.shape[1]), f32)
    for q in range(count_y):
        rows = rows + jnp.dot(sides[q], tables[q][...], preferred_element_type=f32)
    panel_modal = jnp.sum(rows, axis=0, keepdims=True)
    displacement, velocity = advance_modes(
        panel_modal + load, frequency[...], ratio[...], modal[0:1, :], modal[1:2, :]
    )
    state[0:1, :] = displacement
    state[1:2, :] = velocity
    state[2:3, :] = panel_modal
    state[3:4, :] = panel_modal
    message = folded(drift_times(displacement, velocity, shapes), damper_count)
    payload[...] = jnp.broadcast_to(message[None], payload.shape)
    for write in writes:
        write.wait()


def second_kernel(count_x, count_y, slot_count, damper_count, *refs):
    received, shapes, frequency, ratio, state, held = refs[:6]
    smalls = refs[6 : 6 + count_y]
    modal, damper = refs[6 + count_y :]
    iy = lax.axis_index("gy")
    forces = []
    for q in range(count_y):
        piece = lax.rem(iy + q, count_y)
        sums = received[0, piece]
        for i in range(1, count_x):
            sums = sums + received[i, piece]
        stretch, rate = unfolded(sums, damper_count)
        viscous, hysteretic, _ = damper_rows(smalls[q], slot_count, stretch.shape[1])
        hysteresis, force = respond(stretch, rate, held[q], viscous, hysteretic)
        if q == 0:
            damper[...] = hysteresis[:, : damper.shape[1]]
        forces.append(force)
    load = state[2:3, :] + pulled(forces, shapes)
    displacement, velocity = advance_modes(
        load, frequency[...], ratio[...], state[0:1, :], state[1:2, :]
    )
    modal[0:1, :] = displacement
    modal[1:2, :] = velocity


def whole(space=pltpu.VMEM):
    return pl.BlockSpec(memory_space=space)


def body(
    velocity,
    pressure,
    viscosity,
    wind_profile,
    panel_area,
    slot_cell,
    slot_panel,
    panel_shapes,
    node_shapes,
    damper_node,
    damper_viscous,
    damper_hysteretic,
    frequency,
    damping_ratio,
    modal_state,
    damper_state,
):
    count_x = lax.axis_size("gx")
    count_y = lax.axis_size("gy")
    total = count_x * count_y
    both = ("gx", "gy")
    ix = lax.axis_index("gx")
    layers, rows, height = pressure.shape
    slots = slot_cell.shape[1]
    slots_padded = -(-slots // LANES) * LANES
    load_rows = slots_padded // LANES
    slot_count = count_x * slots_padded
    damper_count = damper_node.shape[0]
    damper_padded = -(-damper_count // LANES) * LANES
    mode_count = frequency.shape[0]
    params = pltpu.CompilerParams(vmem_limit_bytes=VMEM_BYTES)
    shape = jax.ShapeDtypeStruct

    raw = [
        pltpu.with_memory_space_constraint(value, pltpu.HBM)
        for value in (velocity, pressure, viscosity)
    ]
    starts = (None,) if count_y == 2 else (rows - PAD, 0)

    def swapped(values):
        if count_y == 2:
            value = lax.ppermute(values[0], "gy", [(0, 1), (1, 0)])
            return value, value
        return (
            lax.ppermute(values[0], "gy", shifts(count_y, 1, False)),
            lax.ppermute(values[1], "gy", shifts(count_y, -1, False)),
        )

    near_shape, far_shape = (9 * rows, height), (9 * rows + 16, height)
    near_message, far_message, *rest = pl.pallas_call(
        functools.partial(pack_kernel, starts),
        out_shape=(pltpu.VMEM(near_shape, bf16), pltpu.VMEM(far_shape, bf16))
        + tuple(shape((5, layers, PAD, height), f32) for _ in starts)
        + tuple(pltpu.VMEM((16, height), bf16) for _ in starts),
        in_specs=[whole(pl.ANY)] * 3,
        out_specs=(whole(),) * 2 + (whole(pl.ANY),) * len(starts) + (whole(),) * len(starts),
        scratch_shapes=[
            pltpu.VMEM((2, 5, 2, rows, height), f32),
            pltpu.SemaphoreType.DMA((2, 3)),
            pltpu.SemaphoreType.DMA((len(starts), 3)),
        ],
        compiler_params=params,
        name="pack",
    )(*raw)
    near_message = lax.ppermute(near_message, "gx", pairs(count_x, 0))
    left, right = swapped(rest[: len(starts)])
    lines = rest[len(starts) :]
    far_message = pl.pallas_call(
        functools.partial(corner_kernel, count_y),
        out_shape=pltpu.VMEM(far_shape, bf16),
        in_specs=[whole()] * 3,
        out_specs=whole(),
        input_output_aliases={2: 0},
        compiler_params=params,
        name="corner",
    )(left, right, far_message)
    tied = lax.optimization_barrier(
        (
            far_message, left, right, panel_shapes, node_shapes, panel_area, slot_panel,
            damper_node, damper_viscous, damper_hysteretic, damper_state, modal_state,
        )
    )
    (
        far_message, left, right, panel_shapes, node_shapes, panel_area, slot_panel,
        damper_node, damper_viscous, damper_hysteretic, damper_state, modal_state,
    ) = tied
    far_message = lax.ppermute(far_message, "gx", pairs(count_x, 1))
    across = [
        [
            (i * count_y + k, j * count_y + k + step)
            for i, j in pairs(count_x, 0)
            for k in range(count_y)
            if 0 <= k + step < count_y
        ]
        for step in (1, -1)
    ]
    if count_y == 2:
        left_lines = right_lines = lax.ppermute(lines[0], both, across[0] + across[1])
    else:
        left_lines = lax.ppermute(lines[0], both, across[0])
        right_lines = lax.ppermute(lines[1], both, across[1])

    def around(value):
        return [value] + [
            lax.ppermute(value, "gy", shifts(count_y, q, True)) for q in range(1, count_y)
        ]

    def damper_row(value, filler=0.0):
        extra = damper_padded - damper_count
        return jnp.pad(value, (0, extra), constant_values=filler)[None]

    tables = around(panel_shapes)
    ids = slot_panel
    if slots != slots_padded:
        ids = jnp.pad(
            ids.reshape(count_x, slots),
            ((0, 0), (0, slots_padded - slots)),
            constant_values=-1,
        ).reshape(1, slot_count)
    own_ids = lax.dynamic_slice_in_dim(ids, ix * slots_padded, slots_padded, axis=1)
    small = jnp.concatenate(
        [
            ids.astype(f32),
            damper_row(damper_viscous),
            damper_row(damper_hysteretic),
            damper_row(damper_state),
            damper_row(damper_node.astype(f32), -4.0),
        ],
        axis=1,
    )
    smalls = around(small)
    cell = jnp.pad(slot_cell, ((0, 0), (0, slots_padded - slots)))

    tall = rows + 2 * PAD
    wind = wind_profile[None, :]
    velocity_next, old, mid, visc, pressure_next = pl.pallas_call(
        functools.partial(inner_kernel, count_y),
        out_shape=(
            pltpu.VMEM(velocity.shape, f32),
            shape((2, 4, 5, tall, height), f32),
            shape((2, 4, 5, tall, height), f32),
            shape((2, 5, tall, height), f32),
            pltpu.VMEM(pressure.shape, f32),
        ),
        in_specs=[whole(pl.ANY)] * 3 + [whole()] + [whole(pl.ANY)] * 2,
        out_specs=(whole(), whole(), whole(), whole(), whole()),
        scratch_shapes=[
            pltpu.VMEM((4, layers, tall, height), f32),
            pltpu.VMEM((4, layers, tall, height), f32),
            pltpu.VMEM((layers, tall, height), f32),
            pltpu.SemaphoreType.DMA((9,)),
        ],
        compiler_params=params,
        name="inner",
    )(*raw, wind, left, right)

    shapes, partial, pick, weight, found, *spreads = pl.pallas_call(
        functools.partial(prepare_kernel, slot_count, damper_padded),
        out_shape=(
            shape((count_y, 2, damper_padded, mode_count), bf16),
            shape((2, damper_padded), f32),
            shape((2, slots_padded, 2 * rows), bf16),
            shape((slots_padded, height), f32),
            shape((slots_padded, height), f32),
        )
        + (shape((LANES, slot_count), bf16),) * count_y,
        in_specs=[whole()] * (6 + count_y),
        out_specs=(whole(),) * (5 + count_y),
        compiler_params=params,
        name="prepare",
    )(
        own_ids, cell, panel_area.reshape(-1, LANES), node_shapes, modal_state,
        pressure_next, *smalls,
    )

    kept = 1 if 2 * damper_count <= damper_padded else 2

    def edge(is_near, result, *operands):
        kept = (velocity_next, pressure_next, old, mid, visc)
        base = len(operands)
        return pl.pallas_call(
            functools.partial(edge_kernel, count_x, count_y, damper_count, is_near),
            out_shape=(
                pltpu.VMEM(velocity.shape, f32),
                pltpu.VMEM(pressure.shape, f32),
                result,
                pltpu.VMEM(old.shape, f32),
                pltpu.VMEM(mid.shape, f32),
                pltpu.VMEM(visc.shape, f32),
            ),
            in_specs=[whole()] * (base + 5),
            out_specs=(whole(),) * 6,
            input_output_aliases={base: 0, base + 1: 1, base + 2: 3, base + 3: 4, base + 4: 5},
            compiler_params=params,
            name="near" if is_near else "far",
        )(*operands, *kept)

    velocity_next, pressure_next, found, old, mid, visc = edge(
        True,
        pltpu.VMEM(found.shape, f32),
        near_message,
        left_lines,
        right_lines,
        wind,
        pick,
        found,
    )
    velocity_next, pressure_next, payload, *_ = edge(
        False,
        shape((total, load_rows + 2 * kept, LANES), bf16),
        far_message,
        wind,
        pick,
        found,
        weight,
        partial,
    )
    received = lax.all_to_all(payload, both, 0, 0, tiled=True)
    received = received.reshape(count_x, count_y, load_rows + 2 * kept, LANES)

    frequency = frequency[None]
    damping_ratio = damping_ratio[None]
    payload, state, hysteresis, velocity_next, pressure_next = pl.pallas_call(
        functools.partial(first_kernel, count_x, count_y, load_rows, damper_count),
        out_shape=(
            shape((total, kept, damper_padded), f32),
            shape((4, mode_count), f32),
            shape((count_y, 1, damper_padded), f32),
            shape(velocity.shape, f32),
            shape(pressure.shape, f32),
        ),
        in_specs=[whole()] * (7 + 3 * count_y),
        out_specs=(whole(),) * 3 + (whole(pl.ANY),) * 2,
        scratch_shapes=[
            pltpu.VMEM((count_x, count_y, load_rows + 2 * kept, LANES), f32),
            pltpu.SemaphoreType.DMA((2,)),
        ],
        compiler_params=params,
        name="first",
    )(
        received, shapes, modal_state, frequency, damping_ratio,
        *smalls, *tables, *spreads, velocity_next, pressure_next,
    )
    received = lax.all_to_all(payload, both, 0, 0, tiled=True)
    received = received.reshape(count_x, count_y, kept, damper_padded)

    modal_next, damper_next = pl.pallas_call(
        functools.partial(second_kernel, count_x, count_y, slot_count, damper_count),
        out_shape=(
            shape((2, mode_count), f32),
            shape((1, damper_count), f32),
        ),
        in_specs=[whole()] * (6 + count_y),
        out_specs=(whole(), whole()),
        compiler_params=params,
        name="second",
    )(received, shapes, frequency, damping_ratio, state, hysteresis, *smalls)
    return (velocity_next, pressure_next, modal_next, damper_next.reshape(damper_count))


def solution(mesh):
    placed = (
        P(None, "gx", "gy", None),
        P("gx", "gy", None),
        P("gx", "gy", None),
        P(),
        P("gy"),
        P("gy", "gx"),
        P("gy", None),
        P("gy", "gx"),
        P(None, "gx"),
        P("gy"),
        P("gy"),
        P("gy"),
        P("gx"),
        P("gx"),
        P(None, "gx"),
        P("gy"),
    )
    return jax.shard_map(
        body,
        mesh=mesh,
        in_specs=placed,
        out_specs=(P(None, "gx", "gy", None), P("gx", "gy", None), P(None, "gx"), P("gy")),
        check_vma=False,
    )
```
